32 devices in a mesh: rad: 4 (over z), ang: 8 (over y, x, core).
Axes of the slice: x: 2, y: 2, z: 4, core: 2. Of those that a mesh axis runs over, the one named last changes fastest.
Arguments:
- coarse_field: float32 [2, 4, 32, 128], P(None, 'rad', 'ang'), may hold values from -6 to 6
- excite_mid: float32 [2, 8, 4, 32, 128], P(None, None, 'rad', 'ang'), may hold values from -6 to 6
- excite_fine: float32 [2, 8, 8, 64, 256], P(None, None, 'rad', 'ang'), may hold values from -6 to 6
- kernels_mid: float32 [16, 8, 27], replicated, may hold values from -0.875 to 0.875
- noise_mid: float32 [16, 8, 8], replicated, may hold values from -1 to 1
- rows_mid: int32 [4], replicated, may hold values from 0 to 15
- kernels_fine: float32 [16, 8, 27], replicated, may hold values from -0.875 to 0.875
- noise_fine: float32 [16, 8, 8], replicated, may hold values from -1 to 1
- rows_fine: int32 [8], replicated, may hold values from 0 to 15
- emission: float32 [16, 128, 512], P('rad', 'ang'), may hold values from 0.3 to 3
- star_bins: int32 [4, 128, 512], P(None, 'ang'), may hold values from 0 to 15
- star_data: float32 [4, 128, 512], P(None, 'ang'), may hold values from -3 to 3
Outputs:
- grad_coarse: float32 [2, 4, 32, 128], P(None, 'rad', 'ang')
- grad_excite_mid: float32 [2, 8, 4, 32, 128], P(None, None, 'rad', 'ang')
- grad_excite_fine: float32 [2, 8, 8, 64, 256], P(None, None, 'rad', 'ang')
- residual: float32 [2, 4, 128, 512], P(None, None, 'ang')
The draws below stay inside these ranges and needn't reach their ends.
All inputs are finite; a program needn't handle non-finite values.
Results may differ from the reference program's by a relative error of at most 0.0003.
Values sent between devices are 32-bit elements; how exact they have to be, the bound alone decides.
No kernel may reach another device: no remote copies, remote signals or barrier semaphores. Data moves between devices by JAX's collectives and lax.ppermute only.
A program may use at most 192 MiB of HBM per device.

```python
import math
import jax
import jax.numpy as jnp
from jax import lax

NB0 = 128
NK = 16
NSTAR = 4
SAMPLES = 2
NR0 = 4
NA0 = 32
NR1 = 8
NA1 = 64
NB1 = 256
NRF = 16
NAF = 128
NBF = 512


def with_ends(drawn, stream_key, least, largest):
    index_at = [jax.random.randint(jax.random.fold_in(stream_key, axis), (), 0, length) for axis, length in enumerate(drawn.shape)]
    longest = drawn.shape.index(max(drawn.shape))
    next_to = index_at[:longest] + [(index_at[longest] + 1) % drawn.shape[longest]] + index_at[longest + 1:]
    return drawn.at[tuple(index_at)].set(least).at[tuple(next_to)].set(largest)


def steps_of(stream_key, dims, cuts, smallest, largest):
    level = 1.0
    for axis_at, shards_of in cuts:
        steps = jax.random.uniform(jax.random.fold_in(jax.random.fold_in(stream_key, 6), axis_at), (shards_of,), jnp.float32, smallest / len(cuts), largest / len(cuts))
        level = level * jnp.repeat(jnp.exp(steps), dims[axis_at] // shards_of).reshape((-1,) + (1,) * (len(dims) - 1 - axis_at))
    return level


def centred(rng, shape, deviation, bound, split=(), kind=jnp.bfloat16):
    result = jax.random.normal(rng, shape, jnp.float32) * deviation
    if len(split) > 0:
        result = steps_of(rng, shape, split, -0.22, 0.18) * result
    return jnp.clip(result, min=-bound, max=bound).astype(kind)


def setup_inputs(seed: int = 0) -> dict:
    keys = jax.random.split(jax.random.key(seed), 13)
    coarse_field = centred(keys[0], (SAMPLES, NR0, NA0, NB0), 1.0, 6.0, ((1, 4), (2, 8)), jnp.float32)
    excite_mid = centred(keys[1], (SAMPLES, 8, NR0, NA0, NB0), 1.0, 6.0, ((2, 4), (3, 8)), jnp.float32)
    excite_fine = centred(keys[2], (SAMPLES, 8, NR1, NA1, NB1), 1.0, 6.0, ((2, 4), (3, 8)), jnp.float32)
    kernels_mid = centred(keys[3], (NK, 8, 27), 54 ** -0.5, 0.875, (), jnp.float32)
    noise_mid = centred(keys[4], (NK, 8, 8), 32 ** -0.5, 1.0, (), jnp.float32)
    rows_mid = with_ends(jax.random.randint(keys[5], (NR0,), 0, NK), jax.random.fold_in(keys[5], 1), 0, NK - 1).astype(jnp.int32)
    kernels_fine = centred(keys[6], (NK, 8, 27), 54 ** -0.5, 0.875, (), jnp.float32)
    noise_fine = centred(keys[7], (NK, 8, 8), 32 ** -0.5, 1.0, (), jnp.float32)
    rows_fine = with_ends(jax.random.randint(keys[8], (NR1,), 0, NK), jax.random.fold_in(keys[8], 1), 0, NK - 1).astype(jnp.int32)
    emission = jnp.clip(jnp.exp(math.log(3.0) - 2.3025851 * jax.random.uniform(keys[9], (NRF, NAF, NBF), jnp.float32) ** steps_of(keys[9], (NRF, NAF, NBF), ((0, 4), (1, 8)), -0.2, 0.2)), 0.3, 3.0)
    star_bins = with_ends(jax.random.randint(keys[10], (NSTAR, NAF, NBF), 0, NRF), jax.random.fold_in(keys[10], 1), 0, NRF - 1).astype(jnp.int32)
    star_data = centred(keys[11], (NSTAR, NAF, NBF), 0.5, 3.0, ((1, 8),), jnp.float32)
    return dict(coarse_field=coarse_field, excite_mid=excite_mid, excite_fine=excite_fine, kernels_mid=kernels_mid, noise_mid=noise_mid, rows_mid=rows_mid, kernels_fine=kernels_fine, noise_fine=noise_fine, rows_fine=rows_fine, emission=emission, star_bins=star_bins, star_data=star_data)


HIGH = lax.Precision.HIGHEST


def alternate(children):
    count_s, _, count_r, count_a, count_b = children.shape
    folded = children.reshape(count_s, 2, 2, 2, count_r, count_a, count_b)
    folded = folded.transpose(0, 4, 1, 5, 2, 6, 3)
    return folded.reshape(count_s, 2 * count_r, 2 * count_a, 2 * count_b)


def split_children(fine_grid):
    count_s, twice_r, twice_a, twice_b = fine_grid.shape
    folded = fine_grid.reshape(count_s, twice_r // 2, 2, twice_a // 2, 2, twice_b // 2, 2)
    folded = folded.transpose(0, 2, 4, 6, 1, 3, 5)
    return folded.reshape(count_s, 8, twice_r // 2, twice_a // 2, twice_b // 2)


def refine(parent, excite, kernels, noise_table, table_rows):
    count_s, count_r, count_a, count_b = parent.shape
    kernel_rows = kernels[table_rows]
    noise_rows = noise_table[table_rows]
    padded = jnp.pad(parent, ((0, 0), (1, 1), (1, 1), (1, 1)))
    children = jnp.einsum('rcj,sjrab->scrab', noise_rows, excite, precision=HIGH)
    for step_r in range(3):
        for step_a in range(3):
            for step_b in range(3):
                slot = 9 * step_r + 3 * step_a + step_b
                piece = padded[:, step_r:step_r + count_r, step_a:step_a + count_a, step_b:step_b + count_b]
                children = children + jnp.einsum('rc,srab->scrab', kernel_rows[:, :, slot], piece, precision=HIGH)
    return alternate(children)


def coarseward(gradient, kernels, noise_table, table_rows):
    child_grad = split_children(gradient)
    count_s, _, count_r, count_a, count_b = child_grad.shape
    kernel_rows = kernels[table_rows]
    noise_rows = noise_table[table_rows]
    grad_excite = jnp.einsum('rcj,scrab->sjrab', noise_rows, child_grad, precision=HIGH)
    spread = jnp.zeros((count_s, count_r + 2, count_a + 2, count_b + 2), jnp.float32)
    for step_r in range(3):
        for step_a in range(3):
            for step_b in range(3):
                slot = 9 * step_r + 3 * step_a + step_b
                weighted = jnp.einsum('rc,scrab->srab', kernel_rows[:, :, slot], child_grad, precision=HIGH)
                spread = spread.at[:, step_r:step_r + count_r, step_a:step_a + count_a, step_b:step_b + count_b].add(weighted)
    return spread[:, 1:-1, 1:-1, 1:-1], grad_excite


def reference(coarse_field, excite_mid, excite_fine, kernels_mid, noise_mid, rows_mid, kernels_fine, noise_fine, rows_fine, emission, star_bins, star_data):
    middle = refine(coarse_field, excite_mid, kernels_mid, noise_mid, rows_mid)
    fine_field = refine(middle, excite_fine, kernels_fine, noise_fine, rows_fine)
    density = jnp.exp(fine_field)
    spacing = 1.0 / NRF
    layer = spacing * density
    depth = jnp.cumsum(layer, axis=1)
    transmission = jnp.exp(-(depth - layer))
    column = jnp.cumsum(spacing * emission[None] * transmission, axis=1)
    indices = jnp.broadcast_to(star_bins[None], (SAMPLES, NSTAR, NAF, NBF)).astype(jnp.int32)
    predicted = jnp.take_along_axis(column, indices, axis=1)
    residual = star_data[None] - predicted
    row_ids = jnp.arange(NRF, dtype=jnp.int32)[:, None, None]
    weight = jnp.zeros(fine_field.shape, jnp.float32)
    for star in range(NSTAR):
        below = (row_ids < star_bins[star][None])[None]
        term = residual[:, star][:, None] * (predicted[:, star][:, None] - column)
        weight = weight + jnp.where(below, term, jnp.float32(0.0))
    grad_field = -density * weight
    grad_middle, grad_excite_fine = coarseward(grad_field, kernels_fine, noise_fine, rows_fine)
    grad_coarse, grad_excite_mid = coarseward(grad_middle, kernels_mid, noise_mid, rows_mid)
    return grad_coarse, grad_excite_mid, grad_excite_fine, residual
```

```python
import functools
import typing

import jax
import jax.numpy as jnp
from jax import lax
from jax.experimental import pallas as pl
from jax.experimental.pallas import tpu as pltpu
from jax.sharding import PartitionSpec as P

F32 = jnp.float32
BF16 = jnp.bfloat16
VMEM_LIMIT = 48 * 1024 * 1024


class Plan(typing.NamedTuple):
    n: int
    m: int
    s: int
    la: int
    b: int
    stars: int
    w: int
    ra: int
    h: int


def make_plan(mesh, coarse, star_bins):
    n, m = mesh.shape["rad"], mesh.shape["ang"]
    s, rows, la, b = coarse.shape
    w = max(d for d in range(1, min(n, la) + 1) if la % d == 0)
    ra = la // w
    assert rows == 1 and m % 2 == 0 and w % 2 == 0 and (w // 2) * ra >= 2
    return Plan(n, m, s, la, b, star_bins.shape[0], w, ra, n * s)


def forward_rows(g):
    fine = 2 * 2 * g.ra * g.s * 16
    emit = fine + 16 * 4 * g.ra
    mix = emit + g.s * 4 * (2 * g.ra + 2)
    return fine, emit, mix, mix + g.s * 8 * (-(-(g.ra + 4) // 8))


def backward_rows(g):
    excite = 2 * 2 * g.ra * g.s * 16
    resid = excite + 4 * g.s * g.stars * 4 * g.ra
    mid = resid + g.s * 4 * (2 * g.ra + 2)
    coarse = mid + g.s * 8 * (-(-(g.ra + 4) // 8))
    return excite, resid, mid, coarse, coarse + g.s * 8


def pick_columns(length, ways, phase):
    src = lax.broadcasted_iota(jnp.int32, (length * ways, length), 0)
    dst = lax.broadcasted_iota(jnp.int32, (length * ways, length), 1)
    return jnp.where(src == ways * dst + phase, 1.0, 0.0).astype(BF16)


def place_columns(length, ways, phase):
    src = lax.broadcasted_iota(jnp.int32, (length, length * ways), 0)
    dst = lax.broadcasted_iota(jnp.int32, (length, length * ways), 1)
    return jnp.where(dst == ways * src + phase, 1.0, 0.0).astype(BF16)


def thirds(x):
    high = x.astype(BF16)
    rest = x - high.astype(F32)
    middle = rest.astype(BF16)
    return high, middle, (rest - middle.astype(F32)).astype(BF16)


def exact_dot(parts, choice):
    high, middle, low = [jnp.dot(part, choice, preferred_element_type=F32) for part in parts]
    return high + (middle + low)


def along_lanes(x, step):
    if step == 0:
        return x
    size = x.shape[1]
    lane = lax.broadcasted_iota(jnp.int32, x.shape, 1)
    edge = 0 if step > 0 else size - 1
    return jnp.where(lane == edge, 0.0, pltpu.roll(x, step % size, axis=1))


def along_rows(x, step):
    if step == 0:
        return x
    size = x.shape[0]
    row = lax.broadcasted_iota(jnp.int32, x.shape, 0)
    kept = row >= step if step > 0 else row < size + step
    return jnp.where(kept, pltpu.roll(x, step % size, axis=0), 0.0)


def edge_kernel(g, rows_ref, noise_ref, coarse_ref, excite_ref, mix_ref, one_ref, two_ref):
    table = rows_ref[lax.axis_index("rad")]
    even = lax.rem(lax.axis_index("ang"), 2) == 0
    for s in range(g.s):
        for c in range(8):
            total = noise_ref[table, c, 0] * excite_ref[s, 0, 0]
            for j in range(1, 8):
                total = total + noise_ref[table, c, j] * excite_ref[s, j, 0]
            mix_ref[s, c] = total
    for s in range(g.s):
        for t in range(2):
            up, down = coarse_ref[s, 0, g.la - 2 + t : g.la - 1 + t], coarse_ref[s, 0, t : t + 1]
            one_ref[2 * s + t : 2 * s + t + 1] = jnp.where(even, up, down)
            two_ref[2 * s + t : 2 * s + t + 1] = jnp.where(even, down, up)
        for cr in range(2):
            for cb in range(2):
                at = 2 * g.s + 4 * s + 2 * cr + cb
                up, down = mix_ref[s, 4 * cr + 2 + cb, g.la - 1 :], mix_ref[s, 4 * cr + cb, :1]
                one_ref[at : at + 1] = jnp.where(even, up, down)
                two_ref[at : at + 1] = jnp.where(even, down, up)


def scatter_kernel(g, rows_ref, noise_ref, fine_ref, emission_ref, coarse_ref, mix_ref, one_ref, two_ref, *rest):
    out_refs, (raw, split, lit, wide, stage) = rest[: g.n], rest[g.n :]
    me, ang = lax.axis_index("rad"), lax.axis_index("ang")
    b, s_count, la = g.b, g.s, g.la
    for i in range(2):
        table = rows_ref[2 * me + i]
        for s in range(s_count):
            for c in range(8):
                total = noise_ref[table, c, 0] * fine_ref[s, 0, i]
                for j in range(1, 8):
                    total = total + noise_ref[table, c, j] * fine_ref[s, j, i]
                at = ((s * 8 + c) * 2 + i) * 2 * la
                raw[at : at + 2 * la] = total
    parts = thirds(raw[...])
    for phase in range(2):
        split[phase] = exact_dot(parts, pick_columns(b, 2, phase))
    parts = thirds(emission_ref[...].reshape(16 * la, 4 * b))
    for phase in range(4):
        lit[:, phase * b : (phase + 1) * b] = exact_dot(parts, pick_columns(b, 4, phase))

    even = lax.rem(ang, 2) == 0
    before = jnp.where(ang > 0, jnp.where(even, two_ref[...], one_ref[...]), 0.0)
    after = jnp.where(ang < g.m - 1, jnp.where(even, one_ref[...], two_ref[...]), 0.0)
    for s in range(s_count):
        wide[s, :2] = before[2 * s : 2 * s + 2]
        wide[s, 2 : 2 + la] = coarse_ref[s, 0]
        wide[s, 2 + la :] = after[2 * s : 2 * s + 2]

    end_fine, end_emit, end_mix, _ = forward_rows(g)
    for q in range(g.w):
        for phase in range(2):
            for a in range(2 * g.ra):
                for s in range(s_count):
                    at = ((phase * 2 * g.ra + a) * s_count + s) * 16
                    rows = pl.ds(s * 32 * la + 2 * q * g.ra + a, 16, stride=2 * la)
                    stage[q, at : at + 16] = split[phase, rows, :]
        for phase in range(4):
            for f in range(4):
                at = end_fine + (phase * 4 + f) * 4 * g.ra
                rows = slice(f * 4 * la + 4 * q * g.ra, f * 4 * la + 4 * (q + 1) * g.ra)
                stage[q, at : at + 4 * g.ra] = lit[rows, phase * b : (phase + 1) * b]
        for s in range(s_count):
            for row in range(2 * g.ra + 2):
                a, ca = divmod(2 * q * g.ra - 1 + row, 2)
                for cr in range(2):
                    for cb in range(2):
                        at = end_emit + ((s * (2 * g.ra + 2) + row) * 2 + cr) * 2 + cb
                        edge = 2 * s_count + 4 * s + 2 * cr + cb
                        if a < 0:
                            value = before[edge : edge + 1]
                        elif a >= la:
                            value = after[edge : edge + 1]
                        else:
                            value = mix_ref[s, 4 * cr + 2 * ca + cb, a : a + 1]
                        stage[q, at : at + 1] = value
            at = end_mix + 8 * s
            stage[q, at : at + g.ra + 4] = wide[s, q * g.ra : q * g.ra + g.ra + 4]
    for k in range(g.n):
        out_refs[k][...] = stage[jnp.minimum(lax.rem(me + k, g.n), g.w - 1)]


def main_kernel(g, rows_mid, rows_fine, mid_table, fine_table, noise_table, bins_ref, data_ref, *rest):
    in_refs, rest = rest[: g.n], rest[g.n :]
    grad_ref, resid_ref, parent_ref, coarse_out, edge_ref = rest[:5]
    got, fine_in, emit_in, mix_in, coarse_in, weights, spread, coarse_ext, mid_ext, tall = rest[5:]
    me, ang = lax.axis_index("rad"), lax.axis_index("ang")
    n, b, s_count, ra, h = g.n, g.b, g.s, g.ra, g.h
    rows_a = 2 * ra + 2
    spacing = 1.0 / (4 * n)
    worker = jnp.minimum(me, g.w - 1)

    for k in range(n):
        got[lax.rem(me + n - k, n)] = in_refs[k][...]
    end_fine, end_emit, end_mix, _ = forward_rows(g)
    for r in range(n):
        for s in range(s_count):
            sub = r * s_count + s
            for x in range(4 * ra):
                at = (x * s_count + s) * 16
                fine_in[pl.ds(x * 16 * h + sub, 16, stride=h), :] = got[r, at : at + 16]
            emit_in[pl.ds(sub, 64 * ra, stride=h), :] = got[r, end_fine:end_emit]
            at = end_emit + s * 4 * rows_a
            mix_in[pl.ds(sub, 4 * rows_a, stride=h), :] = got[r, at : at + 4 * rows_a]
            at = end_mix + 8 * s
            coarse_in[pl.ds(sub, ra + 4, stride=h), :] = got[r, at : at + ra + 4]

    for r in range(n):
        own = slice(r * s_count, (r + 1) * s_count)
        tables = [mid_table[rows_mid[r]], fine_table[rows_fine[2 * r]], fine_table[rows_fine[2 * r + 1]]]
        for level, table in enumerate(tables):
            for c in range(8):
                weights[level, c, own] = jnp.broadcast_to(table[c : c + 1], (s_count, 27))
    for level in range(3):
        for c in range(8):
            tile = weights[level, c]
            for o in range(27):
                spread[(level * 8 + c) * 27 + o] = jnp.broadcast_to(tile[:, o : o + 1], (h, b))

    first = ang * g.la + worker * ra
    top_in = jnp.where(first > 0, 1.0, 0.0).astype(F32)
    bottom_in = jnp.where(first + ra < g.m * g.la, 1.0, 0.0).astype(F32)
    for a in range(ra + 4):
        x = coarse_in[a * h : (a + 1) * h]
        for db in range(3):
            shifted = along_lanes(x, 1 - db)
            for dr in range(3):
                coarse_ext[dr, a, db] = along_rows(shifted, (1 - dr) * s_count)
    for cr in range(2):
        for row in range(rows_a):
            a, ca = divmod(row - 1, 2)
            for cb in range(2):
                c = 4 * cr + 2 * ca + cb
                at = (row * 4 + 2 * cr + cb) * h
                total = mix_in[at : at + h]
                for dr in range(3):
                    for da in range(3):
                        for db in range(3):
                            o = 9 * dr + 3 * da + db
                            total = total + spread[c * 27 + o] * coarse_ext[dr, a + 1 + da, db]
                if row == 0:
                    total = total * top_in
                if row == rows_a - 1:
                    total = total * bottom_in
                for bi, step_b in ((1 + cb, 0), (3, -1) if cb == 0 else (0, 1)):
                    shifted = along_lanes(total, step_b)
                    for ri, step_r in ((1 + cr, 0), (3, -1) if cr == 0 else (0, 1)):
                        mid_ext[ri, row, bi] = along_rows(shifted, step_r * s_count)

    def fine_cells(c, carry):
        cr, ca, cb = c // 4, lax.rem(c // 2, 2), lax.rem(c, 2)
        for pr in range(2):
            weight = [spread[((1 + pr) * 8 + c) * 27 + o] for o in range(27)]
            for a in range(2 * ra):
                for pb in range(2):
                    at = (((pb * 2 * ra + a) * 8 + c) * 2 + pr) * h
                    total = fine_in[pl.ds(pl.multiple_of(at, 8), h), :]
                    for dr in range(3):
                        for da in range(3):
                            for db in range(3):
                                o = 9 * dr + 3 * da + db
                                total = total + weight[o] * mid_ext[pr + dr, a + da, pb + db]
                    grad_ref[2 * pr + cr, 2 * a + ca, 2 * pb + cb] = total
        return carry

    lax.fori_loop(0, 8, fine_cells, 0)

    radial = 4 * (lax.broadcasted_iota(jnp.int32, (h, b), 0) // s_count)

    def sum_before(x):
        step = s_count
        while step < h:
            x = x + along_rows(x, step)
            step *= 2
        return along_rows(x, s_count)

    def sum_all(x):
        step = s_count
        while step < h:
            x = x + pltpu.roll(x, step, axis=0)
            step *= 2
        return x

    def position(at, carry):
        a, pb = at // 4, lax.rem(at, 4)
        density = [jnp.exp(grad_ref[f, a, pb]) for f in range(4)]
        layer = [spacing * d for d in density]
        depth = sum_before(layer[0] + layer[1] + layer[2] + layer[3])
        glow = []
        for f in range(4):
            where_emit = pl.multiple_of(((pb * 4 + f) * 4 * ra + a) * h, 8)
            glow.append(spacing * emit_in[pl.ds(where_emit, h), :] * jnp.exp(-depth))
            depth = depth + layer[f]
        running = sum_before(glow[0] + glow[1] + glow[2] + glow[3])
        column = []
        for f in range(4):
            running = running + glow[f]
            column.append(running)
        total = [jnp.zeros((h, b), F32) for f in range(4)]
        for star in range(g.stars):
            row = (star * 4 * ra + a) * 4 + pb
            bins = jnp.broadcast_to(bins_ref[pl.ds(row, 1), :], (h, b))
            data = jnp.broadcast_to(data_ref[pl.ds(row, 1), :], (h, b))
            bins = bins - radial
            mine = jnp.where(bins == 0, column[0], 0.0)
            for f in range(1, 4):
                mine = jnp.where(bins == f, column[f], mine)
            predicted = sum_all(mine)
            residual = data - predicted
            resid_ref[star, a, pb] = residual
            for f in range(4):
                total[f] = total[f] + jnp.where(bins > f, residual * (predicted - column[f]), 0.0)
        for f in range(4):
            grad_ref[f, a, pb] = -density[f] * total[f]
        return carry

    lax.fori_loop(0, 16 * ra, position, 0)

    tall[...] = jnp.zeros(tall.shape, F32)
    for pr in range(2):
        def gather(c, carry, pr=pr):
            cr, ca, cb = c // 4, lax.rem(c // 2, 2), lax.rem(c, 2)
            cells = {(a, pb): grad_ref[2 * pr + cr, 2 * a + ca, 2 * pb + cb] for a in range(2 * ra) for pb in range(2)}
            for dr in range(3):
                sums = {}
                for da in range(3):
                    for db in range(3):
                        weight = spread[((1 + pr) * 8 + c) * 27 + 9 * dr + 3 * da + db]
                        for (a, pb), cell in cells.items():
                            key = (a + da, pb + db)
                            term = weight * cell
                            sums[key] = sums[key] + term if key in sums else term
                for (row, bi), value in sums.items():
                    tall[pr + dr, row, bi] += value
            return carry

        lax.fori_loop(0, 8, gather, 0)
    for row in range(rows_a):
        for pr in range(2):
            for pb in range(2):
                bi, step_b = (3, 1) if pb == 0 else (0, -1)
                ri, step_r = (3, 1) if pr == 0 else (0, -1)
                near = tall[1 + pr, row, 1 + pb] + along_lanes(tall[1 + pr, row, bi], step_b)
                far = tall[ri, row, 1 + pb] + along_lanes(tall[ri, row, bi], step_b)
                value = near + along_rows(far, step_r * s_count)
                if row == 0:
                    value = value * top_in
                if row == rows_a - 1:
                    value = value * bottom_in
                parent_ref[2 * pr + pb, row] = value

    for a in range(ra + 4):
        coarse_out[a] = jnp.zeros((h, b), F32)
    for dr in range(3):
        for db in range(3):
            sums = {}
            for cr in range(2):
                for row in range(rows_a):
                    a, ca = divmod(row - 1, 2)
                    for cb in range(2):
                        cell = parent_ref[2 * cr + cb, row]
                        for da in range(3):
                            c, o = 4 * cr + 2 * ca + cb, 9 * dr + 3 * da + db
                            term = spread[c * 27 + o] * cell
                            key = a + 1 + da
                            sums[key] = sums[key] + term if key in sums else term
            for a, value in sums.items():
                coarse_out[a] += along_lanes(along_rows(value, (dr - 1) * s_count), db - 1)

    for q in range(g.w):
        @pl.when(worker == q)
        def _(q=q):
            low = q < g.w // 2
            for x in range(4):
                if q == 0 or q == g.w - 1:
                    edge_ref[x] = parent_ref[x, 0 if low else rows_a - 1]
                else:
                    edge_ref[x] = jnp.zeros((h, b), F32)
            for t in range(2):
                a = (t - 2 if low else g.la + t) - q * ra + 2
                if 0 <= a < ra + 4:
                    edge_ref[4 + t] = coarse_out[a]
                else:
                    edge_ref[4 + t] = jnp.zeros((h, b), F32)


def gather_kernel(g, rows_fine, noise_table, grad_ref, resid_ref, parent_ref, coarse_ref, edge_ref, *rest):
    out_refs, (weights, excite, joined, seen, stage) = rest[: g.n], rest[g.n :]
    me, ang = lax.axis_index("rad"), lax.axis_index("ang")
    n, b, s_count, ra, h = g.n, g.b, g.s, g.ra, g.h
    rows_a = 2 * ra + 2
    for r in range(n):
        for i in range(2):
            table = noise_table[rows_fine[2 * r + i]]
            for c in range(8):
                weights[i, c, r * s_count : (r + 1) * s_count] = jnp.broadcast_to(table[c : c + 1], (s_count, 8))
    for i in range(2):
        tiles = [weights[i, c] for c in range(8)]
        for j in range(8):
            weight = [jnp.broadcast_to(tile[:, j : j + 1], (h, b)) for tile in tiles]
            for a in range(2 * ra):
                at = ((a * 8 + j) * 2 + i) * h
                for pb in range(2):
                    total = None
                    for c in range(8):
                        cr, ca, cb = c // 4, c // 2 % 2, c % 2
                        term = weight[c] * grad_ref[2 * i + cr, 2 * a + ca, 2 * pb + cb]
                        total = term if total is None else total + term
                    excite[at : at + h, pb * b : (pb + 1) * b] = total
    order = jnp.concatenate([place_columns(b, 2, phase) for phase in range(2)], axis=0)
    parts = thirds(excite[...])
    for half in range(2):
        joined[half] = exact_dot(parts, order[:, half * b : (half + 1) * b])
    for star in range(g.stars):
        for a in range(4 * ra):
            for pb in range(4):
                for s in range(s_count):
                    row = (s * g.stars + star) * 4 * ra + a
                    seen[row : row + 1, pb * b : (pb + 1) * b] = resid_ref[star, a, pb, s : s + 1]
    order = jnp.concatenate([place_columns(b, 4, phase) for phase in range(4)], axis=0)
    shown = exact_dot(thirds(seen[...]), order)

    live = jnp.where(worker_low(g, me), ang < g.m - 1, ang > 0)
    end_excite, end_resid, end_mid, end_coarse, _ = backward_rows(g)
    per = 4 * g.stars * ra
    parents = parent_ref.reshape(4 * rows_a * h, b)
    coarse = coarse_ref.reshape((ra + 4) * h, b)
    edges = edge_ref.reshape(6 * h, b)
    for r in range(n):
        for s in range(s_count):
            sub = r * s_count + s
            for half in range(2):
                for a in range(2 * ra):
                    at = ((half * 2 * ra + a) * s_count + s) * 16
                    rows = pl.ds(a * 16 * h + sub, 16, stride=h)
                    stage[r, at : at + 16] = joined[half, rows, :]
            for part in range(4):
                at = end_excite + (part * s_count + s) * per
                stage[r, at : at + per] = shown[s * per : (s + 1) * per, part * b : (part + 1) * b]
            at = end_resid + s * 4 * rows_a
            stage[r, at : at + 4 * rows_a] = parents[pl.ds(sub, 4 * rows_a, stride=h), :]
            at = end_mid + 8 * s
            stage[r, at : at + ra + 4] = coarse[pl.ds(sub, ra + 4, stride=h), :]
            at = end_coarse + 8 * s
            stage[r, at : at + 6] = jnp.where(live, edges[pl.ds(sub, 6, stride=h), :], 0.0)
    for k in range(n):
        out_refs[k][...] = stage[lax.rem(me + k, n)]


def worker_low(g, me):
    return jnp.minimum(me, g.w - 1) < g.w // 2


def owner_kernel(g, rows_mid, noise_mid, *rest):
    in_refs, rest = rest[: g.n], rest[g.n :]
    coarse_out, mid_out, fine_out, resid_out, got, fine, grad_mid, grad_coarse = rest
    me = lax.axis_index("rad")
    n, b, s_count, ra, la = g.n, g.b, g.s, g.ra, g.la
    rows_a = 2 * ra + 2
    end_excite, end_resid, end_mid, end_coarse, _ = backward_rows(g)
    per = 4 * g.stars * ra
    for k in range(n):
        got[lax.rem(me + n - k, n)] = in_refs[k][...]
    grad_mid[...] = jnp.zeros(grad_mid.shape, F32)
    grad_coarse[...] = jnp.zeros(grad_coarse.shape, F32)
    for q in range(g.w):
        for s in range(s_count):
            for half in range(2):
                for a in range(2 * ra):
                    at = ((half * 2 * ra + a) * s_count + s) * 16
                    rows = pl.ds(s * 32 * la + 2 * q * ra + a, 16, stride=2 * la)
                    fine[half, rows, :] = got[q, at : at + 16]
            for part in range(4):
                for star in range(g.stars):
                    at = end_excite + (part * s_count + s) * per + star * 4 * ra
                    rows = slice(4 * q * ra, 4 * (q + 1) * ra)
                    resid_out[s, star, rows, part * b : (part + 1) * b] = got[q, at : at + 4 * ra]
            for x in range(4):
                at = end_resid + s * 4 * rows_a + x * rows_a
                grad_mid[s, x, 2 * q * ra : 2 * q * ra + rows_a] += got[q, at : at + rows_a]
                at = end_coarse + 8 * s + x
                row = 2 * la if q < g.w // 2 else 1
                grad_mid[s, x, row : row + 1] += got[q, at : at + 1]
            at = end_mid + 8 * s
            grad_coarse[s, q * ra : q * ra + ra + 4] += got[q, at : at + ra + 4]
            at = end_coarse + 8 * s + 4
            row = la if q < g.w // 2 else 2
            grad_coarse[s, row : row + 2] += got[q, at : at + 2]
    for half in range(2):
        fine_out[..., half * b : (half + 1) * b] = fine[half].reshape(s_count, 8, 2, 2 * la, b)
    table = rows_mid[me]
    for s in range(s_count):
        coarse_out[s, 0] = grad_coarse[s, 2 : 2 + la]
        cells = []
        for c in range(8):
            cr, ca, cb = c // 4, c // 2 % 2, c % 2
            cells.append(grad_mid[s, 2 * cr + cb, pl.ds(1 + ca, la, stride=2), :])
        for j in range(8):
            total = noise_mid[table, 0, j] * cells[0]
            for c in range(1, 8):
                total = total + noise_mid[table, c, j] * cells[c]
            mid_out[s, j, 0] = total


def star_kernel(g, bins_ref, data_ref, bins_out, data_out, gathered):
    worker = jnp.minimum(lax.axis_index("rad"), g.w - 1)
    per, b = 4 * g.ra, g.b
    for q in range(g.w):
        @pl.when(worker == q)
        def _(q=q):
            for star in range(g.stars):
                gathered[0, star * per : (star + 1) * per] = bins_ref[star, q * per : (q + 1) * per].astype(F32)
                gathered[1, star * per : (star + 1) * per] = data_ref[star, q * per : (q + 1) * per]
    bins = gathered[0].astype(BF16)
    parts = thirds(gathered[1])
    for phase in range(4):
        choice = pick_columns(b, 4, phase)
        rows = pl.ds(phase, g.stars * per, stride=4)
        bins_out[rows, :] = jnp.dot(bins, choice, preferred_element_type=F32).astype(jnp.int32)
        data_out[rows, :] = exact_dot(parts, choice)


def call(kernel, name, outs, operands, scratch, scalars):
    smem, vmem = pl.BlockSpec(memory_space=pltpu.SMEM), pl.BlockSpec(memory_space=pltpu.VMEM)
    return pl.pallas_call(
        kernel,
        name=name,
        out_shape=[jax.ShapeDtypeStruct(shape, kind) for shape, kind in outs],
        in_specs=[smem] * scalars + [vmem] * (len(operands) - scalars),
        out_specs=[vmem] * len(outs),
        scratch_shapes=[pltpu.VMEM(shape, F32) for shape in scratch],
        compiler_params=pltpu.CompilerParams(vmem_limit_bytes=VMEM_LIMIT),
    )(*operands)


def per_device(
    g,
    coarse_field,
    excite_mid,
    excite_fine,
    kernels_mid,
    noise_mid,
    rows_mid,
    kernels_fine,
    noise_fine,
    rows_fine,
    emission,
    star_bins,
    star_data,
):
    n, m, s, la, b, stars, w, ra, h = g
    kernel = functools.partial
    pairs = [(i, i ^ 1) for i in range(m)]
    between = [(i, (i + 1) % m if i % 2 else (i - 1) % m) for i in range(m)]

    def around(k):
        return [(i, (i + k) % n) for i in range(n)]

    edge_rows = ((6 * s + 7) // 8 * 8, b)
    mixed, one, two = call(
        kernel(edge_kernel, g),
        "edges",
        [((s, 8, la, b), F32), (edge_rows, F32), (edge_rows, F32)],
        (rows_mid, noise_mid, coarse_field, excite_mid),
        [],
        2,
    )
    one, two = lax.ppermute(one, "ang", pairs), lax.ppermute(two, "ang", between)
    sent = call(
        kernel(scatter_kernel, g),
        "scatter",
        [((forward_rows(g)[-1], b), F32)] * n,
        (rows_fine, noise_fine, excite_fine, emission, coarse_field, mixed, one, two),
        [
            (32 * s * la, 2 * b),
            (2, 32 * s * la, b),
            (16 * la, 4 * b),
            (s, la + 4, b),
            (w, forward_rows(g)[-1], b),
        ],
        2,
    )
    got = [sent[0]] + [lax.ppermute(sent[k], "rad", around(k)) for k in range(1, n)]
    bins, data = call(
        kernel(star_kernel, g),
        "stars",
        [((16 * stars * ra, b), jnp.int32), ((16 * stars * ra, b), F32)],
        (star_bins, star_data),
        [(2, 4 * stars * ra, 4 * b)],
        0,
    )
    rows_a = 2 * ra + 2
    grad, resid, parent, coarse, edge = call(
        kernel(main_kernel, g),
        "main",
        [
            ((4, 4 * ra, 4, h, b), F32),
            ((stars, 4 * ra, 4, h, b), F32),
            ((4, rows_a, h, b), F32),
            ((ra + 4, h, b), F32),
            ((6, h, b), F32),
        ],
        (rows_mid, rows_fine, kernels_mid, kernels_fine, noise_fine, bins, data, *got),
        [
            (n, forward_rows(g)[-1], b),
            (64 * ra * h, b),
            (64 * ra * h, b),
            (4 * rows_a * h, b),
            ((ra + 4) * h, b),
            (3, 8, h, 27),
            (3 * 8 * 27, h, b),
            (3, ra + 4, 3, h, b),
            (4, rows_a, 4, h, b),
            (4, rows_a, 4, h, b),
        ],
        2,
    )
    sideways = [
        (r * m + a, r * m + (a - 1 if min(r, w - 1) < w // 2 else a + 1) % m) for r in range(n) for a in range(m)
    ]
    edge = lax.ppermute(edge, ("rad", "ang"), sideways)
    back = call(
        kernel(gather_kernel, g),
        "gather",
        [((backward_rows(g)[-1], b), F32)] * n,
        (rows_fine, noise_fine, grad, resid, parent, coarse, edge),
        [
            (2, 8, h, 8),
            (32 * ra * h, 2 * b),
            (2, 32 * ra * h, b),
            (4 * stars * ra * s, 4 * b),
            (n, backward_rows(g)[-1], b),
        ],
        1,
    )
    back = [back[0]] + [lax.ppermute(back[k], "rad", around(k)) for k in range(1, n)]
    return tuple(
        call(
            kernel(owner_kernel, g),
            "owner",
            [
                ((s, 1, la, b), F32),
                ((s, 8, 1, la, b), F32),
                ((s, 8, 2, 2 * la, 2 * b), F32),
                ((s, stars, 4 * la, 4 * b), F32),
            ],
            (rows_mid, noise_mid, *back),
            [(n, backward_rows(g)[-1], b), (2, 32 * s * la, b), (s, 4, 2 * la + 2, b), (s, la + 4, b)],
            2,
        )
    )


def solution(mesh):
    placed = (
        P(None, "rad", "ang", None),
        P(None, None, "rad", "ang", None),
        P(None, None, "rad", "ang", None),
        P(),
        P(),
        P(),
        P(),
        P(),
        P(),
        P("rad", "ang", None),
        P(None, "ang", None),
        P(None, "ang", None),
    )

    def local(*args):
        return per_device(make_plan(mesh, args[0], args[10]), *args)

    return jax.shard_map(
        local,
        mesh=mesh,
        in_specs=placed,
        out_specs=(
            P(None, "rad", "ang", None),
            P(None, None, "rad", "ang", None),
            P(None, None, "rad", "ang", None),
            P(None, None, "ang", None),
        ),
        check_vma=False,
    )
```

```python
import functools
import typing

import jax
import jax.numpy as jnp
from jax import lax
from jax.experimental import pallas as pl
from jax.experimental.pallas import tpu as pltpu
from jax.sharding import PartitionSpec as P

F32 = jnp.float32
BF16 = jnp.bfloat16
VMEM_LIMIT = 24 * 1024 * 1024


class Plan(typing.NamedTuple):
    n: int
    m: int
    s: int
    la: int
    b: int
    stars: int
    w: int
    ra: int
    h: int


def make_plan(mesh, coarse, star_bins):
    n, m = mesh.shape["rad"], mesh.shape["ang"]
    s, rows, la, b = coarse.shape
    w = max(d for d in range(1, min(n, la) + 1) if la % d == 0)
    ra = la // w
    assert rows == 1 and m % 2 == 0 and w % 2 == 0 and (w // 2) * ra >= 2
    return Plan(n, m, s, la, b, star_bins.shape[0], w, ra, n * s)


def forward_rows(g):
    fine = 2 * 2 * g.ra * g.s * 16
    emit = fine + 16 * 4 * g.ra
    mix = emit + g.s * 4 * (2 * g.ra + 2)
    return fine, emit, mix, -(-(mix + g.s * (g.ra + 4)) // 8) * 8


def backward_rows(g):
    excite = 2 * 2 * g.ra * g.s * 16
    resid = excite + 4 * g.s * g.stars * 4 * g.ra
    mid = resid + g.s * 4 * (2 * g.ra + 2)
    coarse = mid + g.s * (g.ra + 4)
    return excite, resid, mid, coarse, -(-(coarse + 6 * g.s) // 8) * 8


def table_weights(table_ref, entry):
    lane = lax.broadcasted_iota(jnp.int32, table_ref.shape[1:], 1)
    columns = [
        jnp.sum(jnp.where(lane == entry, table_ref[c], 0.0), axis=1, keepdims=True) for c in range(table_ref.shape[0])
    ]
    return lambda c, j: columns[c][j : j + 1]


def fetch(pairs, sems):
    copies = [pltpu.make_async_copy(source, here, sems.at[i]) for i, (source, here) in enumerate(pairs)]
    for copy in copies:
        copy.start()
    for copy in copies:
        copy.wait()


def pick_columns(length, ways, phase):
    src = lax.broadcasted_iota(jnp.int32, (length * ways, length), 0)
    dst = lax.broadcasted_iota(jnp.int32, (length * ways, length), 1)
    return jnp.where(src == ways * dst + phase, 1.0, 0.0).astype(BF16)


def place_columns(length, ways, phase):
    src = lax.broadcasted_iota(jnp.int32, (length, length * ways), 0)
    dst = lax.broadcasted_iota(jnp.int32, (length, length * ways), 1)
    return jnp.where(dst == ways * src + phase, 1.0, 0.0).astype(BF16)


def thirds(x):
    high = x.astype(BF16)
    rest = x - high.astype(F32)
    middle = rest.astype(BF16)
    return high, middle, (rest - middle.astype(F32)).astype(BF16)


def exact_dot(parts, choice):
    high, middle, low = [jnp.dot(part, choice, preferred_element_type=F32) for part in parts]
    return high + (middle + low)


def along_lanes(x, step):
    if step == 0:
        return x
    size = x.shape[1]
    lane = lax.broadcasted_iota(jnp.int32, x.shape, 1)
    edge = 0 if step > 0 else size - 1
    return jnp.where(lane == edge, 0.0, pltpu.roll(x, step % size, axis=1))


def along_rows(x, step):
    if step == 0:
        return x
    size = x.shape[0]
    row = lax.broadcasted_iota(jnp.int32, x.shape, 0)
    kept = row >= step if step > 0 else row < size + step
    return jnp.where(kept, pltpu.roll(x, step % size, axis=0), 0.0)


def edge_kernel(g, rows_hbm, noise_hbm, coarse_hbm, excite_hbm, mix_ref, one_ref, two_ref, *rest):
    rows_ref, noise_ref, coarse_ref, excite_ref, sems = rest
    fetch(
        [(rows_hbm, rows_ref), (noise_hbm, noise_ref), (coarse_hbm, coarse_ref), (excite_hbm, excite_ref)], sems
    )
    even = lax.rem(lax.axis_index("ang"), 2) == 0
    weight = table_weights(noise_ref, rows_ref[lax.axis_index("rad")])
    for c in range(8):
        for s in range(g.s):
            total = weight(c, 0) * excite_ref[s, 0, 0]
            for j in range(1, 8):
                total = total + weight(c, j) * excite_ref[s, j, 0]
            mix_ref[s, c] = total
    for s in range(g.s):
        up, down = coarse_ref[s, 0, g.la - 2 :], coarse_ref[s, 0, :2]
        one_ref[2 * s : 2 * s + 2] = jnp.where(even, up, down)
        two_ref[2 * s : 2 * s + 2] = jnp.where(even, down, up)
        for cr in range(2):
            for cb in range(2):
                at = 2 * g.s + 4 * s + 2 * cr + cb
                up, down = mix_ref[s, 4 * cr + 2 + cb, g.la - 1 :], mix_ref[s, 4 * cr + cb, :1]
                one_ref[at : at + 1] = jnp.where(even, up, down)
                two_ref[at : at + 1] = jnp.where(even, down, up)


def scatter_kernel(g, rows_hbm, noise_hbm, fine_hbm, emission_hbm, coarse_hbm, mix_ref, one_ref, two_ref, *rest):
    out_refs, rest = rest[: g.n], rest[g.n :]
    rows_ref, noise_ref, fine_ref, emission_ref, coarse_ref, sems, raw, split, lit, wide, stage = rest
    fetch(
        [
            (rows_hbm, rows_ref),
            (noise_hbm, noise_ref),
            (coarse_hbm, coarse_ref),
            (fine_hbm, fine_ref),
            (emission_hbm, emission_ref),
        ],
        sems,
    )
    me, ang = lax.axis_index("rad"), lax.axis_index("ang")
    b, s_count, la = g.b, g.s, g.la
    for i in range(2):
        weight = table_weights(noise_ref, rows_ref[2 * me + i])
        for c in range(8):
            weights = [weight(c, j) for j in range(8)]
            for s in range(s_count):
                total = weights[0] * fine_ref[s, 0, i]
                for j in range(1, 8):
                    total = total + weights[j] * fine_ref[s, j, i]
                at = ((s * 8 + c) * 2 + i) * 2 * la
                raw[at : at + 2 * la] = total
    parts = thirds(raw[...])
    for phase in range(2):
        split[phase] = exact_dot(parts, pick_columns(b, 2, phase))
    parts = thirds(emission_ref[...].reshape(16 * la, 4 * b))
    for phase in range(4):
        lit[:, phase * b : (phase + 1) * b] = exact_dot(parts, pick_columns(b, 4, phase))

    even = lax.rem(ang, 2) == 0
    before = jnp.where(ang > 0, jnp.where(even, two_ref[...], one_ref[...]), 0.0)
    after = jnp.where(ang < g.m - 1, jnp.where(even, one_ref[...], two_ref[...]), 0.0)
    for s in range(s_count):
        wide[s, :2] = before[2 * s : 2 * s + 2]
        wide[s, 2 : 2 + la] = coarse_ref[s, 0]
        wide[s, 2 + la :] = after[2 * s : 2 * s + 2]

    end_fine, end_emit, end_mix, _ = forward_rows(g)
    for q in range(g.w):
        for phase in range(2):
            for a in range(2 * g.ra):
                for s in range(s_count):
                    at = ((phase * 2 * g.ra + a) * s_count + s) * 16
                    rows = pl.ds(s * 32 * la + 2 * q * g.ra + a, 16, stride=2 * la)
                    stage[q, at : at + 16] = split[phase, rows, :]
        for phase in range(4):
            for f in range(4):
                at = end_fine + (phase * 4 + f) * 4 * g.ra
                rows = slice(f * 4 * la + 4 * q * g.ra, f * 4 * la + 4 * (q + 1) * g.ra)
                stage[q, at : at + 4 * g.ra] = lit[rows, phase * b : (phase + 1) * b]
        for s in range(s_count):
            for row in range(2 * g.ra + 2):
                a, ca = divmod(2 * q * g.ra - 1 + row, 2)
                for cr in range(2):
                    for cb in range(2):
                        at = end_emit + ((s * (2 * g.ra + 2) + row) * 2 + cr) * 2 + cb
                        edge = 2 * s_count + 4 * s + 2 * cr + cb
                        if a < 0:
                            value = before[edge : edge + 1]
                        elif a >= la:
                            value = after[edge : edge + 1]
                        else:
                            value = mix_ref[s, 4 * cr + 2 * ca + cb, a : a + 1]
                        stage[q, at : at + 1] = value
            at = end_mix + (g.ra + 4) * s
            stage[q, at : at + g.ra + 4] = wide[s, q * g.ra : q * g.ra + g.ra + 4]
    for k in range(g.n):
        out_refs[k][...] = stage[jnp.minimum(lax.rem(me + k, g.n), g.w - 1)]


def weight_kernel(g, rows_mid, rows_fine, mid_table, fine_table, spread, weights):
    for r in range(g.n):
        own = slice(r * g.s, (r + 1) * g.s)
        tables = [mid_table[rows_mid[r]], fine_table[rows_fine[2 * r]], fine_table[rows_fine[2 * r + 1]]]
        for level, table in enumerate(tables):
            for c in range(8):
                weights[level, c, own] = jnp.broadcast_to(table[c : c + 1], (g.s, 27))
    for level in range(3):
        for c in range(8):
            tile = weights[level, c]
            for o in range(27):
                spread[(level * 8 + c) * 27 + o] = jnp.broadcast_to(tile[:, o : o + 1], (g.h, g.b))


def main_kernel(g, spread, bins_ref, data_ref, *rest):
    n, b, s_count, ra, h = g.n, g.b, g.s, g.ra, g.h
    in_refs, rest = rest[:n], rest[n:]
    cells, seen, parent, coarse_sum, edge_sum = rest[:5]
    got, fine_in, emit_in, mix_in, coarse_in, coarse_ext, mid_ext, tall = rest[5:]
    me, ang = lax.axis_index("rad"), lax.axis_index("ang")
    rows_a = 2 * ra + 2
    spacing = 1.0 / (4 * n)
    worker = jnp.minimum(me, g.w - 1)

    for k in range(n):
        source = lax.rem(me + n - k, n)
        got[source] = in_refs[k][...]
    end_fine, end_emit, end_mix, _ = forward_rows(g)
    for r in range(n):
        for s in range(s_count):
            sub = r * s_count + s
            for x in range(4 * ra):
                at = (x * s_count + s) * 16
                fine_in[pl.ds(x * 16 * h + sub, 16, stride=h), :] = got[r, at : at + 16]
            emit_in[pl.ds(sub, 64 * ra, stride=h), :] = got[r, end_fine:end_emit]
            at = end_emit + s * 4 * rows_a
            mix_in[pl.ds(sub, 4 * rows_a, stride=h), :] = got[r, at : at + 4 * rows_a]
            at = end_mix + (ra + 4) * s
            coarse_in[pl.ds(sub, ra + 4, stride=h), :] = got[r, at : at + ra + 4]

    first = ang * g.la + worker * ra
    top_in = jnp.where(first > 0, 1.0, 0.0).astype(F32)
    bottom_in = jnp.where(first + ra < g.m * g.la, 1.0, 0.0).astype(F32)
    for a in range(ra + 4):
        x = coarse_in[a * h : (a + 1) * h]
        for db in range(3):
            shifted = along_lanes(x, 1 - db)
            for dr in range(3):
                coarse_ext[dr, a, db] = along_rows(shifted, (1 - dr) * s_count)
    for cr in range(2):
        for row in range(rows_a):
            a, ca = divmod(row - 1, 2)
            for cb in range(2):
                c = 4 * cr + 2 * ca + cb
                at = (row * 4 + 2 * cr + cb) * h
                total = mix_in[at : at + h]
                for dr in range(3):
                    for da in range(3):
                        for db in range(3):
                            o = 9 * dr + 3 * da + db
                            total = total + spread[c * 27 + o] * coarse_ext[dr, a + 1 + da, db]
                if row == 0:
                    total = total * top_in
                if row == rows_a - 1:
                    total = total * bottom_in
                for bi, step_b in ((1 + cb, 0), (3, -1) if cb == 0 else (0, 1)):
                    shifted = along_lanes(total, step_b)
                    for ri, step_r in ((1 + cr, 0), (3, -1) if cr == 0 else (0, 1)):
                        mid_ext[ri, row, bi] = along_rows(shifted, step_r * s_count)

    def cell_rows(a, c, pr):
        return pl.ds(pl.multiple_of(((a * 8 + c) * 2 + pr) * h, 8), h)

    def fine_cells(c, carry):
        for pr in range(2):
            weight = [spread[((1 + pr) * 8 + c) * 27 + o] for o in range(27)]
            for a in range(2 * ra):
                for pb in range(2):
                    at = (((pb * 2 * ra + a) * 8 + c) * 2 + pr) * h
                    total = fine_in[pl.ds(pl.multiple_of(at, 8), h), :]
                    for dr in range(3):
                        for da in range(3):
                            for db in range(3):
                                o = 9 * dr + 3 * da + db
                                total = total + weight[o] * mid_ext[pr + dr, a + da, pb + db]
                    cells[pb, cell_rows(a, c, pr), :] = total
        return carry

    lax.fori_loop(0, 8, fine_cells, 0)

    radial = 4 * (lax.broadcasted_iota(jnp.int32, (h, b), 0) // s_count)

    def sum_before(x):
        step = s_count
        while step < h:
            x = x + along_rows(x, step)
            step *= 2
        return along_rows(x, s_count)

    def sum_all(x):
        step = s_count
        while step < h:
            x = x + pltpu.roll(x, step, axis=0)
            step *= 2
        return x

    def position(at, carry):
        a, pb = at // 4, lax.rem(at, 4)
        half = pb // 2
        rows = [cell_rows(a // 2, 4 * (f % 2) + 2 * lax.rem(a, 2) + lax.rem(pb, 2), f // 2) for f in range(4)]
        density = [jnp.exp(cells[half, rows[f], :]) for f in range(4)]
        layer = [spacing * d for d in density]
        depth = sum_before(layer[0] + layer[1] + layer[2] + layer[3])
        glow = []
        for f in range(4):
            where_emit = pl.multiple_of(((pb * 4 + f) * 4 * ra + a) * h, 8)
            glow.append(spacing * emit_in[pl.ds(where_emit, h), :] * jnp.exp(-depth))
            depth = depth + layer[f]
        running = sum_before(glow[0] + glow[1] + glow[2] + glow[3])
        column = []
        for f in range(4):
            running = running + glow[f]
            column.append(running)
        total = [jnp.zeros((h, b), F32) for f in range(4)]
        for star in range(g.stars):
            row = (star * 4 * ra + a) * 4 + pb
            bins = jnp.broadcast_to(bins_ref[pl.ds(row, 1), :], (h, b))
            data = jnp.broadcast_to(data_ref[pl.ds(row, 1), :], (h, b))
            bins = bins - radial
            mine = jnp.where(bins == 0, column[0], 0.0)
            for f in range(1, 4):
                mine = jnp.where(bins == f, column[f], mine)
            predicted = sum_all(mine)
            residual = data - predicted
            for s in range(s_count):
                seen[pb, pl.ds((s * g.stars + star) * 4 * ra + a, 1), :] = residual[s : s + 1]
            for f in range(4):
                total[f] = total[f] + jnp.where(bins > f, residual * (predicted - column[f]), 0.0)
        for f in range(4):
            cells[half, rows[f], :] = -density[f] * total[f]
        return carry

    lax.fori_loop(0, 16 * ra, position, 0)

    tall[...] = jnp.zeros(tall.shape, F32)
    for pr in range(2):
        def gather(c, carry, pr=pr):
            values = {(a, pb): cells[pb, cell_rows(a, c, pr), :] for a in range(2 * ra) for pb in range(2)}
            for dr in range(3):
                sums = {}
                for da in range(3):
                    for db in range(3):
                        weight = spread[((1 + pr) * 8 + c) * 27 + 9 * dr + 3 * da + db]
                        for (a, pb), value in values.items():
                            key = (a + da, pb + db)
                            term = weight * value
                            sums[key] = sums[key] + term if key in sums else term
                for (row, bi), value in sums.items():
                    tall[pr + dr, row, bi] += value
            return carry

        lax.fori_loop(0, 8, gather, 0)
    for row in range(rows_a):
        for pr in range(2):
            for pb in range(2):
                bi, step_b = (3, 1) if pb == 0 else (0, -1)
                ri, step_r = (3, 1) if pr == 0 else (0, -1)
                close = tall[1 + pr, row, 1 + pb] + along_lanes(tall[1 + pr, row, bi], step_b)
                far = tall[ri, row, 1 + pb] + along_lanes(tall[ri, row, bi], step_b)
                value = close + along_rows(far, step_r * s_count)
                if row == 0:
                    value = value * top_in
                if row == rows_a - 1:
                    value = value * bottom_in
                at = ((2 * pr + pb) * rows_a + row) * h
                parent[at : at + h] = value

    coarse_sum[...] = jnp.zeros(coarse_sum.shape, F32)
    for dr in range(3):
        for db in range(3):
            sums = {}
            for cr in range(2):
                for row in range(rows_a):
                    a, ca = divmod(row - 1, 2)
                    for cb in range(2):
                        at = ((2 * cr + cb) * rows_a + row) * h
                        cell = parent[at : at + h]
                        for da in range(3):
                            c, o = 4 * cr + 2 * ca + cb, 9 * dr + 3 * da + db
                            term = spread[c * 27 + o] * cell
                            key = a + 1 + da
                            sums[key] = sums[key] + term if key in sums else term
            for a, value in sums.items():
                coarse_sum[a * h : (a + 1) * h] += along_lanes(along_rows(value, (dr - 1) * s_count), db - 1)

    edge_sum[...] = jnp.zeros(edge_sum.shape, F32)
    for q in range(g.w):
        @pl.when(worker == q)
        def _(q=q):
            low = q < g.w // 2
            if q == 0 or q == g.w - 1:
                for x in range(4):
                    at = (x * rows_a + (0 if low else rows_a - 1)) * h
                    edge_sum[x * h : (x + 1) * h] = parent[at : at + h]
            for t in range(2):
                a = (t - 2 if low else g.la + t) - q * ra + 2
                if 0 <= a < ra + 4:
                    edge_sum[(4 + t) * h : (5 + t) * h] = coarse_sum[a * h : (a + 1) * h]


def gather_kernel(g, cells, seen, parent, coarse_sum, edge_ref, *rest):
    out_refs, (joined, stage) = rest[: g.n], rest[g.n :]
    me, ang = lax.axis_index("rad"), lax.axis_index("ang")
    n, b, s_count, ra, h = g.n, g.b, g.s, g.ra, g.h
    rows_a = 2 * ra + 2
    parts = [thirds(cells[phase]) for phase in range(2)]
    order = [place_columns(b, 2, phase) for phase in range(2)]
    for half in range(2):
        lanes = slice(half * b, (half + 1) * b)
        joined[half] = exact_dot(parts[0], order[0][:, lanes]) + exact_dot(parts[1], order[1][:, lanes])
    shown = None
    for phase in range(4):
        value = exact_dot(thirds(seen[phase]), place_columns(b, 4, phase))
        shown = value if shown is None else shown + value
    live = jnp.where(jnp.minimum(me, g.w - 1) < g.w // 2, ang < g.m - 1, ang > 0)
    end_excite, end_resid, end_mid, end_coarse, _ = backward_rows(g)
    per = 4 * g.stars * ra
    for r in range(n):
        for s in range(s_count):
            sub = r * s_count + s
            for half in range(2):
                for a in range(2 * ra):
                    at = ((half * 2 * ra + a) * s_count + s) * 16
                    stage[r, at : at + 16] = joined[half, pl.ds(a * 16 * h + sub, 16, stride=h), :]
            for part in range(4):
                at = end_excite + (part * s_count + s) * per
                stage[r, at : at + per] = shown[s * per : (s + 1) * per, part * b : (part + 1) * b]
            at = end_resid + s * 4 * rows_a
            stage[r, at : at + 4 * rows_a] = parent[pl.ds(sub, 4 * rows_a, stride=h), :]
            at = end_mid + (ra + 4) * s
            stage[r, at : at + ra + 4] = coarse_sum[pl.ds(sub, ra + 4, stride=h), :]
            at = end_coarse + 6 * s
            stage[r, at : at + 6] = jnp.where(live, edge_ref[pl.ds(sub, 6, stride=h), :], 0.0)
    for k in range(n):
        out_refs[k][...] = stage[lax.rem(me + k, n)]


def mixing_kernel(g, rows_mid, rows_fine, noise_mid, noise_fine, mid_out, fine_out):
    me = lax.axis_index("rad")
    entries = [(mid_out, noise_mid, rows_mid[me])]
    entries += [(fine_out.at[i], noise_fine, rows_fine[2 * me + i]) for i in range(2)]
    for out, table, entry in entries:
        lane = lax.broadcasted_iota(jnp.int32, table.shape[1:], 1)
        for c in range(8):
            column = jnp.sum(jnp.where(lane == entry, table[c], 0.0), axis=1, keepdims=True)
            out[c] = jnp.broadcast_to(column, (8, g.b))


def owner_kernel(g, mid_weights, fine_weights, *rest):
    in_refs, rest = rest[: g.n], rest[g.n :]
    coarse_out, mid_out, fine_out, resid_out, got, fine, grad_mid, grad_coarse = rest
    me = lax.axis_index("rad")
    n, b, s_count, ra, la = g.n, g.b, g.s, g.ra, g.la
    rows_a = 2 * ra + 2
    end_excite, end_resid, end_mid, end_coarse, _ = backward_rows(g)
    per = 4 * g.stars * ra
    for k in range(n):
        got[lax.rem(me + n - k, n)] = in_refs[k][...]
    grad_mid[...] = jnp.zeros(grad_mid.shape, F32)
    grad_coarse[...] = jnp.zeros(grad_coarse.shape, F32)
    for q in range(g.w):
        low = q < g.w // 2
        for s in range(s_count):
            for half in range(2):
                for a in range(2 * ra):
                    at = ((half * 2 * ra + a) * s_count + s) * 16
                    rows = pl.ds(s * 32 * la + 2 * q * ra + a, 16, stride=2 * la)
                    fine[half, rows, :] = got[q, at : at + 16]
            for part in range(4):
                for star in range(g.stars):
                    at = end_excite + (part * s_count + s) * per + star * 4 * ra
                    rows = slice(4 * q * ra, 4 * (q + 1) * ra)
                    resid_out[s, star, rows, part * b : (part + 1) * b] = got[q, at : at + 4 * ra]
            edge = got[q, end_coarse + 6 * s : end_coarse + 6 * s + 6]
            for x in range(4):
                at = end_resid + s * 4 * rows_a + x * rows_a
                grad_mid[s, x, 2 * q * ra : 2 * q * ra + rows_a] += got[q, at : at + rows_a]
                row = 2 * la if low else 1
                grad_mid[s, x, row : row + 1] += edge[x : x + 1]
            at = end_mid + (ra + 4) * s
            grad_coarse[s, q * ra : q * ra + ra + 4] += got[q, at : at + ra + 4]
            row = la if low else 2
            grad_coarse[s, row : row + 2] += edge[4:6]
    for i in range(2):
        for j in range(8):
            weight = [fine_weights[i, c, j : j + 1] for c in range(8)]
            for s in range(s_count):
                for half in range(2):
                    total = None
                    for c in range(8):
                        at = ((s * 8 + c) * 2 + i) * 2 * la
                        term = weight[c] * fine[half, at : at + 2 * la]
                        total = term if total is None else total + term
                    fine_out[s, j, i, :, half * b : (half + 1) * b] = total
    for s in range(s_count):
        coarse_out[s, 0] = grad_coarse[s, 2 : 2 + la]
        cells = []
        for c in range(8):
            cr, ca, cb = c // 4, c // 2 % 2, c % 2
            cells.append(grad_mid[s, 2 * cr + cb, pl.ds(1 + ca, la, stride=2), :])
        for j in range(8):
            total = mid_weights[0, j : j + 1] * cells[0]
            for c in range(1, 8):
                total = total + mid_weights[c, j : j + 1] * cells[c]
            mid_out[s, j, 0] = total


def star_kernel(g, bins_ref, data_ref, bins_out, data_out, gathered):
    worker = jnp.minimum(lax.axis_index("rad"), g.w - 1)
    per, b = 4 * g.ra, g.b
    for q in range(g.w):
        @pl.when(worker == q)
        def _(q=q):
            for star in range(g.stars):
                gathered[0, star * per : (star + 1) * per] = bins_ref[star, q * per : (q + 1) * per].astype(F32)
                gathered[1, star * per : (star + 1) * per] = data_ref[star, q * per : (q + 1) * per]
    bins = gathered[0].astype(BF16)
    parts = thirds(gathered[1])
    for phase in range(4):
        choice = pick_columns(b, 4, phase)
        rows = pl.ds(phase, g.stars * per, stride=4)
        bins_out[rows, :] = jnp.dot(bins, choice, preferred_element_type=F32).astype(jnp.int32)
        data_out[rows, :] = exact_dot(parts, choice)


def call(kernel, name, outs, operands, scratch, scalars=0, unmoved=0):
    smem, vmem = pl.BlockSpec(memory_space=pltpu.SMEM), pl.BlockSpec(memory_space=pltpu.VMEM)
    placed = pl.BlockSpec(memory_space=pl.ANY)
    limit = None if unmoved else VMEM_LIMIT
    return pl.pallas_call(
        kernel,
        name=name,
        out_shape=[jax.ShapeDtypeStruct(shape, kind) for shape, kind in outs],
        in_specs=[placed] * unmoved + [smem] * scalars + [vmem] * (len(operands) - scalars - unmoved),
        out_specs=[vmem] * len(outs),
        scratch_shapes=[pltpu.VMEM(shape, F32) if isinstance(shape, tuple) else shape for shape in scratch],
        compiler_params=pltpu.CompilerParams(vmem_limit_bytes=limit),
    )(*operands)


def per_device(
    g,
    coarse_field,
    excite_mid,
    excite_fine,
    kernels_mid,
    noise_mid,
    rows_mid,
    kernels_fine,
    noise_fine,
    rows_fine,
    emission,
    star_bins,
    star_data,
):
    n, m, s, la, b, stars, w, ra, h = g
    kernel = functools.partial
    rows_a = 2 * ra + 2
    there, back = forward_rows(g)[-1], backward_rows(g)[-1]
    pairs = [(i, i ^ 1) for i in range(m)]
    between = [(i, (i + 1) % m if i % 2 else (i - 1) % m) for i in range(m)]
    workers = [(r, a, 1 if min(r, w - 1) < w // 2 else -1) for r in range(n) for a in range(m)]
    sideways = [(r * m + a, r * m + (a - step) % m) for r, a, step in workers]

    def exchange(blocks):
        return [blocks[0]] + [lax.ppermute(blocks[k], "rad", [(i, (i + k) % n) for i in range(n)]) for k in range(1, n)]

    noise_mid, noise_fine = noise_mid.transpose(1, 2, 0), noise_fine.transpose(1, 2, 0)
    edge_rows = (-(-6 * s // 8) * 8, b)
    mixed, one, two = call(
        kernel(edge_kernel, g),
        "edges",
        [((s, 8, la, b), F32), (edge_rows, F32), (edge_rows, F32)],
        (rows_mid, noise_mid, coarse_field, excite_mid),
        [
            pltpu.SMEM(rows_mid.shape, jnp.int32),
            noise_mid.shape,
            coarse_field.shape,
            excite_mid.shape,
            pltpu.SemaphoreType.DMA((4,)),
        ],
        unmoved=4,
    )
    one, two = lax.ppermute(one, "ang", pairs), lax.ppermute(two, "ang", between)
    sent = call(
        kernel(scatter_kernel, g),
        "scatter",
        [((there, b), F32)] * n,
        (rows_fine, noise_fine, excite_fine, emission, coarse_field, mixed, one, two),
        [
            pltpu.SMEM(rows_fine.shape, jnp.int32),
            noise_fine.shape,
            excite_fine.shape,
            emission.shape,
            coarse_field.shape,
            pltpu.SemaphoreType.DMA((5,)),
            (32 * s * la, 2 * b),
            (2, 32 * s * la, b),
            (16 * la, 4 * b),
            (s, la + 4, b),
            (w, there, b),
        ],
        unmoved=5,
    )
    got = exchange(sent)
    bins, data = call(
        kernel(star_kernel, g),
        "stars",
        [((16 * stars * ra, b), jnp.int32), ((16 * stars * ra, b), F32)],
        (star_bins, star_data),
        [(2, 4 * stars * ra, 4 * b)],
    )
    (spread,) = call(
        kernel(weight_kernel, g),
        "weights",
        [((3 * 8 * 27, h, b), F32)],
        (rows_mid, rows_fine, kernels_mid, kernels_fine),
        [(3, 8, h, 27)],
        scalars=2,
    )
    cells, seen, parent, coarse_sum, edge = call(
        kernel(main_kernel, g),
        "main",
        [
            ((2, 32 * ra * h, b), F32),
            ((4, 4 * stars * ra * s, b), F32),
            ((4 * rows_a * h, b), F32),
            (((ra + 4) * h, b), F32),
            ((6 * h, b), F32),
        ],
        (spread, bins, data, *got),
        [
            (n, there, b),
            (64 * ra * h, b),
            (64 * ra * h, b),
            (4 * rows_a * h, b),
            ((ra + 4) * h, b),
            (3, ra + 4, 3, h, b),
            (4, rows_a, 4, h, b),
            (4, rows_a, 4, h, b),
        ],
    )
    edge = lax.ppermute(edge, ("rad", "ang"), sideways)
    done = call(
        kernel(gather_kernel, g),
        "gather",
        [((back, b), F32)] * n,
        (cells, seen, parent, coarse_sum, edge),
        [(2, 32 * ra * h, b), (n, back, b)],
    )
    got = exchange(done)
    mid_weights, fine_weights = call(
        kernel(mixing_kernel, g),
        "mixing",
        [((8, 8, b), F32), ((2, 8, 8, b), F32)],
        (rows_mid, rows_fine, noise_mid, noise_fine),
        [],
        scalars=2,
    )
    return tuple(
        call(
            kernel(owner_kernel, g),
            "owner",
            [
                ((s, 1, la, b), F32),
                ((s, 8, 1, la, b), F32),
                ((s, 8, 2, 2 * la, 2 * b), F32),
                ((s, stars, 4 * la, 4 * b), F32),
            ],
            (mid_weights, fine_weights, *got),
            [(n, back, b), (2, 32 * s * la, b), (s, 4, 2 * la + 2, b), (s, la + 4, b)],
        )
    )


def solution(mesh):
    placed = (
        P(None, "rad", "ang", None),
        P(None, None, "rad", "ang", None),
        P(None, None, "rad", "ang", None),
        P(),
        P(),
        P(),
        P(),
        P(),
        P(),
        P("rad", "ang", None),
        P(None, "ang", None),
        P(None, "ang", None),
    )

    def local(*args):
        return per_device(make_plan(mesh, args[0], args[10]), *args)

    return jax.shard_map(
        local,
        mesh=mesh,
        in_specs=placed,
        out_specs=(
            P(None, "rad", "ang", None),
            P(None, None, "rad", "ang", None),
            P(None, None, "rad", "ang", None),
            P(None, None, "ang", None),
        ),
        check_vma=False,
    )
```

```python
import functools
import typing

import jax
import jax.numpy as jnp
from jax import lax
from jax.experimental import pallas as pl
from jax.experimental.pallas import tpu as pltpu
from jax.sharding import PartitionSpec as P

F32 = jnp.float32
BF16 = jnp.bfloat16
VMEM_LIMIT = 24 * 1024 * 1024


class Plan(typing.NamedTuple):
    n: int
    m: int
    s: int
    la: int
    b: int
    stars: int
    w: int
    ra: int
    h: int


def make_plan(mesh, coarse, star_bins):
    n, m = mesh.shape["rad"], mesh.shape["ang"]
    s, rows, la, b = coarse.shape
    w = max(d for d in range(1, min(n, la) + 1) if la % d == 0)
    ra = la // w
    assert rows == 1 and m % 2 == 0 and w % 2 == 0 and (w // 2) * ra >= 2
    return Plan(n, m, s, la, b, star_bins.shape[0], w, ra, n * s)


def eights(rows):
    return -(-rows // 8) * 8


def large_there(g):
    fine = 2 * 2 * g.ra * g.s * 16
    return fine, fine + 16 * 4 * g.ra


def small_there(g):
    mix = g.s * 4 * (2 * g.ra + 2)
    return mix, eights(mix + g.s * (g.ra + 4))


def large_back(g):
    field = 2 * 2 * g.ra * g.s * 16
    return field, field + 4 * g.s * g.stars * 4 * g.ra


def small_back(g):
    mid = g.s * 4 * (2 * g.ra + 2)
    coarse = mid + g.s * (g.ra + 4)
    return mid, coarse, eights(coarse + 6 * g.s)


def prepared_rows(g):
    sizes = dict(
        mixed=8 * g.s * g.la,
        coarse=eights(g.s * g.la),
        stencil=24 * g.h,
        bins=16 * g.stars * g.ra,
        data=16 * g.stars * g.ra,
        mid=64,
        fine=128,
    )
    begins, at = {}, 0
    for part, size in sizes.items():
        begins[part] = at
        at += size
    return begins, at


def table_weights(table_ref, entry):
    lane = lax.broadcasted_iota(jnp.int32, table_ref.shape[1:], 1)
    columns = [
        jnp.sum(jnp.where(lane == entry, table_ref[c], 0.0), axis=1, keepdims=True) for c in range(table_ref.shape[0])
    ]
    return lambda c, j: columns[c][j : j + 1]


def start_all(pairs, sems, first=0):
    copies = [pltpu.make_async_copy(source, here, sems.at[first + i]) for i, (source, here) in enumerate(pairs)]
    for copy in copies:
        copy.start()
    return copies


def wait_all(copies):
    for copy in copies:
        copy.wait()


def pick_columns(length, ways, phase):
    src = lax.broadcasted_iota(jnp.int32, (length * ways, length), 0)
    dst = lax.broadcasted_iota(jnp.int32, (length * ways, length), 1)
    return jnp.where(src == ways * dst + phase, 1.0, 0.0).astype(BF16)


def place_columns(length, ways, phase):
    src = lax.broadcasted_iota(jnp.int32, (length, length * ways), 0)
    dst = lax.broadcasted_iota(jnp.int32, (length, length * ways), 1)
    return jnp.where(dst == ways * src + phase, 1.0, 0.0).astype(BF16)


def thirds(x):
    high = x.astype(BF16)
    rest = x - high.astype(F32)
    middle = rest.astype(BF16)
    return high, middle, (rest - middle.astype(F32)).astype(BF16)


def exact_dot(parts, choice):
    high, middle, low = [jnp.dot(part, choice, preferred_element_type=F32) for part in parts]
    return high + (middle + low)


def along_lanes(x, step):
    if step == 0:
        return x
    size = x.shape[1]
    lane = lax.broadcasted_iota(jnp.int32, x.shape, 1)
    edge = 0 if step > 0 else size - 1
    return jnp.where(lane == edge, 0.0, pltpu.roll(x, step % size, axis=1))


def along_rows(x, step):
    if step == 0:
        return x
    size = x.shape[0]
    row = lax.broadcasted_iota(jnp.int32, x.shape, 0)
    kept = row >= step if step > 0 else row < size + step
    return jnp.where(kept, pltpu.roll(x, step % size, axis=0), 0.0)


def prepare_kernel(g, *rest):
    sources, (one_ref, two_ref, block), rest = rest[:10], rest[11:14], rest[14:]
    held, (sems, gathered) = rest[:10], rest[10:]
    copies = start_all(list(zip(sources, held)), sems)
    rows_mid, rows_fine, noise_mid, noise_fine, mid_table, fine_table = held[:6]
    coarse_ref, excite_ref, bins_ref, data_ref = held[6:]
    begins, _ = prepared_rows(g)
    me = lax.axis_index("rad")
    even = lax.rem(lax.axis_index("ang"), 2) == 0
    worker = jnp.minimum(me, g.w - 1)
    per, b = 4 * g.ra, g.b
    choices = [pick_columns(b, 4, phase) for phase in range(4)]
    wait_all(copies)
    weight = table_weights(noise_mid, rows_mid[me])
    for c in range(8):
        for s in range(g.s):
            total = weight(c, 0) * excite_ref[s, 0, 0]
            for j in range(1, 8):
                total = total + weight(c, j) * excite_ref[s, j, 0]
            at = begins["mixed"] + (s * 8 + c) * g.la
            block[at : at + g.la] = total
    for s in range(g.s):
        up, down = coarse_ref[s, 0, g.la - 2 :], coarse_ref[s, 0, :2]
        one_ref[2 * s : 2 * s + 2] = jnp.where(even, up, down)
        two_ref[2 * s : 2 * s + 2] = jnp.where(even, down, up)
        for cr in range(2):
            for cb in range(2):
                at = 2 * g.s + 4 * s + 2 * cr + cb
                last = begins["mixed"] + (s * 8 + 4 * cr + 2 + cb) * g.la + g.la - 1
                leading = begins["mixed"] + (s * 8 + 4 * cr + cb) * g.la
                up, down = block[last : last + 1], block[leading : leading + 1]
                one_ref[at : at + 1] = jnp.where(even, up, down)
                two_ref[at : at + 1] = jnp.where(even, down, up)
        at = begins["coarse"] + s * g.la
        block[at : at + g.la] = coarse_ref[s, 0]
    for r in range(g.n):
        tables = [mid_table[rows_mid[r]], fine_table[rows_fine[2 * r]], fine_table[rows_fine[2 * r + 1]]]
        for level, table in enumerate(tables):
            for c in range(8):
                at = begins["stencil"] + (level * 8 + c) * g.h + r * g.s
                block[at : at + g.s, :27] = jnp.broadcast_to(table[c : c + 1], (g.s, 27))
    entries = [(begins["mid"], noise_mid, rows_mid[me])]
    entries += [(begins["fine"] + 64 * i, noise_fine, rows_fine[2 * me + i]) for i in range(2)]
    for at, table, entry in entries:
        lane = lax.broadcasted_iota(jnp.int32, table.shape[1:], 1)
        for c in range(8):
            column = jnp.sum(jnp.where(lane == entry, table[c], 0.0), axis=1, keepdims=True)
            block[at + 8 * c : at + 8 * c + 8] = jnp.broadcast_to(column, (8, b))
    for q in range(g.w):
        @pl.when(worker == q)
        def _(q=q):
            for star in range(g.stars):
                gathered[0, star * per : (star + 1) * per] = bins_ref[star, q * per : (q + 1) * per].astype(F32)
                gathered[1, star * per : (star + 1) * per] = data_ref[star, q * per : (q + 1) * per]
    bins = gathered[0].astype(BF16)
    parts = thirds(gathered[1])
    for phase in range(4):
        rows = pl.ds(begins["bins"] + phase, g.stars * per, stride=4)
        block[rows, :] = jnp.dot(bins, choices[phase], preferred_element_type=F32)
        rows = pl.ds(begins["data"] + phase, g.stars * per, stride=4)
        block[rows, :] = exact_dot(parts, choices[phase])


def scatter_kernel(g, rows_hbm, noise_hbm, fine_hbm, emission_hbm, *rest):
    out_refs, rest = rest[: g.n], rest[g.n :]
    rows_ref, noise_ref, fine_ref, emission_ref, sems, out_sems, raw, split, lit, stage = rest
    operands = [(emission_hbm, emission_ref), (rows_hbm, rows_ref), (noise_hbm, noise_ref), (fine_hbm, fine_ref)]
    copies = start_all(operands, sems)
    me = lax.axis_index("rad")
    b, s_count, la = g.b, g.s, g.la
    end_fine, _ = large_there(g)
    choices = [pick_columns(b, 4, phase) for phase in range(4)]
    copies[0].wait()
    parts = thirds(emission_ref[...].reshape(16 * la, 4 * b))
    for phase in range(4):
        lit[phase] = exact_dot(parts, choices[phase])
    for q in range(g.w):
        for phase in range(4):
            for f in range(4):
                at = end_fine + (phase * 4 + f) * 4 * g.ra
                rows = slice(f * 4 * la + 4 * q * g.ra, f * 4 * la + 4 * (q + 1) * g.ra)
                stage[q, at : at + 4 * g.ra] = lit[phase, rows]
    wait_all(copies[1:])
    for i in range(2):
        weight = table_weights(noise_ref, rows_ref[2 * me + i])
        for c in range(8):
            weights = [weight(c, j) for j in range(8)]
            for s in range(s_count):
                total = weights[0] * fine_ref[s, 0, i]
                for j in range(1, 8):
                    total = total + weights[j] * fine_ref[s, j, i]
                at = ((s * 8 + c) * 2 + i) * 2 * la
                raw[at : at + 2 * la] = total
    parts = thirds(raw[...])
    for phase in range(2):
        split[phase] = exact_dot(parts, pick_columns(b, 2, phase))
    for q in range(g.w):
        for phase in range(2):
            for a in range(2 * g.ra):
                for s in range(s_count):
                    at = ((phase * 2 * g.ra + a) * s_count + s) * 16
                    rows = pl.ds(s * 32 * la + 2 * q * g.ra + a, 16, stride=2 * la)
                    stage[q, at : at + 16] = split[phase, rows, :]
    workers = [jnp.minimum(lax.rem(me + k, g.n), g.w - 1) for k in range(g.n)]
    wait_all(start_all([(stage.at[worker], out) for worker, out in zip(workers, out_refs)], out_sems))


def halo_kernel(g, block, one_ref, two_ref, *rest):
    out_refs, (wide, stage) = rest[: g.n], rest[g.n :]
    begins, _ = prepared_rows(g)
    me, ang = lax.axis_index("rad"), lax.axis_index("ang")
    even = lax.rem(ang, 2) == 0
    before = jnp.where(ang > 0, jnp.where(even, two_ref[...], one_ref[...]), 0.0)
    after = jnp.where(ang < g.m - 1, jnp.where(even, one_ref[...], two_ref[...]), 0.0)
    for s in range(g.s):
        wide[s, :2] = before[2 * s : 2 * s + 2]
        at = begins["coarse"] + s * g.la
        wide[s, 2 : 2 + g.la] = block[at : at + g.la]
        wide[s, 2 + g.la :] = after[2 * s : 2 * s + 2]
    end_mix, _ = small_there(g)
    for q in range(g.w):
        for s in range(g.s):
            for row in range(2 * g.ra + 2):
                a, ca = divmod(2 * q * g.ra - 1 + row, 2)
                for cr in range(2):
                    for cb in range(2):
                        at = ((s * (2 * g.ra + 2) + row) * 2 + cr) * 2 + cb
                        edge = 2 * g.s + 4 * s + 2 * cr + cb
                        if a < 0:
                            value = before[edge : edge + 1]
                        elif a >= g.la:
                            value = after[edge : edge + 1]
                        else:
                            own = begins["mixed"] + (s * 8 + 4 * cr + 2 * ca + cb) * g.la + a
                            value = block[own : own + 1]
                        stage[q, at : at + 1] = value
            at = end_mix + (g.ra + 4) * s
            stage[q, at : at + g.ra + 4] = wide[s, q * g.ra : q * g.ra + g.ra + 4]
    for k in range(g.n):
        out_refs[k][...] = stage[jnp.minimum(lax.rem(me + k, g.n), g.w - 1)]


def weight_kernel(g, block, spread):
    begins, _ = prepared_rows(g)
    for x in range(24):
        at = begins["stencil"] + x * g.h
        tile = block[at : at + g.h]
        for o in range(27):
            spread[x * 27 + o] = jnp.broadcast_to(tile[:, o : o + 1], (g.h, g.b))


def main_kernel(g, block, spread, *rest):
    n, b, s_count, ra, h = g.n, g.b, g.s, g.ra, g.h
    large_refs, small_refs, out_refs, rest = rest[:n], rest[n : 2 * n], rest[2 * n : 3 * n], rest[3 * n :]
    parent, coarse_sum, edge_sum = rest[:3]
    got, near, fine_in, emit_in, mix_in, coarse_in, coarse_ext, mid_ext, tall, cells, seen, joined, stage = rest[3:]
    me, ang = lax.axis_index("rad"), lax.axis_index("ang")
    rows_a = 2 * ra + 2
    spacing = 1.0 / (4 * n)
    worker = jnp.minimum(me, g.w - 1)
    begins, _ = prepared_rows(g)

    def weight_at(level, c, o):
        return spread[(level * 8 + c) * 27 + o]

    for k in range(n):
        source = lax.rem(me + n - k, n)
        got[source] = large_refs[k][...]
        near[source] = small_refs[k][...]
    end_fine, end_emit = large_there(g)
    end_mix, _ = small_there(g)
    for r in range(n):
        for s in range(s_count):
            sub = r * s_count + s
            at = s * 4 * rows_a
            mix_in[pl.ds(sub, 4 * rows_a, stride=h), :] = near[r, at : at + 4 * rows_a]
            at = end_mix + (ra + 4) * s
            coarse_in[pl.ds(sub, ra + 4, stride=h), :] = near[r, at : at + ra + 4]

    first = ang * g.la + worker * ra
    top_in = jnp.where(first > 0, 1.0, 0.0).astype(F32)
    bottom_in = jnp.where(first + ra < g.m * g.la, 1.0, 0.0).astype(F32)
    for a in range(ra + 4):
        x = coarse_in[a * h : (a + 1) * h]
        for db in range(3):
            shifted = along_lanes(x, 1 - db)
            for dr in range(3):
                coarse_ext[dr, a, db] = along_rows(shifted, (1 - dr) * s_count)
    for c in range(8):
        cr, ca, cb = c // 4, c // 2 % 2, c % 2
        weight = [weight_at(0, c, o) for o in range(27)]
        for row in range(1 - ca, rows_a, 2):
            a = (row - 1) // 2
            at = (row * 4 + 2 * cr + cb) * h
            total = mix_in[at : at + h]
            for dr in range(3):
                for da in range(3):
                    for db in range(3):
                        total = total + weight[9 * dr + 3 * da + db] * coarse_ext[dr, a + 1 + da, db]
            if row == 0:
                total = total * top_in
            if row == rows_a - 1:
                total = total * bottom_in
            for bi, step_b in ((1 + cb, 0), (3, -1) if cb == 0 else (0, 1)):
                shifted = along_lanes(total, step_b)
                for ri, step_r in ((1 + cr, 0), (3, -1) if cr == 0 else (0, 1)):
                    mid_ext[ri, row, bi] = along_rows(shifted, step_r * s_count)

    for r in range(n):
        for s in range(s_count):
            sub = r * s_count + s
            for x in range(4 * ra):
                at = (x * s_count + s) * 16
                fine_in[pl.ds(x * 16 * h + sub, 16, stride=h), :] = got[r, at : at + 16]
            emit_in[pl.ds(sub, 64 * ra, stride=h), :] = got[r, end_fine:end_emit]

    def cell_rows(a, c, pr):
        return pl.ds(pl.multiple_of(((a * 8 + c) * 2 + pr) * h, 8), h)

    def fine_cells(c, carry):
        for pr in range(2):
            weight = [weight_at(1 + pr, c, o) for o in range(27)]
            for a in range(2 * ra):
                for pb in range(2):
                    at = (((pb * 2 * ra + a) * 8 + c) * 2 + pr) * h
                    total = fine_in[pl.ds(pl.multiple_of(at, 8), h), :]
                    for dr in range(3):
                        for da in range(3):
                            for db in range(3):
                                o = 9 * dr + 3 * da + db
                                total = total + weight[o] * mid_ext[pr + dr, a + da, pb + db]
                    cells[pb, cell_rows(a, c, pr), :] = total
        return carry

    lax.fori_loop(0, 8, fine_cells, 0)

    radial = (4 * (lax.broadcasted_iota(jnp.int32, (h, b), 0) // s_count)).astype(F32)

    def sum_before(x):
        step = s_count
        while step < h:
            x = x + along_rows(x, step)
            step *= 2
        return along_rows(x, s_count)

    def sum_all(x):
        step = s_count
        while step < h:
            x = x + pltpu.roll(x, step, axis=0)
            step *= 2
        return x

    def position(at, carry):
        a, pb = at // 4, lax.rem(at, 4)
        half = pb // 2
        rows = [cell_rows(a // 2, 4 * (f % 2) + 2 * lax.rem(a, 2) + lax.rem(pb, 2), f // 2) for f in range(4)]
        density = [jnp.exp(cells[half, rows[f], :]) for f in range(4)]
        layer = [spacing * d for d in density]
        depth = sum_before(layer[0] + layer[1] + layer[2] + layer[3])
        glow = []
        for f in range(4):
            where_emit = pl.multiple_of(((pb * 4 + f) * 4 * ra + a) * h, 8)
            glow.append(spacing * emit_in[pl.ds(where_emit, h), :] * jnp.exp(-depth))
            depth = depth + layer[f]
        running = sum_before(glow[0] + glow[1] + glow[2] + glow[3])
        column = []
        for f in range(4):
            running = running + glow[f]
            column.append(running)
        total = [jnp.zeros((h, b), F32) for f in range(4)]
        for star in range(g.stars):
            row = (star * 4 * ra + a) * 4 + pb
            bins = jnp.broadcast_to(block[pl.ds(begins["bins"] + row, 1), :], (h, b)) - radial
            data = jnp.broadcast_to(block[pl.ds(begins["data"] + row, 1), :], (h, b))
            mine = jnp.where(bins == 0, column[0], 0.0)
            for f in range(1, 4):
                mine = jnp.where(bins == f, column[f], mine)
            predicted = sum_all(mine)
            residual = data - predicted
            for s in range(s_count):
                seen[pb, pl.ds((s * g.stars + star) * 4 * ra + a, 1), :] = residual[s : s + 1]
            for f in range(4):
                total[f] = total[f] + jnp.where(bins > f, residual * (predicted - column[f]), 0.0)
        for f in range(4):
            cells[half, rows[f], :] = -density[f] * total[f]
        return carry

    lax.fori_loop(0, 16 * ra, position, 0)

    parts = [thirds(cells[phase]) for phase in range(2)]
    order = [place_columns(b, 2, phase) for phase in range(2)]
    for half in range(2):
        lanes = slice(half * b, (half + 1) * b)
        joined[half] = exact_dot(parts[0], order[0][:, lanes]) + exact_dot(parts[1], order[1][:, lanes])
    shown = None
    for phase in range(4):
        value = exact_dot(thirds(seen[phase]), place_columns(b, 4, phase))
        shown = value if shown is None else shown + value
    end_field, _ = large_back(g)
    per = 4 * g.stars * ra
    for r in range(n):
        for s in range(s_count):
            sub = r * s_count + s
            for half in range(2):
                for a in range(2 * ra):
                    at = ((half * 2 * ra + a) * s_count + s) * 16
                    stage[r, at : at + 16] = joined[half, pl.ds(a * 16 * h + sub, 16, stride=h), :]
            for part in range(4):
                at = end_field + (part * s_count + s) * per
                stage[r, at : at + per] = shown[s * per : (s + 1) * per, part * b : (part + 1) * b]
    for k in range(n):
        out_refs[k][...] = stage[lax.rem(me + k, n)]

    tall[...] = jnp.zeros(tall.shape, F32)
    for pr in range(2):
        def gather(c, carry, pr=pr):
            values = {(a, pb): cells[pb, cell_rows(a, c, pr), :] for a in range(2 * ra) for pb in range(2)}
            for dr in range(3):
                sums = {}
                for da in range(3):
                    for db in range(3):
                        weight = weight_at(1 + pr, c, 9 * dr + 3 * da + db)
                        for (a, pb), value in values.items():
                            key = (a + da, pb + db)
                            term = weight * value
                            sums[key] = sums[key] + term if key in sums else term
                for (row, bi), value in sums.items():
                    tall[pr + dr, row, bi] += value
            return carry

        lax.fori_loop(0, 8, gather, 0)
    for row in range(rows_a):
        for pr in range(2):
            for pb in range(2):
                bi, step_b = (3, 1) if pb == 0 else (0, -1)
                ri, step_r = (3, 1) if pr == 0 else (0, -1)
                close = tall[1 + pr, row, 1 + pb] + along_lanes(tall[1 + pr, row, bi], step_b)
                far = tall[ri, row, 1 + pb] + along_lanes(tall[ri, row, bi], step_b)
                value = close + along_rows(far, step_r * s_count)
                if row == 0:
                    value = value * top_in
                if row == rows_a - 1:
                    value = value * bottom_in
                at = ((2 * pr + pb) * rows_a + row) * h
                parent[at : at + h] = value

    coarse_sum[...] = jnp.zeros(coarse_sum.shape, F32)
    for dr in range(3):
        for db in range(3):
            sums = {}
            for c in range(8):
                cr, ca, cb = c // 4, c // 2 % 2, c % 2
                for da in range(3):
                    weight = weight_at(0, c, 9 * dr + 3 * da + db)
                    for row in range(1 - ca, rows_a, 2):
                        at = ((2 * cr + cb) * rows_a + row) * h
                        term = weight * parent[at : at + h]
                        key = (row - 1) // 2 + 1 + da
                        sums[key] = sums[key] + term if key in sums else term
            for a, value in sums.items():
                coarse_sum[a * h : (a + 1) * h] += along_lanes(along_rows(value, (dr - 1) * s_count), db - 1)

    edge_sum[...] = jnp.zeros(edge_sum.shape, F32)
    for q in range(g.w):
        @pl.when(worker == q)
        def _(q=q):
            low = q < g.w // 2
            if q == 0 or q == g.w - 1:
                for x in range(4):
                    at = (x * rows_a + (0 if low else rows_a - 1)) * h
                    edge_sum[x * h : (x + 1) * h] = parent[at : at + h]
            for t in range(2):
                a = (t - 2 if low else g.la + t) - q * ra + 2
                if 0 <= a < ra + 4:
                    edge_sum[(4 + t) * h : (5 + t) * h] = coarse_sum[a * h : (a + 1) * h]


def sums_kernel(g, parent, coarse_sum, edge_ref, *rest):
    out_refs, (stage,) = rest[: g.n], rest[g.n :]
    me, ang = lax.axis_index("rad"), lax.axis_index("ang")
    n, s_count, ra, h = g.n, g.s, g.ra, g.h
    rows_a = 2 * ra + 2
    live = jnp.where(jnp.minimum(me, g.w - 1) < g.w // 2, ang < g.m - 1, ang > 0)
    end_mid, end_coarse, _ = small_back(g)
    for r in range(n):
        for s in range(s_count):
            sub = r * s_count + s
            at = s * 4 * rows_a
            stage[r, at : at + 4 * rows_a] = parent[pl.ds(sub, 4 * rows_a, stride=h), :]
            at = end_mid + (ra + 4) * s
            stage[r, at : at + ra + 4] = coarse_sum[pl.ds(sub, ra + 4, stride=h), :]
            at = end_coarse + 6 * s
            stage[r, at : at + 6] = jnp.where(live, edge_ref[pl.ds(sub, 6, stride=h), :], 0.0)
    for k in range(n):
        out_refs[k][...] = stage[lax.rem(me + k, n)]


def owner_kernel(g, block, *rest):
    large_refs, small_refs, rest = rest[: g.n], rest[g.n : 2 * g.n], rest[2 * g.n :]
    coarse_out, mid_out, fine_out, resid_out, got, near, fine, grad_mid, grad_coarse = rest
    me = lax.axis_index("rad")
    n, b, s_count, ra, la = g.n, g.b, g.s, g.ra, g.la
    rows_a = 2 * ra + 2
    begins, _ = prepared_rows(g)
    end_field, _ = large_back(g)
    end_mid, end_coarse, _ = small_back(g)
    per = 4 * g.stars * ra
    for k in range(n):
        source = lax.rem(me + n - k, n)
        got[source] = large_refs[k][...]
        near[source] = small_refs[k][...]
    grad_mid[...] = jnp.zeros(grad_mid.shape, F32)
    grad_coarse[...] = jnp.zeros(grad_coarse.shape, F32)
    for q in range(g.w):
        low = q < g.w // 2
        for s in range(s_count):
            for half in range(2):
                for a in range(2 * ra):
                    at = ((half * 2 * ra + a) * s_count + s) * 16
                    rows = pl.ds(s * 32 * la + 2 * q * ra + a, 16, stride=2 * la)
                    fine[half, rows, :] = got[q, at : at + 16]
            for part in range(4):
                for star in range(g.stars):
                    at = end_field + (part * s_count + s) * per + star * 4 * ra
                    rows = slice(4 * q * ra, 4 * (q + 1) * ra)
                    resid_out[s, star, rows, part * b : (part + 1) * b] = got[q, at : at + 4 * ra]
            edge = near[q, end_coarse + 6 * s : end_coarse + 6 * s + 6]
            for x in range(4):
                at = s * 4 * rows_a + x * rows_a
                grad_mid[s, x, 2 * q * ra : 2 * q * ra + rows_a] += near[q, at : at + rows_a]
                row = 2 * la if low else 1
                grad_mid[s, x, row : row + 1] += edge[x : x + 1]
            at = end_mid + (ra + 4) * s
            grad_coarse[s, q * ra : q * ra + ra + 4] += near[q, at : at + ra + 4]
            row = la if low else 2
            grad_coarse[s, row : row + 2] += edge[4:6]
    for i in range(2):
        for j in range(8):
            rows = [begins["fine"] + 64 * i + 8 * c + j for c in range(8)]
            weight = [block[row : row + 1] for row in rows]
            for s in range(s_count):
                for half in range(2):
                    total = None
                    for c in range(8):
                        at = ((s * 8 + c) * 2 + i) * 2 * la
                        term = weight[c] * fine[half, at : at + 2 * la]
                        total = term if total is None else total + term
                    fine_out[s, j, i, :, half * b : (half + 1) * b] = total
    for s in range(s_count):
        coarse_out[s, 0] = grad_coarse[s, 2 : 2 + la]
        cells = []
        for c in range(8):
            cr, ca, cb = c // 4, c // 2 % 2, c % 2
            cells.append(grad_mid[s, 2 * cr + cb, pl.ds(1 + ca, la, stride=2), :])
        for j in range(8):
            row = begins["mid"] + j
            total = block[row : row + 1] * cells[0]
            for c in range(1, 8):
                total = total + block[row + 8 * c : row + 8 * c + 1] * cells[c]
            mid_out[s, j, 0] = total


def call(kernel, name, outs, operands, scratch, unmoved=0, written=0):
    vmem = pl.BlockSpec(memory_space=pltpu.VMEM)
    placed = pl.BlockSpec(memory_space=pl.ANY)
    limit = None if unmoved else VMEM_LIMIT
    return pl.pallas_call(
        kernel,
        name=name,
        out_shape=[jax.ShapeDtypeStruct(shape, kind) for shape, kind in outs],
        in_specs=[placed] * unmoved + [vmem] * (len(operands) - unmoved),
        out_specs=[placed] * written + [vmem] * (len(outs) - written),
        scratch_shapes=[pltpu.VMEM(shape, F32) if isinstance(shape, tuple) else shape for shape in scratch],
        compiler_params=pltpu.CompilerParams(vmem_limit_bytes=limit),
    )(*operands)


def per_device(
    g,
    coarse_field,
    excite_mid,
    excite_fine,
    kernels_mid,
    noise_mid,
    rows_mid,
    kernels_fine,
    noise_fine,
    rows_fine,
    emission,
    star_bins,
    star_data,
):
    n, m, s, la, b, stars, w, ra, h = g
    kernel = functools.partial
    rows_a = 2 * ra + 2
    pairs = [(i, i ^ 1) for i in range(m)]
    between = [(i, (i + 1) % m if i % 2 else (i - 1) % m) for i in range(m)]
    workers = [(r, a, 1 if min(r, w - 1) < w // 2 else -1) for r in range(n) for a in range(m)]
    sideways = [(r * m + a, r * m + (a - step) % m) for r, a, step in workers]

    def exchange(blocks):
        return [blocks[0]] + [lax.ppermute(blocks[k], "rad", [(i, (i + k) % n) for i in range(n)]) for k in range(1, n)]

    noise_mid, noise_fine = noise_mid.transpose(1, 2, 0), noise_fine.transpose(1, 2, 0)
    edge_rows = (eights(6 * s), b)
    large, small = (large_there(g)[-1], b), (small_there(g)[-1], b)
    sent = call(
        kernel(scatter_kernel, g),
        "scatter",
        [(large, F32)] * n,
        (rows_fine, noise_fine, excite_fine, emission),
        [
            pltpu.SMEM(rows_fine.shape, jnp.int32),
            noise_fine.shape,
            excite_fine.shape,
            emission.shape,
            pltpu.SemaphoreType.DMA((4,)),
            pltpu.SemaphoreType.DMA((n,)),
            (32 * s * la, 2 * b),
            (2, 32 * s * la, b),
            (4, 16 * la, b),
            (w, *large),
        ],
        unmoved=4,
        written=n,
    )
    got = exchange(sent)
    operands = (rows_mid, rows_fine, noise_mid, noise_fine, kernels_mid, kernels_fine)
    operands += (coarse_field, excite_mid, star_bins, star_data)
    one, two, block = call(
        kernel(prepare_kernel, g),
        "prepare",
        [(edge_rows, F32), (edge_rows, F32), ((prepared_rows(g)[1], b), F32)],
        (*operands, sent[0]),
        [
            *[(pltpu.SMEM if len(x.shape) == 1 else pltpu.VMEM)(x.shape, x.dtype) for x in operands],
            pltpu.SemaphoreType.DMA((10,)),
            (2, 4 * stars * ra, 4 * b),
        ],
        unmoved=11,
    )
    one, two = lax.ppermute(one, "ang", pairs), lax.ppermute(two, "ang", between)
    got += exchange(
        call(
            kernel(halo_kernel, g),
            "halos",
            [(small, F32)] * n,
            (block, one, two),
            [(s, la + 4, b), (w, *small)],
        )
    )
    (spread,) = call(kernel(weight_kernel, g), "weights", [((24 * 27, h, b), F32)], (block,), [])
    large_out = (large_back(g)[-1], b)
    *done, parent, coarse_sum, edge = call(
        kernel(main_kernel, g),
        "main",
        [(large_out, F32)] * n + [((4 * rows_a * h, b), F32), (((ra + 4) * h, b), F32), ((6 * h, b), F32)],
        (block, spread, *got),
        [
            (n, *large),
            (n, *small),
            (64 * ra * h, b),
            (64 * ra * h, b),
            (4 * rows_a * h, b),
            ((ra + 4) * h, b),
            (3, ra + 4, 3, h, b),
            (4, rows_a, 4, h, b),
            (4, rows_a, 4, h, b),
            (2, 32 * ra * h, b),
            (4, 4 * stars * ra * s, b),
            (2, 32 * ra * h, b),
            (n, *large_out),
        ],
    )
    large, small = (large_back(g)[-1], b), (small_back(g)[-1], b)
    got = exchange(done)
    edge = lax.ppermute(edge, ("rad", "ang"), sideways)
    got += exchange(
        call(
            kernel(sums_kernel, g),
            "sums",
            [(small, F32)] * n,
            (parent, coarse_sum, edge),
            [(n, *small)],
        )
    )
    return tuple(
        call(
            kernel(owner_kernel, g),
            "owner",
            [
                ((s, 1, la, b), F32),
                ((s, 8, 1, la, b), F32),
                ((s, 8, 2, 2 * la, 2 * b), F32),
                ((s, stars, 4 * la, 4 * b), F32),
            ],
            (block, *got),
            [(n, *large), (n, *small), (2, 32 * s * la, b), (s, 4, 2 * la + 2, b), (s, la + 4, b)],
        )
    )


def solution(mesh):
    placed = (
        P(None, "rad", "ang", None),
        P(None, None, "rad", "ang", None),
        P(None, None, "rad", "ang", None),
        P(),
        P(),
        P(),
        P(),
        P(),
        P(),
        P("rad", "ang", None),
        P(None, "ang", None),
        P(None, "ang", None),
    )

    def local(*args):
        return per_device(make_plan(mesh, args[0], args[10]), *args)

    return jax.shard_map(
        local,
        mesh=mesh,
        in_specs=placed,
        out_specs=(
            P(None, "rad", "ang", None),
            P(None, None, "rad", "ang", None),
            P(None, None, "rad", "ang", None),
            P(None, None, "ang", None),
        ),
        check_vma=False,
    )
```

```python
import functools
import typing

import jax
import jax.numpy as jnp
from jax import lax
from jax.experimental import pallas as pl
from jax.experimental.pallas import tpu as pltpu
from jax.sharding import PartitionSpec as P

F32 = jnp.float32
BF16 = jnp.bfloat16
VMEM_LIMIT = 24 * 1024 * 1024


class Plan(typing.NamedTuple):
    n: int
    m: int
    s: int
    la: int
    b: int
    stars: int
    w: int
    ra: int
    h: int


def make_plan(mesh, coarse, star_bins):
    n, m = mesh.shape["rad"], mesh.shape["ang"]
    s, rows, la, b = coarse.shape
    w = max(d for d in range(1, min(n, la) + 1) if la % d == 0)
    ra = la // w
    assert rows == 1 and n & (n - 1) == 0 and w % 2 == 0 and (w // 2) * ra >= 2
    return Plan(n, m, s, la, b, star_bins.shape[0], w, ra, n * s)


def eights(rows):
    return -(-rows // 8) * 8


def large_there(g):
    fine = 2 * 2 * g.ra * g.s * 16
    emit = fine + 16 * 4 * g.ra
    mix = emit + g.s * 4 * (2 * g.ra + 2)
    coarse = mix + g.s * (g.ra + 4)
    return fine, emit, mix, coarse, eights(coarse + 6 * g.s)


def large_back(g):
    return 2 * 2 * g.ra * g.s * 16, 4 * g.s * 4 * g.stars * g.ra


def small_back(g):
    mid = g.s * 4 * (2 * g.ra + 2)
    coarse = mid + g.s * (g.ra + 4)
    return mid, coarse, eights(coarse + 6 * g.s)


def prepared_rows(g):
    sizes = dict(
        stencil=24 * g.h,
        bins=16 * g.stars * g.ra,
        data=16 * g.stars * g.ra,
        mid=64,
        fine=128,
    )
    begins, at = {}, 0
    for part, size in sizes.items():
        begins[part] = at
        at += size
    return begins, at


def table_weights(table_ref, entry):
    lane = lax.broadcasted_iota(jnp.int32, table_ref.shape[1:], 1)
    columns = [
        jnp.sum(jnp.where(lane == entry, table_ref[c], 0.0), axis=1, keepdims=True) for c in range(table_ref.shape[0])
    ]
    return lambda c, j: columns[c][j : j + 1]


def start_all(pairs, sems, first=0):
    copies = [pltpu.make_async_copy(source, here, sems.at[first + i]) for i, (source, here) in enumerate(pairs)]
    for copy in copies:
        copy.start()
    return copies


def wait_all(copies):
    for copy in copies:
        copy.wait()


def pick_columns(length, ways, phase):
    src = lax.broadcasted_iota(jnp.int32, (length * ways, length), 0)
    dst = lax.broadcasted_iota(jnp.int32, (length * ways, length), 1)
    return jnp.where(src == ways * dst + phase, 1.0, 0.0).astype(BF16)


def place_columns(length, ways, phase):
    src = lax.broadcasted_iota(jnp.int32, (length, length * ways), 0)
    dst = lax.broadcasted_iota(jnp.int32, (length, length * ways), 1)
    return jnp.where(dst == ways * src + phase, 1.0, 0.0).astype(BF16)


def thirds(x):
    high = x.astype(BF16)
    rest = x - high.astype(F32)
    middle = rest.astype(BF16)
    return high, middle, (rest - middle.astype(F32)).astype(BF16)


def exact_dot(parts, choice):
    high, middle, low = [jnp.dot(part, choice, preferred_element_type=F32) for part in parts]
    return high + (middle + low)


def along_lanes(x, step):
    if step == 0:
        return x
    size = x.shape[1]
    lane = lax.broadcasted_iota(jnp.int32, x.shape, 1)
    edge = 0 if step > 0 else size - 1
    return jnp.where(lane == edge, 0.0, pltpu.roll(x, step % size, axis=1))


def along_rows(x, step):
    if step == 0:
        return x
    size = x.shape[0]
    row = lax.broadcasted_iota(jnp.int32, x.shape, 0)
    kept = row >= step if step > 0 else row < size + step
    return jnp.where(kept, pltpu.roll(x, step % size, axis=0), 0.0)


def prepare_kernel(g, *rest):
    sources, block, rest = rest[:8], rest[9], rest[10:]
    held, (sems, gathered) = rest[:8], rest[8:]
    copies = start_all(list(zip(sources, held)), sems)
    rows_mid, rows_fine, noise_mid, noise_fine, mid_table, fine_table, bins_ref, data_ref = held
    begins, _ = prepared_rows(g)
    me = lax.axis_index("rad")
    worker = jnp.minimum(me, g.w - 1)
    per, b = 4 * g.ra, g.b
    choices = [pick_columns(b, 4, phase) for phase in range(4)]
    wait_all(copies)
    for r in range(g.n):
        tables = [mid_table[rows_mid[r]], fine_table[rows_fine[2 * r]], fine_table[rows_fine[2 * r + 1]]]
        for level, table in enumerate(tables):
            for c in range(8):
                at = begins["stencil"] + (level * 8 + c) * g.h + r * g.s
                block[at : at + g.s, :27] = jnp.broadcast_to(table[c : c + 1], (g.s, 27))
    entries = [(begins["mid"], noise_mid, rows_mid[me])]
    entries += [(begins["fine"] + 64 * i, noise_fine, rows_fine[2 * me + i]) for i in range(2)]
    for at, table, entry in entries:
        lane = lax.broadcasted_iota(jnp.int32, table.shape[1:], 1)
        for c in range(8):
            column = jnp.sum(jnp.where(lane == entry, table[c], 0.0), axis=1, keepdims=True)
            block[at + 8 * c : at + 8 * c + 8] = jnp.broadcast_to(column, (8, b))
    for q in range(g.w):
        @pl.when(worker == q)
        def _(q=q):
            for star in range(g.stars):
                gathered[0, star * per : (star + 1) * per] = bins_ref[star, q * per : (q + 1) * per].astype(F32)
                gathered[1, star * per : (star + 1) * per] = data_ref[star, q * per : (q + 1) * per]
    bins = gathered[0].astype(BF16)
    parts = thirds(gathered[1])
    for phase in range(4):
        rows = pl.ds(begins["bins"] + phase, g.stars * per, stride=4)
        block[rows, :] = jnp.dot(bins, choices[phase], preferred_element_type=F32)
        rows = pl.ds(begins["data"] + phase, g.stars * per, stride=4)
        block[rows, :] = exact_dot(parts, choices[phase])


def scatter_kernel(g, *rest):
    sources, out_refs, rest = rest[:8], rest[8 : 8 + g.n], rest[8 + g.n :]
    held, (sems, out_sems, raw, split, lit, stage, mixed, wide) = rest[:8], rest[8:]
    copies = start_all(list(zip(sources, held)), sems)
    emission_ref, rows_mid, noise_mid, coarse_ref, excite_ref, rows_ref, noise_ref, fine_ref = held
    me = lax.axis_index("rad")
    b, s_count, la = g.b, g.s, g.la
    end_fine, end_emit, end_mix, end_coarse, _ = large_there(g)
    choices = [pick_columns(b, 4, phase) for phase in range(4)]
    copies[0].wait()
    parts = thirds(emission_ref[...].reshape(16 * la, 4 * b))
    for phase in range(4):
        lit[phase] = exact_dot(parts, choices[phase])
    for q in range(g.w):
        for phase in range(4):
            for f in range(4):
                at = end_fine + (phase * 4 + f) * 4 * g.ra
                rows = slice(f * 4 * la + 4 * q * g.ra, f * 4 * la + 4 * (q + 1) * g.ra)
                stage[q, at : at + 4 * g.ra] = lit[phase, rows]
    wait_all(copies[1:5])
    weight = table_weights(noise_mid, rows_mid[me])
    for c in range(8):
        for s in range(s_count):
            total = weight(c, 0) * excite_ref[s, 0, 0]
            for j in range(1, 8):
                total = total + weight(c, j) * excite_ref[s, j, 0]
            mixed[s, c] = total
    wide[...] = jnp.zeros(wide.shape, F32)
    for s in range(s_count):
        wide[s, 2 : 2 + la] = coarse_ref[s, 0]
    for q in range(g.w):
        low = q < g.w // 2
        for s in range(s_count):
            for row in range(2 * g.ra + 2):
                a, ca = divmod(2 * q * g.ra - 1 + row, 2)
                for cr in range(2):
                    for cb in range(2):
                        at = end_emit + ((s * (2 * g.ra + 2) + row) * 2 + cr) * 2 + cb
                        if 0 <= a < la:
                            stage[q, at : at + 1] = mixed[s, 4 * cr + 2 * ca + cb, a : a + 1]
                        else:
                            stage[q, at : at + 1] = jnp.zeros((1, b), F32)
            at = end_mix + (g.ra + 4) * s
            stage[q, at : at + g.ra + 4] = wide[s, q * g.ra : q * g.ra + g.ra + 4]
            at = end_coarse + 6 * s
            row = la - 1 if low else 0
            for cr in range(2):
                for cb in range(2):
                    c = 4 * cr + (2 if low else 0) + cb
                    stage[q, at + 2 * cr + cb : at + 2 * cr + cb + 1] = mixed[s, c, row : row + 1]
            row = la - 2 if low else 0
            stage[q, at + 4 : at + 6] = coarse_ref[s, 0, row : row + 2]
    wait_all(copies[5:])
    for i in range(2):
        weight = table_weights(noise_ref, rows_ref[2 * me + i])
        for c in range(8):
            weights = [weight(c, j) for j in range(8)]
            for s in range(s_count):
                total = weights[0] * fine_ref[s, 0, i]
                for j in range(1, 8):
                    total = total + weights[j] * fine_ref[s, j, i]
                at = ((s * 8 + c) * 2 + i) * 2 * la
                raw[at : at + 2 * la] = total
    parts = thirds(raw[...])
    for phase in range(2):
        split[phase] = exact_dot(parts, pick_columns(b, 2, phase))
    for q in range(g.w):
        for phase in range(2):
            for a in range(2 * g.ra):
                for s in range(s_count):
                    at = ((phase * 2 * g.ra + a) * s_count + s) * 16
                    rows = pl.ds(s * 32 * la + 2 * q * g.ra + a, 16, stride=2 * la)
                    stage[q, at : at + 16] = split[phase, rows, :]
    workers = [jnp.minimum(lax.rem(me + k, g.n), g.w - 1) for k in range(g.n)]
    wait_all(start_all([(stage.at[worker], out) for worker, out in zip(workers, out_refs)], out_sems))


def relay_kernel(g, *rest):
    in_refs, (edge_out,) = rest[: g.n], rest[g.n :]
    me = lax.axis_index("rad")
    _, _, _, end_coarse, _ = large_there(g)
    for k in range(g.n):
        source = lax.rem(me + g.n - k, g.n)
        for s in range(g.s):
            rows = pl.ds(source * g.s + s, 6, stride=g.h)
            edge_out[rows, :] = in_refs[k][end_coarse + 6 * s : end_coarse + 6 * s + 6]


def unpack_kernel(g, *rest):
    in_refs, (fine_out, emit_out, mix_out, coarse_out) = rest[: g.n], rest[g.n :]
    me = lax.axis_index("rad")
    end_fine, end_emit, end_mix, _, _ = large_there(g)
    h, ra, rows_a = g.h, g.ra, 2 * g.ra + 2
    for k in range(g.n):
        source = lax.rem(me + g.n - k, g.n)
        got = in_refs[k]
        for s in range(g.s):
            sub = source * g.s + s
            for x in range(4 * ra):
                at = (x * g.s + s) * 16
                fine_out[pl.ds(x * 16 * h + sub, 16, stride=h), :] = got[at : at + 16]
            emit_out[pl.ds(sub, 64 * ra, stride=h), :] = got[end_fine:end_emit]
            at = end_emit + s * 4 * rows_a
            mix_out[pl.ds(sub, 4 * rows_a, stride=h), :] = got[at : at + 4 * rows_a]
            at = end_mix + (ra + 4) * s
            coarse_out[pl.ds(sub, ra + 4, stride=h), :] = got[at : at + ra + 4]


def weight_kernel(g, block, own, spread, own_out, block_out):
    own_out[...] = own[...]
    block_out[...] = block[...]
    begins, _ = prepared_rows(g)
    for x in range(24):
        at = begins["stencil"] + x * g.h
        tile = block[at : at + g.h]
        for o in range(27):
            spread[x * 27 + o] = jnp.broadcast_to(tile[:, o : o + 1], (g.h, g.b))


def main_kernel(g, block, spread, *rest):
    n, b, s_count, ra, h = g.n, g.b, g.s, g.ra, g.h
    fine_in, emit_in, mixed, coarse, near = rest[:5]
    out_refs, (resid_out, parent, coarse_sum, edge_sum), rest = rest[5 : 5 + n], rest[5 + n : 9 + n], rest[9 + n :]
    mix_in, coarse_in, coarse_ext, mid_ext, tall, cells, seen, joined, stage = rest
    me, ang = lax.axis_index("rad"), lax.axis_index("ang")
    rows_a = 2 * ra + 2
    spacing = 1.0 / (4 * n)
    worker = jnp.minimum(me, g.w - 1)
    begins, _ = prepared_rows(g)

    def weight_at(level, c, o):
        return spread[(level * 8 + c) * 27 + o]

    mix_in[...] = mixed[...]
    coarse_in[...] = coarse[...]
    live = jnp.where(worker < g.w // 2, ang > 0, ang < g.m - 1)
    for q in range(g.w):
        @pl.when(jnp.logical_and(worker == q, live))
        def _(q=q):
            if q == 0:
                mix_in[: 4 * h] = near[: 4 * h]
            if q == g.w - 1:
                mix_in[4 * (rows_a - 1) * h :] = near[: 4 * h]
            for a in range(ra + 4):
                row = q * ra - 2 + a
                if row < 0 or row >= g.la:
                    at = (4 + (row + 2 if row < 0 else row - g.la)) * h
                    coarse_in[a * h : (a + 1) * h] = near[at : at + h]

    first = ang * g.la + worker * ra
    top_in = jnp.where(first > 0, 1.0, 0.0).astype(F32)
    bottom_in = jnp.where(first + ra < g.m * g.la, 1.0, 0.0).astype(F32)
    for a in range(ra + 4):
        x = coarse_in[a * h : (a + 1) * h]
        for db in range(3):
            shifted = along_lanes(x, 1 - db)
            for dr in range(3):
                coarse_ext[dr, a, db] = along_rows(shifted, (1 - dr) * s_count)
    for c in range(8):
        cr, ca, cb = c // 4, c // 2 % 2, c % 2
        weight = [weight_at(0, c, o) for o in range(27)]
        for row in range(1 - ca, rows_a, 2):
            a = (row - 1) // 2
            at = (row * 4 + 2 * cr + cb) * h
            total = mix_in[at : at + h]
            for dr in range(3):
                for da in range(3):
                    for db in range(3):
                        total = total + weight[9 * dr + 3 * da + db] * coarse_ext[dr, a + 1 + da, db]
            if row == 0:
                total = total * top_in
            if row == rows_a - 1:
                total = total * bottom_in
            for bi, step_b in ((1 + cb, 0), (3, -1) if cb == 0 else (0, 1)):
                shifted = along_lanes(total, step_b)
                for ri, step_r in ((1 + cr, 0), (3, -1) if cr == 0 else (0, 1)):
                    mid_ext[ri, row, bi] = along_rows(shifted, step_r * s_count)

    def cell_rows(a, c, pr):
        return pl.ds(pl.multiple_of(((a * 8 + c) * 2 + pr) * h, 8), h)

    def fine_cells(c, carry):
        for pr in range(2):
            weight = [weight_at(1 + pr, c, o) for o in range(27)]
            for a in range(2 * ra):
                for pb in range(2):
                    at = (((pb * 2 * ra + a) * 8 + c) * 2 + pr) * h
                    total = fine_in[pl.ds(pl.multiple_of(at, 8), h), :]
                    for dr in range(3):
                        for da in range(3):
                            for db in range(3):
                                o = 9 * dr + 3 * da + db
                                total = total + weight[o] * mid_ext[pr + dr, a + da, pb + db]
                    cells[pb, cell_rows(a, c, pr), :] = total
        return carry

    lax.fori_loop(0, 8, fine_cells, 0)

    radial = (4 * (lax.broadcasted_iota(jnp.int32, (h, b), 0) // s_count)).astype(F32)

    def sum_before(x):
        step = s_count
        while step < h:
            x = x + along_rows(x, step)
            step *= 2
        return along_rows(x, s_count)

    def sum_all(x):
        step = s_count
        while step < h:
            x = x + pltpu.roll(x, step, axis=0)
            step *= 2
        return x

    def positions(at, carry):
        a, half = at // 2, lax.rem(at, 2)
        spots = []
        for cb in range(2):
            pb = 2 * half + cb
            rows = [cell_rows(a // 2, 4 * (f % 2) + 2 * lax.rem(a, 2) + cb, f // 2) for f in range(4)]
            emit = [pl.multiple_of(((pb * 4 + f) * 4 * ra + a) * h, 8) for f in range(4)]
            stars = [(star * 4 * ra + a) * 4 + pb for star in range(g.stars)]
            spots.append((pb, rows, emit, stars))
        density = [[jnp.exp(cells[half, rows[f], :]) for f in range(4)] for _, rows, _, _ in spots]
        glow = [[spacing * emit_in[pl.ds(emit[f], h), :] for f in range(4)] for _, _, emit, _ in spots]
        bins = [[block[pl.ds(begins["bins"] + row, 1), :] for row in stars] for _, _, _, stars in spots]
        data = [[block[pl.ds(begins["data"] + row, 1), :] for row in stars] for _, _, _, stars in spots]
        column = []
        for d, light in zip(density, glow):
            layer = [spacing * x for x in d]
            depth = sum_before(layer[0] + layer[1] + layer[2] + layer[3])
            for f in range(4):
                light[f] = light[f] * jnp.exp(-depth)
                depth = depth + layer[f]
            running = sum_before(light[0] + light[1] + light[2] + light[3])
            column.append([])
            for f in range(4):
                running = running + light[f]
                column[-1].append(running)
        total = [[jnp.zeros((h, b), F32) for f in range(4)] for _ in spots]
        seen_at = []
        for star in range(g.stars):
            for x, (pb, _, _, _) in enumerate(spots):
                bin_here = jnp.broadcast_to(bins[x][star], (h, b)) - radial
                mine = jnp.where(bin_here == 0, column[x][0], 0.0)
                for f in range(1, 4):
                    mine = jnp.where(bin_here == f, column[x][f], mine)
                predicted = sum_all(mine)
                residual = jnp.broadcast_to(data[x][star], (h, b)) - predicted
                seen_at.append((pb, star, residual))
                for f in range(4):
                    term = residual * (predicted - column[x][f])
                    total[x][f] = total[x][f] + jnp.where(bin_here > f, term, 0.0)
        for pb, star, residual in seen_at:
            for s in range(s_count):
                seen[pb, pl.ds((s * g.stars + star) * 4 * ra + a, 1), :] = residual[s : s + 1]
        for x, (_, rows, _, _) in enumerate(spots):
            for f in range(4):
                cells[half, rows[f], :] = -density[x][f] * total[x][f]
        return carry

    lax.fori_loop(0, 8 * ra, positions, 0)

    parts = [thirds(cells[phase]) for phase in range(2)]
    order = [place_columns(b, 2, phase) for phase in range(2)]
    for half in range(2):
        lanes = slice(half * b, (half + 1) * b)
        joined[half] = exact_dot(parts[0], order[0][:, lanes]) + exact_dot(parts[1], order[1][:, lanes])
    shown = None
    for phase in range(4):
        value = exact_dot(thirds(seen[phase]), place_columns(b, 4, phase))
        shown = value if shown is None else shown + value
    per = 4 * g.stars * ra * s_count
    for part in range(4):
        resid_out[part * per : (part + 1) * per] = shown[:, part * b : (part + 1) * b]
    for r in range(n):
        for s in range(s_count):
            sub = r * s_count + s
            for half in range(2):
                for a in range(2 * ra):
                    at = ((half * 2 * ra + a) * s_count + s) * 16
                    stage[r, at : at + 16] = joined[half, pl.ds(a * 16 * h + sub, 16, stride=h), :]
    for k in range(n):
        out_refs[k][...] = stage[lax.rem(me + k, n)]

    tall[...] = jnp.zeros(tall.shape, F32)
    for pr in range(2):
        def gather(c, carry, pr=pr):
            values = {(a, pb): cells[pb, cell_rows(a, c, pr), :] for a in range(2 * ra) for pb in range(2)}
            for dr in range(3):
                sums = {}
                for da in range(3):
                    for db in range(3):
                        weight = weight_at(1 + pr, c, 9 * dr + 3 * da + db)
                        for (a, pb), value in values.items():
                            key = (a + da, pb + db)
                            term = weight * value
                            sums[key] = sums[key] + term if key in sums else term
                for (row, bi), value in sums.items():
                    tall[pr + dr, row, bi] += value
            return carry

        lax.fori_loop(0, 8, gather, 0)
    for row in range(rows_a):
        for pr in range(2):
            for pb in range(2):
                bi, step_b = (3, 1) if pb == 0 else (0, -1)
                ri, step_r = (3, 1) if pr == 0 else (0, -1)
                close = tall[1 + pr, row, 1 + pb] + along_lanes(tall[1 + pr, row, bi], step_b)
                far = tall[ri, row, 1 + pb] + along_lanes(tall[ri, row, bi], step_b)
                value = close + along_rows(far, step_r * s_count)
                if row == 0:
                    value = value * top_in
                if row == rows_a - 1:
                    value = value * bottom_in
                at = ((2 * pr + pb) * rows_a + row) * h
                parent[at : at + h] = value

    coarse_sum[...] = jnp.zeros(coarse_sum.shape, F32)
    for dr in range(3):
        for db in range(3):
            sums = {}
            for c in range(8):
                cr, ca, cb = c // 4, c // 2 % 2, c % 2
                for da in range(3):
                    weight = weight_at(0, c, 9 * dr + 3 * da + db)
                    for row in range(1 - ca, rows_a, 2):
                        at = ((2 * cr + cb) * rows_a + row) * h
                        term = weight * parent[at : at + h]
                        key = (row - 1) // 2 + 1 + da
                        sums[key] = sums[key] + term if key in sums else term
            for a, value in sums.items():
                coarse_sum[a * h : (a + 1) * h] += along_lanes(along_rows(value, (dr - 1) * s_count), db - 1)

    edge_sum[...] = jnp.zeros(edge_sum.shape, F32)
    for q in range(g.w):
        @pl.when(worker == q)
        def _(q=q):
            low = q < g.w // 2
            if q == 0 or q == g.w - 1:
                for x in range(4):
                    at = (x * rows_a + (0 if low else rows_a - 1)) * h
                    edge_sum[x * h : (x + 1) * h] = parent[at : at + h]
            for t in range(2):
                a = (t - 2 if low else g.la + t) - q * ra + 2
                if 0 <= a < ra + 4:
                    edge_sum[(4 + t) * h : (5 + t) * h] = coarse_sum[a * h : (a + 1) * h]


def sums_kernel(g, parent, coarse_sum, edge_ref, *rest):
    out_refs, (stage,) = rest[: g.n], rest[g.n :]
    me, ang = lax.axis_index("rad"), lax.axis_index("ang")
    n, s_count, ra, h = g.n, g.s, g.ra, g.h
    rows_a = 2 * ra + 2
    live = jnp.where(jnp.minimum(me, g.w - 1) < g.w // 2, ang < g.m - 1, ang > 0)
    end_mid, end_coarse, _ = small_back(g)
    for r in range(n):
        for s in range(s_count):
            sub = r * s_count + s
            at = s * 4 * rows_a
            stage[r, at : at + 4 * rows_a] = parent[pl.ds(sub, 4 * rows_a, stride=h), :]
            at = end_mid + (ra + 4) * s
            stage[r, at : at + ra + 4] = coarse_sum[pl.ds(sub, ra + 4, stride=h), :]
            at = end_coarse + 6 * s
            stage[r, at : at + 6] = jnp.where(live, edge_ref[pl.ds(sub, 6, stride=h), :], 0.0)
    for k in range(n):
        out_refs[k][...] = stage[lax.rem(me + k, n)]


def large_owner_kernel(g, block, *rest):
    in_refs, shown_refs, rest = rest[: g.n], rest[g.n : 2 * g.n], rest[2 * g.n :]
    fine_out, resid_out, mid_mix, got, shown, fine = rest
    me = lax.axis_index("rad")
    n, b, s_count, ra, la = g.n, g.b, g.s, g.ra, g.la
    begins, _ = prepared_rows(g)
    per = 4 * g.stars * ra
    mid_mix[...] = block[begins["mid"] : begins["mid"] + 64]
    for k in range(n):
        got[lax.rem(me + n - k, n)] = in_refs[k][...]
        shown[me ^ k] = shown_refs[k][...]
    for q in range(g.w):
        for s in range(s_count):
            for half in range(2):
                for a in range(2 * ra):
                    at = ((half * 2 * ra + a) * s_count + s) * 16
                    rows = pl.ds(s * 32 * la + 2 * q * ra + a, 16, stride=2 * la)
                    fine[half, rows, :] = got[q, at : at + 16]
            for part in range(4):
                for star in range(g.stars):
                    at = (part * s_count + s) * per + star * 4 * ra
                    rows = slice(4 * q * ra, 4 * (q + 1) * ra)
                    resid_out[s, star, rows, part * b : (part + 1) * b] = shown[q, at : at + 4 * ra]
    for i in range(2):
        for j in range(8):
            rows = [begins["fine"] + 64 * i + 8 * c + j for c in range(8)]
            weight = [block[row : row + 1] for row in rows]
            for s in range(s_count):
                for half in range(2):
                    total = None
                    for c in range(8):
                        at = ((s * 8 + c) * 2 + i) * 2 * la
                        term = weight[c] * fine[half, at : at + 2 * la]
                        total = term if total is None else total + term
                    fine_out[s, j, i, :, half * b : (half + 1) * b] = total


def small_owner_kernel(g, mid_mix, *rest):
    in_refs, (coarse_out, mid_out, near, grad_mid, grad_coarse) = rest[: g.n], rest[g.n :]
    me = lax.axis_index("rad")
    n, s_count, ra, la = g.n, g.s, g.ra, g.la
    rows_a = 2 * ra + 2
    end_mid, end_coarse, _ = small_back(g)
    for k in range(n):
        near[lax.rem(me + n - k, n)] = in_refs[k][...]
    grad_mid[...] = jnp.zeros(grad_mid.shape, F32)
    grad_coarse[...] = jnp.zeros(grad_coarse.shape, F32)
    for q in range(g.w):
        low = q < g.w // 2
        for s in range(s_count):
            edge = near[q, end_coarse + 6 * s : end_coarse + 6 * s + 6]
            for x in range(4):
                at = s * 4 * rows_a + x * rows_a
                grad_mid[s, x, 2 * q * ra : 2 * q * ra + rows_a] += near[q, at : at + rows_a]
                row = 2 * la if low else 1
                grad_mid[s, x, row : row + 1] += edge[x : x + 1]
            at = end_mid + (ra + 4) * s
            grad_coarse[s, q * ra : q * ra + ra + 4] += near[q, at : at + ra + 4]
            row = la if low else 2
            grad_coarse[s, row : row + 2] += edge[4:6]
    for s in range(s_count):
        coarse_out[s, 0] = grad_coarse[s, 2 : 2 + la]
        cells = []
        for c in range(8):
            cr, ca, cb = c // 4, c // 2 % 2, c % 2
            cells.append(grad_mid[s, 2 * cr + cb, pl.ds(1 + ca, la, stride=2), :])
        for j in range(8):
            total = mid_mix[j : j + 1] * cells[0]
            for c in range(1, 8):
                total = total + mid_mix[j + 8 * c : j + 8 * c + 1] * cells[c]
            mid_out[s, j, 0] = total


def held(arrays):
    return [(pltpu.SMEM if len(x.shape) == 1 else pltpu.VMEM)(x.shape, x.dtype) for x in arrays]


def call(kernel, name, outs, operands, scratch, unmoved=0, written=0):
    vmem = pl.BlockSpec(memory_space=pltpu.VMEM)
    placed = pl.BlockSpec(memory_space=pl.ANY)
    limit = None if unmoved else VMEM_LIMIT
    return pl.pallas_call(
        kernel,
        name=name,
        out_shape=[jax.ShapeDtypeStruct(shape, kind) for shape, kind in outs],
        in_specs=[placed] * unmoved + [vmem] * (len(operands) - unmoved),
        out_specs=[placed] * written + [vmem] * (len(outs) - written),
        scratch_shapes=[pltpu.VMEM(shape, F32) if isinstance(shape, tuple) else shape for shape in scratch],
        compiler_params=pltpu.CompilerParams(vmem_limit_bytes=limit),
    )(*operands)


def per_device(
    g,
    coarse_field,
    excite_mid,
    excite_fine,
    kernels_mid,
    noise_mid,
    rows_mid,
    kernels_fine,
    noise_fine,
    rows_fine,
    emission,
    star_bins,
    star_data,
):
    n, m, s, la, b, stars, w, ra, h = g
    kernel = functools.partial
    rows_a = 2 * ra + 2
    workers = [(r, a, 1 if min(r, w - 1) < w // 2 else -1) for r in range(n) for a in range(m)]
    sideways = [(r * m + a, r * m + (a - step) % m) for r, a, step in workers]
    inward = [(to, at) for at, to in sideways]

    def exchange(blocks):
        return [blocks[0]] + [lax.ppermute(blocks[k], "rad", [(i, (i + k) % n) for i in range(n)]) for k in range(1, n)]

    noise_mid, noise_fine = noise_mid.transpose(1, 2, 0), noise_fine.transpose(1, 2, 0)
    large = (large_there(g)[-1], b)
    operands = (emission, rows_mid, noise_mid, coarse_field, excite_mid, rows_fine, noise_fine, excite_fine)
    sent = call(
        kernel(scatter_kernel, g),
        "scatter",
        [(large, F32)] * n,
        operands,
        [
            *held(operands),
            pltpu.SemaphoreType.DMA((8,)),
            pltpu.SemaphoreType.DMA((n,)),
            (32 * s * la, 2 * b),
            (2, 32 * s * la, b),
            (4, 16 * la, b),
            (w, *large),
            (s, 8, la, b),
            (s, la + 4, b),
        ],
        unmoved=8,
        written=n,
    )
    got = exchange(sent)
    operands = (rows_mid, rows_fine, noise_mid, noise_fine, kernels_mid, kernels_fine, star_bins, star_data)
    (block,) = call(
        kernel(prepare_kernel, g),
        "prepare",
        [((prepared_rows(g)[1], b), F32)],
        (*operands, sent[0]),
        [*held(operands), pltpu.SemaphoreType.DMA((8,)), (2, 4 * stars * ra, 4 * b)],
        unmoved=9,
    )
    spread, got[0], block = call(
        kernel(weight_kernel, g),
        "weights",
        [((24 * 27, h, b), F32), (large, F32), (block.shape, F32)],
        (block, sent[0]),
        [],
    )
    (near,) = call(kernel(relay_kernel, g), "relay", [((6 * h, b), F32)], got, [])
    near = lax.ppermute(near, ("rad", "ang"), inward)
    parts = [(64 * ra * h, b), (64 * ra * h, b), (4 * rows_a * h, b), ((ra + 4) * h, b)]
    unpacked = call(kernel(unpack_kernel, g), "unpack", [(part, F32) for part in parts], got, [])
    def everywhere(block):
        held, bit = {0: block}, n // 2
        while bit:
            swap = [(i, i ^ bit) for i in range(n)]
            held |= {i ^ bit: lax.ppermute(x, "rad", swap) for i, x in held.items()}
            bit //= 2
        return [held[i] for i in range(n)]

    field_out, resid_out = [(rows, b) for rows in large_back(g)]
    *done, shown, parent, coarse_sum, edge = call(
        kernel(main_kernel, g),
        "main",
        [(field_out, F32)] * n
        + [(shape, F32) for shape in (resid_out, (4 * rows_a * h, b), ((ra + 4) * h, b), (6 * h, b))],
        (block, spread, *unpacked, near),
        [
            (4 * rows_a * h, b),
            ((ra + 4) * h, b),
            (3, ra + 4, 3, h, b),
            (4, rows_a, 4, h, b),
            (4, rows_a, 4, h, b),
            (2, 32 * ra * h, b),
            (4, 4 * stars * ra * s, b),
            (2, 32 * ra * h, b),
            (n, *field_out),
        ],
    )
    small = (small_back(g)[-1], b)
    shown = everywhere(shown)
    got = exchange(done)
    edge = lax.ppermute(edge, ("rad", "ang"), sideways)
    near = exchange(
        call(
            kernel(sums_kernel, g),
            "sums",
            [(small, F32)] * n,
            (parent, coarse_sum, edge),
            [(n, *small)],
        )
    )
    grad_fine, residual, mid_mix = call(
        kernel(large_owner_kernel, g),
        "large_owner",
        [((s, 8, 2, 2 * la, 2 * b), F32), ((s, stars, 4 * la, 4 * b), F32), ((64, b), F32)],
        (block, *got, *shown),
        [(n, *field_out), (n, *resid_out), (2, 32 * s * la, b)],
    )
    grad_coarse, grad_mid = call(
        kernel(small_owner_kernel, g),
        "small_owner",
        [((s, 1, la, b), F32), ((s, 8, 1, la, b), F32)],
        (mid_mix, *near),
        [(n, *small), (s, 4, 2 * la + 2, b), (s, la + 4, b)],
    )
    return grad_coarse, grad_mid, grad_fine, residual


def solution(mesh):
    placed = (
        P(None, "rad", "ang", None),
        P(None, None, "rad", "ang", None),
        P(None, None, "rad", "ang", None),
        P(),
        P(),
        P(),
        P(),
        P(),
        P(),
        P("rad", "ang", None),
        P(None, "ang", None),
        P(None, "ang", None),
    )

    def local(*args):
        return per_device(make_plan(mesh, args[0], args[10]), *args)

    return jax.shard_map(
        local,
        mesh=mesh,
        in_specs=placed,
        out_specs=(
            P(None, "rad", "ang", None),
            P(None, None, "rad", "ang", None),
            P(None, None, "rad", "ang", None),
            P(None, None, "ang", None),
        ),
        check_vma=False,
    )
```

```python
import functools
import typing

import jax
import jax.numpy as jnp
from jax import lax
from jax.experimental import pallas as pl
from jax.experimental.pallas import tpu as pltpu
from jax.sharding import PartitionSpec as P

F32 = jnp.float32
BF16 = jnp.bfloat16
VMEM_LIMIT = 24 * 1024 * 1024


class Plan(typing.NamedTuple):
    n: int
    m: int
    s: int
    la: int
    b: int
    stars: int
    w: int
    ra: int
    h: int


def make_plan(mesh, coarse, star_bins):
    n, m = mesh.shape["rad"], mesh.shape["ang"]
    s, rows, la, b = coarse.shape
    w = max(d for d in range(1, min(n, la) + 1) if la % d == 0)
    ra = la // w
    assert rows == 1 and n & (n - 1) == 0 and w % 2 == 0 and (w // 2) * ra >= 2
    return Plan(n, m, s, la, b, star_bins.shape[0], w, ra, n * s)


def eights(rows):
    return -(-rows // 8) * 8


def large_there(g):
    fine = 2 * 2 * g.ra * g.s * 16
    emit = fine + 16 * 4 * g.ra
    mix = emit + g.s * 4 * (2 * g.ra + 2)
    coarse = mix + g.s * (g.ra + 4)
    return fine, emit, mix, coarse, eights(coarse + 6 * g.s)


def rows_back(g):
    field = 2 * 2 * g.ra * g.s * 16
    mid = field + g.s * 4 * (2 * g.ra + 2)
    coarse = mid + g.s * (g.ra + 4)
    return field, mid, coarse, eights(coarse + 6 * g.s)


def prepared_rows(g):
    sizes = dict(
        stencil=24 * g.h,
        bins=16 * g.stars * g.ra,
        data=16 * g.stars * g.ra,
        mid=64,
        fine=128,
    )
    begins, at = {}, 0
    for part, size in sizes.items():
        begins[part] = at
        at += size
    return begins, at


def table_weights(table_ref, entry):
    lane = lax.broadcasted_iota(jnp.int32, table_ref.shape[1:], 1)
    columns = [
        jnp.sum(jnp.where(lane == entry, table_ref[c], 0.0), axis=1, keepdims=True) for c in range(table_ref.shape[0])
    ]
    return lambda c, j: columns[c][j : j + 1]


def start_all(pairs, sems, first=0):
    copies = [pltpu.make_async_copy(source, here, sems.at[first + i]) for i, (source, here) in enumerate(pairs)]
    for copy in copies:
        copy.start()
    return copies


def wait_all(copies):
    for copy in copies:
        copy.wait()


def pick_columns(length, ways, phase):
    src = lax.broadcasted_iota(jnp.int32, (length * ways, length), 0)
    dst = lax.broadcasted_iota(jnp.int32, (length * ways, length), 1)
    return jnp.where(src == ways * dst + phase, 1.0, 0.0).astype(BF16)


def place_columns(length, ways, phase):
    src = lax.broadcasted_iota(jnp.int32, (length, length * ways), 0)
    dst = lax.broadcasted_iota(jnp.int32, (length, length * ways), 1)
    return jnp.where(dst == ways * src + phase, 1.0, 0.0).astype(BF16)


def thirds(x):
    high = x.astype(BF16)
    rest = x - high.astype(F32)
    middle = rest.astype(BF16)
    return high, middle, (rest - middle.astype(F32)).astype(BF16)


def exact_dot(parts, choice):
    high, middle, low = [jnp.dot(part, choice, preferred_element_type=F32) for part in parts]
    return high + (middle + low)


def along_lanes(x, step):
    if step == 0:
        return x
    size = x.shape[1]
    lane = lax.broadcasted_iota(jnp.int32, x.shape, 1)
    edge = 0 if step > 0 else size - 1
    return jnp.where(lane == edge, 0.0, pltpu.roll(x, step % size, axis=1))


def along_rows(x, step):
    if step == 0:
        return x
    size = x.shape[0]
    row = lax.broadcasted_iota(jnp.int32, x.shape, 0)
    kept = row >= step if step > 0 else row < size + step
    return jnp.where(kept, pltpu.roll(x, step % size, axis=0), 0.0)


def prepare_kernel(g, *rest):
    sources, block, rest = rest[:8], rest[9], rest[10:]
    held, (sems, gathered) = rest[:8], rest[8:]
    copies = start_all(list(zip(sources, held)), sems)
    rows_mid, rows_fine, noise_mid, noise_fine, mid_table, fine_table, bins_ref, data_ref = held
    begins, _ = prepared_rows(g)
    me = lax.axis_index("rad")
    worker = jnp.minimum(me, g.w - 1)
    per, b = 4 * g.ra, g.b
    choices = [pick_columns(b, 4, phase) for phase in range(4)]
    wait_all(copies)
    for r in range(g.n):
        tables = [mid_table[rows_mid[r]], fine_table[rows_fine[2 * r]], fine_table[rows_fine[2 * r + 1]]]
        for level, table in enumerate(tables):
            for c in range(8):
                at = begins["stencil"] + (level * 8 + c) * g.h + r * g.s
                block[at : at + g.s, :27] = jnp.broadcast_to(table[c : c + 1], (g.s, 27))
    entries = [(begins["mid"], noise_mid, rows_mid[me])]
    entries += [(begins["fine"] + 64 * i, noise_fine, rows_fine[2 * me + i]) for i in range(2)]
    for at, table, entry in entries:
        lane = lax.broadcasted_iota(jnp.int32, table.shape[1:], 1)
        for c in range(8):
            column = jnp.sum(jnp.where(lane == entry, table[c], 0.0), axis=1, keepdims=True)
            block[at + 8 * c : at + 8 * c + 8] = jnp.broadcast_to(column, (8, b))
    for q in range(g.w):
        @pl.when(worker == q)
        def _(q=q):
            for star in range(g.stars):
                gathered[0, star * per : (star + 1) * per] = bins_ref[star, q * per : (q + 1) * per].astype(F32)
                gathered[1, star * per : (star + 1) * per] = data_ref[star, q * per : (q + 1) * per]
    bins = gathered[0].astype(BF16)
    parts = thirds(gathered[1])
    for phase in range(4):
        rows = pl.ds(begins["bins"] + phase, g.stars * per, stride=4)
        block[rows, :] = jnp.dot(bins, choices[phase], preferred_element_type=F32)
        rows = pl.ds(begins["data"] + phase, g.stars * per, stride=4)
        block[rows, :] = exact_dot(parts, choices[phase])


def scatter_kernel(g, *rest):
    sources, out_refs, rest = rest[:8], rest[8 : 8 + g.n], rest[8 + g.n :]
    held, (sems, out_sems, raw, split, lit, stage, mixed, wide) = rest[:8], rest[8:]
    copies = start_all(list(zip(sources, held)), sems)
    emission_ref, rows_mid, noise_mid, coarse_ref, excite_ref, rows_ref, noise_ref, fine_ref = held
    me = lax.axis_index("rad")
    b, s_count, la = g.b, g.s, g.la
    end_fine, end_emit, end_mix, end_coarse, _ = large_there(g)
    choices = [pick_columns(b, 4, phase) for phase in range(4)]
    copies[0].wait()
    parts = thirds(emission_ref[...].reshape(16 * la, 4 * b))
    for phase in range(4):
        lit[phase] = exact_dot(parts, choices[phase])
    for q in range(g.w):
        for phase in range(4):
            for f in range(4):
                at = end_fine + (phase * 4 + f) * 4 * g.ra
                rows = slice(f * 4 * la + 4 * q * g.ra, f * 4 * la + 4 * (q + 1) * g.ra)
                stage[q, at : at + 4 * g.ra] = lit[phase, rows]
    wait_all(copies[1:5])
    weight = table_weights(noise_mid, rows_mid[me])
    for c in range(8):
        for s in range(s_count):
            total = weight(c, 0) * excite_ref[s, 0, 0]
            for j in range(1, 8):
                total = total + weight(c, j) * excite_ref[s, j, 0]
            mixed[s, c] = total
    wide[...] = jnp.zeros(wide.shape, F32)
    for s in range(s_count):
        wide[s, 2 : 2 + la] = coarse_ref[s, 0]
    for q in range(g.w):
        low = q < g.w // 2
        for s in range(s_count):
            for row in range(2 * g.ra + 2):
                a, ca = divmod(2 * q * g.ra - 1 + row, 2)
                for cr in range(2):
                    for cb in range(2):
                        at = end_emit + ((s * (2 * g.ra + 2) + row) * 2 + cr) * 2 + cb
                        if 0 <= a < la:
                            stage[q, at : at + 1] = mixed[s, 4 * cr + 2 * ca + cb, a : a + 1]
                        else:
                            stage[q, at : at + 1] = jnp.zeros((1, b), F32)
            at = end_mix + (g.ra + 4) * s
            stage[q, at : at + g.ra + 4] = wide[s, q * g.ra : q * g.ra + g.ra + 4]
            at = end_coarse + 6 * s
            row = la - 1 if low else 0
            for cr in range(2):
                for cb in range(2):
                    c = 4 * cr + (2 if low else 0) + cb
                    stage[q, at + 2 * cr + cb : at + 2 * cr + cb + 1] = mixed[s, c, row : row + 1]
            row = la - 2 if low else 0
            stage[q, at + 4 : at + 6] = coarse_ref[s, 0, row : row + 2]
    wait_all(copies[5:])
    for i in range(2):
        weight = table_weights(noise_ref, rows_ref[2 * me + i])
        for c in range(8):
            weights = [weight(c, j) for j in range(8)]
            for s in range(s_count):
                total = weights[0] * fine_ref[s, 0, i]
                for j in range(1, 8):
                    total = total + weights[j] * fine_ref[s, j, i]
                at = ((s * 8 + c) * 2 + i) * 2 * la
                raw[at : at + 2 * la] = total
    parts = thirds(raw[...])
    for phase in range(2):
        split[phase] = exact_dot(parts, pick_columns(b, 2, phase))
    for q in range(g.w):
        for phase in range(2):
            for a in range(2 * g.ra):
                for s in range(s_count):
                    at = ((phase * 2 * g.ra + a) * s_count + s) * 16
                    rows = pl.ds(s * 32 * la + 2 * q * g.ra + a, 16, stride=2 * la)
                    stage[q, at : at + 16] = split[phase, rows, :]
    workers = [jnp.minimum(lax.rem(me + k, g.n), g.w - 1) for k in range(g.n)]
    wait_all(start_all([(stage.at[worker], out) for worker, out in zip(workers, out_refs)], out_sems))


def relay_kernel(g, *rest):
    in_refs, (edge_out,) = rest[: g.n], rest[g.n :]
    me = lax.axis_index("rad")
    _, _, _, end_coarse, _ = large_there(g)
    for k in range(g.n):
        source = lax.rem(me + g.n - k, g.n)
        for s in range(g.s):
            rows = pl.ds(source * g.s + s, 6, stride=g.h)
            edge_out[rows, :] = in_refs[k][end_coarse + 6 * s : end_coarse + 6 * s + 6]


def unpack_kernel(g, *rest):
    in_refs, (fine_out, emit_out, mix_out, coarse_out) = rest[: g.n], rest[g.n :]
    me = lax.axis_index("rad")
    end_fine, end_emit, end_mix, _, _ = large_there(g)
    h, ra, rows_a = g.h, g.ra, 2 * g.ra + 2
    for k in range(g.n):
        source = lax.rem(me + g.n - k, g.n)
        got = in_refs[k]
        for s in range(g.s):
            sub = source * g.s + s
            for x in range(4 * ra):
                at = (x * g.s + s) * 16
                fine_out[pl.ds(x * 16 * h + sub, 16, stride=h), :] = got[at : at + 16]
            emit_out[pl.ds(sub, 64 * ra, stride=h), :] = got[end_fine:end_emit]
            at = end_emit + s * 4 * rows_a
            mix_out[pl.ds(sub, 4 * rows_a, stride=h), :] = got[at : at + 4 * rows_a]
            at = end_mix + (ra + 4) * s
            coarse_out[pl.ds(sub, ra + 4, stride=h), :] = got[at : at + ra + 4]


def weight_kernel(g, block, own, spread, own_out, block_out):
    own_out[...] = own[...]
    block_out[...] = block[...]
    begins, _ = prepared_rows(g)
    for x in range(24):
        at = begins["stencil"] + x * g.h
        tile = block[at : at + g.h]
        for o in range(27):
            spread[x * 27 + o] = jnp.broadcast_to(tile[:, o : o + 1], (g.h, g.b))


def edges_inside(g, worker):
    first = lax.axis_index("ang") * g.la + worker * g.ra
    inside = jnp.where(first > 0, 1.0, 0.0), jnp.where(first + g.ra < g.m * g.la, 1.0, 0.0)
    return [x.astype(F32) for x in inside]


def cell_rows_of(g, a, c, pr):
    return pl.ds(pl.multiple_of(((a * 8 + c) * 2 + pr) * g.h, 8), g.h)


def forward_kernel(g, block, spread, *rest):
    n, b, s_count, ra, h = g.n, g.b, g.s, g.ra, g.h
    fine_in, emit_in, mixed, coarse, near = rest[:5]
    cells, resid_out = rest[5:7]
    mix_in, coarse_in, coarse_ext, mid_ext, seen = rest[7:]
    me, ang = lax.axis_index("rad"), lax.axis_index("ang")
    rows_a = 2 * ra + 2
    spacing = 1.0 / (4 * n)
    worker = jnp.minimum(me, g.w - 1)
    begins, _ = prepared_rows(g)

    def weight_at(level, c, o):
        return spread[(level * 8 + c) * 27 + o]

    mix_in[...] = mixed[...]
    coarse_in[...] = coarse[...]
    live = jnp.where(worker < g.w // 2, ang > 0, ang < g.m - 1)
    for q in range(g.w):
        @pl.when(jnp.logical_and(worker == q, live))
        def _(q=q):
            if q == 0:
                mix_in[: 4 * h] = near[: 4 * h]
            if q == g.w - 1:
                mix_in[4 * (rows_a - 1) * h :] = near[: 4 * h]
            for a in range(ra + 4):
                row = q * ra - 2 + a
                if row < 0 or row >= g.la:
                    at = (4 + (row + 2 if row < 0 else row - g.la)) * h
                    coarse_in[a * h : (a + 1) * h] = near[at : at + h]

    top_in, bottom_in = edges_inside(g, worker)
    for a in range(ra + 4):
        x = coarse_in[a * h : (a + 1) * h]
        for db in range(3):
            shifted = along_lanes(x, 1 - db)
            for dr in range(3):
                coarse_ext[dr, a, db] = along_rows(shifted, (1 - dr) * s_count)
    for c in range(8):
        cr, ca, cb = c // 4, c // 2 % 2, c % 2
        weight = [weight_at(0, c, o) for o in range(27)]
        for row in range(1 - ca, rows_a, 2):
            a = (row - 1) // 2
            at = (row * 4 + 2 * cr + cb) * h
            total = mix_in[at : at + h]
            for dr in range(3):
                for da in range(3):
                    for db in range(3):
                        total = total + weight[9 * dr + 3 * da + db] * coarse_ext[dr, a + 1 + da, db]
            if row == 0:
                total = total * top_in
            if row == rows_a - 1:
                total = total * bottom_in
            for bi, step_b in ((1 + cb, 0), (3, -1) if cb == 0 else (0, 1)):
                shifted = along_lanes(total, step_b)
                for ri, step_r in ((1 + cr, 0), (3, -1) if cr == 0 else (0, 1)):
                    mid_ext[ri, row, bi] = along_rows(shifted, step_r * s_count)

    cell_rows = functools.partial(cell_rows_of, g)

    def fine_cells(c, carry):
        for pr in range(2):
            weight = [weight_at(1 + pr, c, o) for o in range(27)]
            for a in range(2 * ra):
                for pb in range(2):
                    at = (((pb * 2 * ra + a) * 8 + c) * 2 + pr) * h
                    total = fine_in[pl.ds(pl.multiple_of(at, 8), h), :]
                    for dr in range(3):
                        for da in range(3):
                            for db in range(3):
                                o = 9 * dr + 3 * da + db
                                total = total + weight[o] * mid_ext[pr + dr, a + da, pb + db]
                    cells[pb, cell_rows(a, c, pr), :] = total
        return carry

    lax.fori_loop(0, 8, fine_cells, 0)

    radial = (4 * (lax.broadcasted_iota(jnp.int32, (h, b), 0) // s_count)).astype(F32)

    def sum_before(x):
        step = s_count
        while step < h:
            x = x + along_rows(x, step)
            step *= 2
        return along_rows(x, s_count)

    def sum_all(x):
        step = s_count
        while step < h:
            x = x + pltpu.roll(x, step, axis=0)
            step *= 2
        return x

    def positions(at, carry):
        a, half = at // 2, lax.rem(at, 2)
        spots = []
        for cb in range(2):
            pb = 2 * half + cb
            rows = [cell_rows(a // 2, 4 * (f % 2) + 2 * lax.rem(a, 2) + cb, f // 2) for f in range(4)]
            emit = [pl.multiple_of(((pb * 4 + f) * 4 * ra + a) * h, 8) for f in range(4)]
            stars = [(star * 4 * ra + a) * 4 + pb for star in range(g.stars)]
            spots.append((pb, rows, emit, stars))
        density = [[jnp.exp(cells[half, rows[f], :]) for f in range(4)] for _, rows, _, _ in spots]
        glow = [[spacing * emit_in[pl.ds(emit[f], h), :] for f in range(4)] for _, _, emit, _ in spots]
        bins = [[block[pl.ds(begins["bins"] + row, 1), :] for row in stars] for _, _, _, stars in spots]
        data = [[block[pl.ds(begins["data"] + row, 1), :] for row in stars] for _, _, _, stars in spots]
        column = []
        for d, light in zip(density, glow):
            layer = [spacing * x for x in d]
            depth = sum_before(layer[0] + layer[1] + layer[2] + layer[3])
            for f in range(4):
                light[f] = light[f] * jnp.exp(-depth)
                depth = depth + layer[f]
            running = sum_before(light[0] + light[1] + light[2] + light[3])
            column.append([])
            for f in range(4):
                running = running + light[f]
                column[-1].append(running)
        total = [[jnp.zeros((h, b), F32) for f in range(4)] for _ in spots]
        seen_at = []
        for star in range(g.stars):
            for x, (pb, _, _, _) in enumerate(spots):
                bin_here = jnp.broadcast_to(bins[x][star], (h, b)) - radial
                mine = jnp.where(bin_here == 0, column[x][0], 0.0)
                for f in range(1, 4):
                    mine = jnp.where(bin_here == f, column[x][f], mine)
                predicted = sum_all(mine)
                residual = jnp.broadcast_to(data[x][star], (h, b)) - predicted
                seen_at.append((pb, star, residual))
                for f in range(4):
                    term = residual * (predicted - column[x][f])
                    total[x][f] = total[x][f] + jnp.where(bin_here > f, term, 0.0)
        for pb, star, residual in seen_at:
            for s in range(s_count):
                seen[pb, pl.ds((s * g.stars + star) * 4 * ra + a, 1), :] = residual[s : s + 1]
        for x, (_, rows, _, _) in enumerate(spots):
            for f in range(4):
                cells[half, rows[f], :] = -density[x][f] * total[x][f]
        return carry

    lax.fori_loop(0, 8 * ra, positions, 0)

    shown = None
    for phase in range(4):
        value = exact_dot(thirds(seen[phase]), place_columns(b, 4, phase))
        shown = value if shown is None else shown + value
    per = 4 * g.stars * ra * s_count
    for part in range(4):
        resid_out[part * per : (part + 1) * per] = shown[:, part * b : (part + 1) * b]


def backward_kernel(g, spread, cells, parent, coarse_sum, edge_sum, tall):
    n, b, s_count, ra, h = g.n, g.b, g.s, g.ra, g.h
    rows_a = 2 * ra + 2
    worker = jnp.minimum(lax.axis_index("rad"), g.w - 1)
    top_in, bottom_in = edges_inside(g, worker)
    cell_rows = functools.partial(cell_rows_of, g)

    def weight_at(level, c, o):
        return spread[(level * 8 + c) * 27 + o]

    tall[...] = jnp.zeros(tall.shape, F32)
    for pr in range(2):
        def gather(c, carry, pr=pr):
            values = {(a, pb): cells[pb, cell_rows(a, c, pr), :] for a in range(2 * ra) for pb in range(2)}
            for dr in range(3):
                sums = {}
                for da in range(3):
                    for db in range(3):
                        weight = weight_at(1 + pr, c, 9 * dr + 3 * da + db)
                        for (a, pb), value in values.items():
                            key = (a + da, pb + db)
                            term = weight * value
                            sums[key] = sums[key] + term if key in sums else term
                for (row, bi), value in sums.items():
                    tall[pr + dr, row, bi] += value
            return carry

        lax.fori_loop(0, 8, gather, 0)
    for row in range(rows_a):
        for pr in range(2):
            for pb in range(2):
                bi, step_b = (3, 1) if pb == 0 else (0, -1)
                ri, step_r = (3, 1) if pr == 0 else (0, -1)
                close = tall[1 + pr, row, 1 + pb] + along_lanes(tall[1 + pr, row, bi], step_b)
                far = tall[ri, row, 1 + pb] + along_lanes(tall[ri, row, bi], step_b)
                value = close + along_rows(far, step_r * s_count)
                if row == 0:
                    value = value * top_in
                if row == rows_a - 1:
                    value = value * bottom_in
                at = ((2 * pr + pb) * rows_a + row) * h
                parent[at : at + h] = value

    coarse_sum[...] = jnp.zeros(coarse_sum.shape, F32)
    for dr in range(3):
        for db in range(3):
            sums = {}
            for c in range(8):
                cr, ca, cb = c // 4, c // 2 % 2, c % 2
                for da in range(3):
                    weight = weight_at(0, c, 9 * dr + 3 * da + db)
                    for row in range(1 - ca, rows_a, 2):
                        at = ((2 * cr + cb) * rows_a + row) * h
                        term = weight * parent[at : at + h]
                        key = (row - 1) // 2 + 1 + da
                        sums[key] = sums[key] + term if key in sums else term
            for a, value in sums.items():
                coarse_sum[a * h : (a + 1) * h] += along_lanes(along_rows(value, (dr - 1) * s_count), db - 1)

    edge_sum[...] = jnp.zeros(edge_sum.shape, F32)
    for q in range(g.w):
        @pl.when(worker == q)
        def _(q=q):
            low = q < g.w // 2
            if q == 0 or q == g.w - 1:
                for x in range(4):
                    at = (x * rows_a + (0 if low else rows_a - 1)) * h
                    edge_sum[x * h : (x + 1) * h] = parent[at : at + h]
            for t in range(2):
                a = (t - 2 if low else g.la + t) - q * ra + 2
                if 0 <= a < ra + 4:
                    edge_sum[(4 + t) * h : (5 + t) * h] = coarse_sum[a * h : (a + 1) * h]


def lanes_kernel(g, cells, out, joined):
    n, b, s_count, ra, h = g.n, g.b, g.s, g.ra, g.h
    parts = [thirds(cells[phase]) for phase in range(2)]
    order = [place_columns(b, 2, phase) for phase in range(2)]
    for half in range(2):
        lanes = slice(half * b, (half + 1) * b)
        joined[half] = exact_dot(parts[0], order[0][:, lanes]) + exact_dot(parts[1], order[1][:, lanes])
    for r in range(n):
        for s in range(s_count):
            for half in range(2):
                for a in range(2 * ra):
                    at = ((half * 2 * ra + a) * s_count + s) * 16
                    out[r, at : at + 16] = joined[half, pl.ds(a * 16 * h + r * s_count + s, 16, stride=h), :]


def sums_kernel(g, field, parent, coarse_sum, edge_ref, *rest):
    out_refs, (stage,) = rest[: g.n], rest[g.n :]
    me, ang = lax.axis_index("rad"), lax.axis_index("ang")
    n, s_count, ra, h = g.n, g.s, g.ra, g.h
    rows_a = 2 * ra + 2
    live = jnp.where(jnp.minimum(me, g.w - 1) < g.w // 2, ang < g.m - 1, ang > 0)
    end_field, end_mid, end_coarse, end = rows_back(g)
    for r in range(n):
        for s in range(s_count):
            sub = r * s_count + s
            at = s * 4 * rows_a
            stage[r, at : at + 4 * rows_a] = parent[pl.ds(sub, 4 * rows_a, stride=h), :]
            at = end_mid - end_field + (ra + 4) * s
            stage[r, at : at + ra + 4] = coarse_sum[pl.ds(sub, ra + 4, stride=h), :]
            at = end_coarse - end_field + 6 * s
            stage[r, at : at + 6] = jnp.where(live, edge_ref[pl.ds(sub, 6, stride=h), :], 0.0)
    for k in range(n):
        owner = lax.rem(me + k, n)
        out_refs[k][:end_field] = field[owner]
        out_refs[k][end_field:end] = stage[owner]


def join_kernel(g, one, two, after, out):
    rows = one.shape[0]
    out[:rows] = one[...]
    out[rows:] = two[...]


def resid_owner_kernel(g, ids, block, *rest):
    in_refs, (resid_out, mixes, shown) = rest[:-3], rest[-3:]
    me = lax.axis_index("rad")
    b, s_count, ra = g.b, g.s, g.ra
    begins, end = prepared_rows(g)
    per = 4 * g.stars * ra
    mixes[...] = block[begins["mid"] : end]
    for ref, held_ids in zip(in_refs, ids):
        for at, i in enumerate(held_ids):
            shown[me ^ i] = ref[at * 4 * s_count * per : (at + 1) * 4 * s_count * per]
    for q in range(g.w):
        for s in range(s_count):
            for part in range(4):
                for star in range(g.stars):
                    at = (part * s_count + s) * per + star * 4 * ra
                    rows = slice(4 * q * ra, 4 * (q + 1) * ra)
                    resid_out[s, star, rows, part * b : (part + 1) * b] = shown[q, at : at + 4 * ra]


def owner_kernel(g, mixes, *rest):
    in_refs, (coarse_out, mid_out, fine_out, got, fine, grad_mid, grad_coarse) = rest[: g.n], rest[g.n :]
    me = lax.axis_index("rad")
    n, b, s_count, ra, la = g.n, g.b, g.s, g.ra, g.la
    rows_a = 2 * ra + 2
    end_field, end_mid, end_coarse, _ = rows_back(g)
    for k in range(n):
        got[lax.rem(me + n - k, n)] = in_refs[k][...]
    grad_mid[...] = jnp.zeros(grad_mid.shape, F32)
    grad_coarse[...] = jnp.zeros(grad_coarse.shape, F32)
    for q in range(g.w):
        low = q < g.w // 2
        for s in range(s_count):
            for half in range(2):
                for a in range(2 * ra):
                    at = ((half * 2 * ra + a) * s_count + s) * 16
                    rows = pl.ds(s * 32 * la + 2 * q * ra + a, 16, stride=2 * la)
                    fine[half, rows, :] = got[q, at : at + 16]
            edge = got[q, end_coarse + 6 * s : end_coarse + 6 * s + 6]
            for x in range(4):
                at = end_field + s * 4 * rows_a + x * rows_a
                grad_mid[s, x, 2 * q * ra : 2 * q * ra + rows_a] += got[q, at : at + rows_a]
                row = 2 * la if low else 1
                grad_mid[s, x, row : row + 1] += edge[x : x + 1]
            at = end_mid + (ra + 4) * s
            grad_coarse[s, q * ra : q * ra + ra + 4] += got[q, at : at + ra + 4]
            row = la if low else 2
            grad_coarse[s, row : row + 2] += edge[4:6]
    for i in range(2):
        for j in range(8):
            rows = [64 + 64 * i + 8 * c + j for c in range(8)]
            weight = [mixes[row : row + 1] for row in rows]
            for s in range(s_count):
                for half in range(2):
                    total = None
                    for c in range(8):
                        at = ((s * 8 + c) * 2 + i) * 2 * la
                        term = weight[c] * fine[half, at : at + 2 * la]
                        total = term if total is None else total + term
                    fine_out[s, j, i, :, half * b : (half + 1) * b] = total
    for s in range(s_count):
        coarse_out[s, 0] = grad_coarse[s, 2 : 2 + la]
        cells = []
        for c in range(8):
            cr, ca, cb = c // 4, c // 2 % 2, c % 2
            cells.append(grad_mid[s, 2 * cr + cb, pl.ds(1 + ca, la, stride=2), :])
        for j in range(8):
            total = mixes[j : j + 1] * cells[0]
            for c in range(1, 8):
                total = total + mixes[j + 8 * c : j + 8 * c + 1] * cells[c]
            mid_out[s, j, 0] = total


def held(arrays):
    return [(pltpu.SMEM if len(x.shape) == 1 else pltpu.VMEM)(x.shape, x.dtype) for x in arrays]


def call(kernel, name, outs, operands, scratch, unmoved=0, written=0):
    vmem = pl.BlockSpec(memory_space=pltpu.VMEM)
    placed = pl.BlockSpec(memory_space=pl.ANY)
    limit = None if unmoved else VMEM_LIMIT
    return pl.pallas_call(
        kernel,
        name=name,
        out_shape=[jax.ShapeDtypeStruct(shape, kind) for shape, kind in outs],
        in_specs=[placed] * unmoved + [vmem] * (len(operands) - unmoved),
        out_specs=[placed] * written + [vmem] * (len(outs) - written),
        scratch_shapes=[pltpu.VMEM(shape, F32) if isinstance(shape, tuple) else shape for shape in scratch],
        compiler_params=pltpu.CompilerParams(vmem_limit_bytes=limit),
    )(*operands)


def per_device(
    g,
    coarse_field,
    excite_mid,
    excite_fine,
    kernels_mid,
    noise_mid,
    rows_mid,
    kernels_fine,
    noise_fine,
    rows_fine,
    emission,
    star_bins,
    star_data,
):
    n, m, s, la, b, stars, w, ra, h = g
    kernel = functools.partial
    rows_a = 2 * ra + 2
    workers = [(r, a, 1 if min(r, w - 1) < w // 2 else -1) for r in range(n) for a in range(m)]
    sideways = [(r * m + a, r * m + (a - step) % m) for r, a, step in workers]
    inward = [(to, at) for at, to in sideways]

    def exchange(blocks):
        return [blocks[0]] + [lax.ppermute(blocks[k], "rad", [(i, (i + k) % n) for i in range(n)]) for k in range(1, n)]

    noise_mid, noise_fine = noise_mid.transpose(1, 2, 0), noise_fine.transpose(1, 2, 0)
    large = (large_there(g)[-1], b)
    operands = (emission, rows_mid, noise_mid, coarse_field, excite_mid, rows_fine, noise_fine, excite_fine)
    sent = call(
        kernel(scatter_kernel, g),
        "scatter",
        [(large, F32)] * n,
        operands,
        [
            *held(operands),
            pltpu.SemaphoreType.DMA((8,)),
            pltpu.SemaphoreType.DMA((n,)),
            (32 * s * la, 2 * b),
            (2, 32 * s * la, b),
            (4, 16 * la, b),
            (w, *large),
            (s, 8, la, b),
            (s, la + 4, b),
        ],
        unmoved=8,
        written=n,
    )
    got = exchange(sent)
    operands = (rows_mid, rows_fine, noise_mid, noise_fine, kernels_mid, kernels_fine, star_bins, star_data)
    (block,) = call(
        kernel(prepare_kernel, g),
        "prepare",
        [((prepared_rows(g)[1], b), F32)],
        (*operands, sent[0]),
        [*held(operands), pltpu.SemaphoreType.DMA((8,)), (2, 4 * stars * ra, 4 * b)],
        unmoved=9,
    )
    spread, got[0], block = call(
        kernel(weight_kernel, g),
        "weights",
        [((24 * 27, h, b), F32), (large, F32), (block.shape, F32)],
        (block, sent[0]),
        [],
    )
    (near,) = call(kernel(relay_kernel, g), "relay", [((6 * h, b), F32)], got, [])
    near = lax.ppermute(near, ("rad", "ang"), inward)
    parts = [(64 * ra * h, b), (64 * ra * h, b), (4 * rows_a * h, b), ((ra + 4) * h, b)]
    unpacked = call(kernel(unpack_kernel, g), "unpack", [(part, F32) for part in parts], got, [])
    def everywhere(block, after):
        ids, bit = [0], n // 2
        while True:
            got = lax.ppermute(block, "rad", [(i, i ^ bit) for i in range(n)])
            more = [i ^ bit for i in ids]
            if bit == 1:
                return (block, got), (ids, more)
            shape = (2 * block.shape[0], b)
            (block,) = call(kernel(join_kernel, g), "join", [(shape, F32)], (block, got, after), [])
            ids, bit = ids + more, bit // 2

    end_field, _, _, end = rows_back(g)
    resid_rows = 16 * stars * ra * s
    cells, shown = call(
        kernel(forward_kernel, g),
        "forward",
        [((2, 32 * ra * h, b), F32), ((resid_rows, b), F32)],
        (block, spread, *unpacked, near),
        [
            (4 * rows_a * h, b),
            ((ra + 4) * h, b),
            (3, ra + 4, 3, h, b),
            (4, rows_a, 4, h, b),
            (4, 4 * stars * ra * s, b),
        ],
    )
    parent, coarse_sum, edge = call(
        kernel(backward_kernel, g),
        "backward",
        [((4 * rows_a * h, b), F32), (((ra + 4) * h, b), F32), ((6 * h, b), F32)],
        (spread, cells),
        [(4, rows_a, 4, h, b)],
    )
    edge = lax.ppermute(edge, ("rad", "ang"), sideways)
    (field,) = call(
        kernel(lanes_kernel, g), "lanes", [((n, end_field, b), F32)], (cells,), [(2, 32 * ra * h, b)]
    )
    got = exchange(
        call(
            kernel(sums_kernel, g),
            "sums",
            [((end, b), F32)] * n,
            (field, parent, coarse_sum, edge),
            [(n, end - end_field, b)],
        )
    )
    shown, ids = everywhere(shown, got[0])
    residual, mixes = call(
        kernel(resid_owner_kernel, g, ids),
        "resid_owner",
        [((s, stars, 4 * la, 4 * b), F32), ((192, b), F32)],
        (block, *shown),
        [(n, resid_rows, b)],
    )
    grad_coarse, grad_mid, grad_fine = call(
        kernel(owner_kernel, g),
        "owner",
        [((s, 1, la, b), F32), ((s, 8, 1, la, b), F32), ((s, 8, 2, 2 * la, 2 * b), F32)],
        (mixes, *got),
        [(n, end, b), (2, 32 * s * la, b), (s, 4, 2 * la + 2, b), (s, la + 4, b)],
    )
    return grad_coarse, grad_mid, grad_fine, residual


def solution(mesh):
    placed = (
        P(None, "rad", "ang", None),
        P(None, None, "rad", "ang", None),
        P(None, None, "rad", "ang", None),
        P(),
        P(),
        P(),
        P(),
        P(),
        P(),
        P("rad", "ang", None),
        P(None, "ang", None),
        P(None, "ang", None),
    )

    def local(*args):
        return per_device(make_plan(mesh, args[0], args[10]), *args)

    return jax.shard_map(
        local,
        mesh=mesh,
        in_specs=placed,
        out_specs=(
            P(None, "rad", "ang", None),
            P(None, None, "rad", "ang", None),
            P(None, None, "rad", "ang", None),
            P(None, None, "ang", None),
        ),
        check_vma=False,
    )
```

```python
import functools
import typing

import jax
import jax.numpy as jnp
from jax import lax
from jax.experimental import pallas as pl
from jax.experimental.pallas import tpu as pltpu
from jax.sharding import PartitionSpec as P

F32 = jnp.float32
BF16 = jnp.bfloat16
VMEM_LIMIT = 24 * 1024 * 1024


class Plan(typing.NamedTuple):
    n: int
    m: int
    s: int
    la: int
    b: int
    stars: int
    w: int
    ra: int
    h: int


def make_plan(mesh, coarse, star_bins):
    n, m = mesh.shape["rad"], mesh.shape["ang"]
    s, rows, la, b = coarse.shape
    w = max(d for d in range(1, min(n, la) + 1) if la % d == 0)
    ra = la // w
    assert rows == 1 and n & (n - 1) == 0 and w % 2 == 0 and (w // 2) * ra >= 2
    return Plan(n, m, s, la, b, star_bins.shape[0], w, ra, n * s)


def eights(rows):
    return -(-rows // 8) * 8


def large_there(g):
    fine = 2 * 2 * g.ra * g.s * 16
    emit = fine + 16 * 4 * g.ra
    mix = emit + g.s * 4 * (2 * g.ra + 2)
    return fine, emit, mix, eights(mix + g.s * (g.ra + 4))


def rows_back(g):
    field = 2 * 2 * g.ra * g.s * 16
    mid = field + g.s * 4 * (2 * g.ra + 2)
    return field, mid, eights(mid + g.s * (g.ra + 4))


def prepared_rows(g):
    sizes = dict(
        stencil=24 * g.h,
        bins=16 * g.stars * g.ra,
        data=16 * g.stars * g.ra,
        mid=64,
        fine=128,
    )
    begins, at = {}, 0
    for part, size in sizes.items():
        begins[part] = at
        at += size
    return begins, at


def table_weights(table_ref, entry):
    lane = lax.broadcasted_iota(jnp.int32, table_ref.shape[1:], 1)
    columns = [
        jnp.sum(jnp.where(lane == entry, table_ref[c], 0.0), axis=1, keepdims=True) for c in range(table_ref.shape[0])
    ]
    return lambda c, j: columns[c][j : j + 1]


def start_all(pairs, sems, first=0):
    copies = [pltpu.make_async_copy(source, here, sems.at[first + i]) for i, (source, here) in enumerate(pairs)]
    for copy in copies:
        copy.start()
    return copies


def wait_all(copies):
    for copy in copies:
        copy.wait()


def pick_columns(length, ways, phase):
    src = lax.broadcasted_iota(jnp.int32, (length * ways, length), 0)
    dst = lax.broadcasted_iota(jnp.int32, (length * ways, length), 1)
    return jnp.where(src == ways * dst + phase, 1.0, 0.0).astype(BF16)


def place_columns(length, ways, phase):
    src = lax.broadcasted_iota(jnp.int32, (length, length * ways), 0)
    dst = lax.broadcasted_iota(jnp.int32, (length, length * ways), 1)
    return jnp.where(dst == ways * src + phase, 1.0, 0.0).astype(BF16)


def thirds(x):
    high = x.astype(BF16)
    rest = x - high.astype(F32)
    middle = rest.astype(BF16)
    return jnp.concatenate([high, middle, (rest - middle.astype(F32)).astype(BF16)], axis=0)


def exact_dot(parts, choice):
    sums = jnp.dot(parts, choice, preferred_element_type=F32)
    rows = sums.shape[0] // 3
    return sums[:rows] + (sums[rows : 2 * rows] + sums[2 * rows :])


def along_lanes(x, step):
    if step == 0:
        return x
    size = x.shape[1]
    lane = lax.broadcasted_iota(jnp.int32, x.shape, 1)
    edge = 0 if step > 0 else size - 1
    return jnp.where(lane == edge, 0.0, pltpu.roll(x, step % size, axis=1))


def along_rows(x, step):
    if step == 0:
        return x
    size = x.shape[0]
    row = lax.broadcasted_iota(jnp.int32, x.shape, 0)
    kept = row >= step if step > 0 else row < size + step
    return jnp.where(kept, pltpu.roll(x, step % size, axis=0), 0.0)


def prepare_kernel(g, *rest):
    sources, block, rest = rest[:8], rest[9], rest[10:]
    held, (sems, gathered) = rest[:8], rest[8:]
    copies = start_all(list(zip(sources, held)), sems)
    rows_mid, rows_fine, noise_mid, noise_fine, mid_table, fine_table, bins_ref, data_ref = held
    begins, _ = prepared_rows(g)
    me = lax.axis_index("rad")
    worker = jnp.minimum(me, g.w - 1)
    per, b = 4 * g.ra, g.b
    choices = [pick_columns(b, 4, phase) for phase in range(4)]
    wait_all(copies)
    for r in range(g.n):
        tables = [mid_table[rows_mid[r]], fine_table[rows_fine[2 * r]], fine_table[rows_fine[2 * r + 1]]]
        for level, table in enumerate(tables):
            for c in range(8):
                at = begins["stencil"] + (level * 8 + c) * g.h + r * g.s
                block[at : at + g.s, :27] = jnp.broadcast_to(table[c : c + 1], (g.s, 27))
    entries = [(begins["mid"], noise_mid, rows_mid[me])]
    entries += [(begins["fine"] + 64 * i, noise_fine, rows_fine[2 * me + i]) for i in range(2)]
    for at, table, entry in entries:
        lane = lax.broadcasted_iota(jnp.int32, table.shape[1:], 1)
        for c in range(8):
            column = jnp.sum(jnp.where(lane == entry, table[c], 0.0), axis=1, keepdims=True)
            block[at + 8 * c : at + 8 * c + 8] = jnp.broadcast_to(column, (8, b))
    for q in range(g.w):
        @pl.when(worker == q)
        def _(q=q):
            for star in range(g.stars):
                gathered[0, star * per : (star + 1) * per] = bins_ref[star, q * per : (q + 1) * per].astype(F32)
                gathered[1, star * per : (star + 1) * per] = data_ref[star, q * per : (q + 1) * per]
    bins = gathered[0].astype(BF16)
    parts = thirds(gathered[1])
    for phase in range(4):
        rows = pl.ds(begins["bins"] + phase, g.stars * per, stride=4)
        block[rows, :] = jnp.dot(bins, choices[phase], preferred_element_type=F32)
        rows = pl.ds(begins["data"] + phase, g.stars * per, stride=4)
        block[rows, :] = exact_dot(parts, choices[phase])


def scatter_kernel(g, *rest):
    sources, out_refs, rest = rest[:8], rest[8 : 8 + g.n], rest[8 + g.n :]
    held, (sems, out_sems, raw, split, lit, stage, mixed, wide) = rest[:8], rest[8:]
    light = start_all([(sources[0].at[f], held[0].at[f]) for f in range(4)], sems)
    copies = start_all(list(zip(sources[1:7], held[1:7])), sems, 4)
    spots = [(s, slice(4 * part, 4 * part + 4)) for s in range(g.s) for part in range(2)]
    copies += start_all([(sources[7].at[spot], held[7].at[spot]) for spot in spots], sems, 10)
    emission_ref, rows_mid, noise_mid, coarse_ref, excite_ref, rows_ref, noise_ref, fine_ref = held
    me = lax.axis_index("rad")
    b, s_count, la = g.b, g.s, g.la
    end_fine, end_emit, end_mix, _ = large_there(g)
    choices = [pick_columns(b, 4, phase) for phase in range(4)]
    halves = [pick_columns(b, 2, phase) for phase in range(2)]
    wait_all(light)
    parts = thirds(emission_ref[...].reshape(16 * la, 4 * b))
    for phase in range(4):
        lit[phase] = exact_dot(parts, choices[phase])
    for q in range(g.w):
        for phase in range(4):
            for f in range(4):
                at = end_fine + (phase * 4 + f) * 4 * g.ra
                rows = slice(f * 4 * la + 4 * q * g.ra, f * 4 * la + 4 * (q + 1) * g.ra)
                stage[q, at : at + 4 * g.ra] = lit[phase, rows]
    wait_all(copies[:4])
    weight = table_weights(noise_mid, rows_mid[me])
    for c in range(8):
        for s in range(s_count):
            total = weight(c, 0) * excite_ref[s, 0, 0]
            for j in range(1, 8):
                total = total + weight(c, j) * excite_ref[s, j, 0]
            mixed[s, c] = total
    for s in range(s_count):
        wide[s, :2] = coarse_ref[s, 0, la - 2 :]
        wide[s, 2 : 2 + la] = coarse_ref[s, 0]
        wide[s, 2 + la :] = coarse_ref[s, 0, :2]
    for q in range(g.w):
        for s in range(s_count):
            for row in range(2 * g.ra + 2):
                a, ca = divmod((2 * q * g.ra - 1 + row) % (2 * la), 2)
                for cr in range(2):
                    for cb in range(2):
                        at = end_emit + ((s * (2 * g.ra + 2) + row) * 2 + cr) * 2 + cb
                        stage[q, at : at + 1] = mixed[s, 4 * cr + 2 * ca + cb, a : a + 1]
            at = end_mix + (g.ra + 4) * s
            stage[q, at : at + g.ra + 4] = wide[s, q * g.ra : q * g.ra + g.ra + 4]
    workers = [jnp.minimum(lax.rem(me + k, g.n), g.w - 1) for k in range(g.n)]
    done = [(stage.at[worker, end_fine:], out.at[end_fine:]) for worker, out in zip(workers, out_refs)]
    done = start_all(done, out_sems)
    wait_all(copies[4:])
    for i in range(2):
        weight = table_weights(noise_ref, rows_ref[2 * me + i])
        for c in range(8):
            weights = [weight(c, j) for j in range(8)]
            for s in range(s_count):
                total = weights[0] * fine_ref[s, 0, i]
                for j in range(1, 8):
                    total = total + weights[j] * fine_ref[s, j, i]
                at = ((s * 8 + c) * 2 + i) * 2 * la
                raw[at : at + 2 * la] = total
    parts = thirds(raw[...])
    for phase in range(2):
        split[phase] = exact_dot(parts, halves[phase])
    for q in range(g.w):
        for phase in range(2):
            for a in range(2 * g.ra):
                for s in range(s_count):
                    at = ((phase * 2 * g.ra + a) * s_count + s) * 16
                    rows = pl.ds(s * 32 * la + 2 * q * g.ra + a, 16, stride=2 * la)
                    stage[q, at : at + 16] = split[phase, rows, :]
    last = [(stage.at[worker, :end_fine], out.at[:end_fine]) for worker, out in zip(workers, out_refs)]
    wait_all(done + start_all(last, out_sems, g.n))


def relay_kernel(g, *rest):
    in_refs, (edge_out,) = rest[: g.n], rest[g.n :]
    me = lax.axis_index("rad")
    low = jnp.minimum(me, g.w - 1) < g.w // 2
    _, end_emit, end_mix, _ = large_there(g)
    rows_a = 2 * g.ra + 2
    for k in range(g.n):
        source = lax.rem(me + g.n - k, g.n)
        for s in range(g.s):
            sub = source * g.s + s
            mid = end_emit + s * 4 * rows_a
            coarse = end_mix + (g.ra + 4) * s
            end_mid, end_coarse = mid + 4 * rows_a, coarse + g.ra + 4
            value = jnp.where(low, in_refs[k][mid : mid + 4], in_refs[k][end_mid - 4 : end_mid])
            edge_out[pl.ds(sub, 4, stride=g.h), :] = value
            value = jnp.where(low, in_refs[k][coarse : coarse + 2], in_refs[k][end_coarse - 2 : end_coarse])
            edge_out[pl.ds(4 * g.h + sub, 2, stride=g.h), :] = value


def outside(g, q):
    low = q < g.w // 2
    rows = [(a, q * g.ra - 2 + a) for a in range(g.ra + 4)]
    return [(a, a if low else a - g.ra - 2) for a, row in rows if row < 0 or row >= g.la]


def unpack_kernel(g, *rest):
    in_refs, (fine_out, emit_out, mix_out, coarse_out) = rest[: g.n], rest[g.n :]
    me = lax.axis_index("rad")
    end_fine, end_emit, end_mix, _ = large_there(g)
    h, ra, rows_a = g.h, g.ra, 2 * g.ra + 2
    for k in range(g.n):
        source = lax.rem(me + g.n - k, g.n)
        got = in_refs[k]
        for s in range(g.s):
            sub = source * g.s + s
            for x in range(4 * ra):
                at = (x * g.s + s) * 16
                fine_out[pl.ds(x * 16 * h + sub, 16, stride=h), :] = got[at : at + 16]
            emit_out[pl.ds(sub, 64 * ra, stride=h), :] = got[end_fine:end_emit]
            at = end_emit + s * 4 * rows_a
            mix_out[pl.ds(sub, 4 * rows_a, stride=h), :] = got[at : at + 4 * rows_a]
            at = end_mix + (ra + 4) * s
            coarse_out[pl.ds(sub, ra + 4, stride=h), :] = got[at : at + ra + 4]


def weight_kernel(g, block, own, spread, own_out, block_out):
    own_out[...] = own[...]
    block_out[...] = block[...]
    begins, _ = prepared_rows(g)
    for x in range(24):
        at = begins["stencil"] + x * g.h
        tile = block[at : at + g.h]
        for o in range(27):
            spread[x * 27 + o] = jnp.broadcast_to(tile[:, o : o + 1], (g.h, g.b))


def edges_inside(g, worker):
    first = lax.axis_index("ang") * g.la + worker * g.ra
    inside = jnp.where(first > 0, 1.0, 0.0), jnp.where(first + g.ra < g.m * g.la, 1.0, 0.0)
    return [x.astype(F32) for x in inside]


def cell_rows_of(g, a, c, pr):
    return pl.ds(pl.multiple_of(((a * 8 + c) * 2 + pr) * g.h, 8), g.h)


def forward_kernel(g, block, spread, *rest):
    n, b, s_count, ra, h = g.n, g.b, g.s, g.ra, g.h
    fine_in, emit_in, mixed, coarse, near = rest[:5]
    cells, resid_out = rest[5:7]
    mix_in, coarse_in, coarse_ext, mid_ext, seen = rest[7:]
    me, ang = lax.axis_index("rad"), lax.axis_index("ang")
    rows_a = 2 * ra + 2
    spacing = 1.0 / (4 * n)
    worker = jnp.minimum(me, g.w - 1)
    begins, _ = prepared_rows(g)

    def weight_at(level, c, o):
        return spread[(level * 8 + c) * 27 + o]

    mix_in[...] = mixed[...]
    coarse_in[...] = coarse[...]
    live = jnp.where(worker < g.w // 2, ang > 0, ang < g.m - 1)
    for q in range(g.w):
        @pl.when(worker == q)
        def _(q=q):
            if q == 0:
                mix_in[: 4 * h] = jnp.where(live, near[: 4 * h], 0.0)
            if q == g.w - 1:
                mix_in[4 * (rows_a - 1) * h :] = jnp.where(live, near[: 4 * h], 0.0)
            for a, place in outside(g, q):
                at = (4 + place) * h
                coarse_in[a * h : (a + 1) * h] = jnp.where(live, near[at : at + h], 0.0)

    top_in, bottom_in = edges_inside(g, worker)
    for a in range(ra + 4):
        x = coarse_in[a * h : (a + 1) * h]
        for db in range(3):
            shifted = along_lanes(x, 1 - db)
            for dr in range(3):
                coarse_ext[dr, a, db] = along_rows(shifted, (1 - dr) * s_count)
    for c in range(8):
        cr, ca, cb = c // 4, c // 2 % 2, c % 2
        weight = [weight_at(0, c, o) for o in range(27)]
        for row in range(1 - ca, rows_a, 2):
            a = (row - 1) // 2
            at = (row * 4 + 2 * cr + cb) * h
            total = mix_in[at : at + h]
            for dr in range(3):
                for da in range(3):
                    for db in range(3):
                        total = total + weight[9 * dr + 3 * da + db] * coarse_ext[dr, a + 1 + da, db]
            if row == 0:
                total = total * top_in
            if row == rows_a - 1:
                total = total * bottom_in
            for bi, step_b in ((1 + cb, 0), (3, -1) if cb == 0 else (0, 1)):
                shifted = along_lanes(total, step_b)
                for ri, step_r in ((1 + cr, 0), (3, -1) if cr == 0 else (0, 1)):
                    mid_ext[ri, row, bi] = along_rows(shifted, step_r * s_count)

    cell_rows = functools.partial(cell_rows_of, g)

    def fine_cells(c, carry):
        for pr in range(2):
            weight = [weight_at(1 + pr, c, o) for o in range(27)]
            for a in range(2 * ra):
                for pb in range(2):
                    at = (((pb * 2 * ra + a) * 8 + c) * 2 + pr) * h
                    total = fine_in[pl.ds(pl.multiple_of(at, 8), h), :]
                    for dr in range(3):
                        for da in range(3):
                            for db in range(3):
                                o = 9 * dr + 3 * da + db
                                total = total + weight[o] * mid_ext[pr + dr, a + da, pb + db]
                    cells[pb, cell_rows(a, c, pr), :] = total
        return carry

    lax.fori_loop(0, 8, fine_cells, 0)

    radial = (4 * (lax.broadcasted_iota(jnp.int32, (h, b), 0) // s_count)).astype(F32)

    def sum_before(x):
        step = s_count
        while step < h:
            x = x + along_rows(x, step)
            step *= 2
        return along_rows(x, s_count)

    def sum_all(x):
        step = s_count
        while step < h:
            x = x + pltpu.roll(x, step, axis=0)
            step *= 2
        return x

    def positions(at, carry):
        a, half = at // 2, lax.rem(at, 2)
        spots = []
        for cb in range(2):
            pb = 2 * half + cb
            rows = [cell_rows(a // 2, 4 * (f % 2) + 2 * lax.rem(a, 2) + cb, f // 2) for f in range(4)]
            emit = [pl.multiple_of(((pb * 4 + f) * 4 * ra + a) * h, 8) for f in range(4)]
            stars = [(star * 4 * ra + a) * 4 + pb for star in range(g.stars)]
            spots.append((pb, rows, emit, stars))
        density = [[jnp.exp(cells[half, rows[f], :]) for f in range(4)] for _, rows, _, _ in spots]
        glow = [[spacing * emit_in[pl.ds(emit[f], h), :] for f in range(4)] for _, _, emit, _ in spots]
        bins = [[block[pl.ds(begins["bins"] + row, 1), :] for row in stars] for _, _, _, stars in spots]
        data = [[block[pl.ds(begins["data"] + row, 1), :] for row in stars] for _, _, _, stars in spots]
        column = []
        for d, light in zip(density, glow):
            layer = [spacing * x for x in d]
            depth = sum_before(layer[0] + layer[1] + layer[2] + layer[3])
            for f in range(4):
                light[f] = light[f] * jnp.exp(-depth)
                depth = depth + layer[f]
            running = sum_before(light[0] + light[1] + light[2] + light[3])
            column.append([])
            for f in range(4):
                running = running + light[f]
                column[-1].append(running)
        total = [[jnp.zeros((h, b), F32) for f in range(4)] for _ in spots]
        seen_at = []
        for star in range(g.stars):
            for x, (pb, _, _, _) in enumerate(spots):
                bin_here = jnp.broadcast_to(bins[x][star], (h, b)) - radial
                mine = jnp.where(bin_here == 0, column[x][0], 0.0)
                for f in range(1, 4):
                    mine = jnp.where(bin_here == f, column[x][f], mine)
                predicted = sum_all(mine)
                residual = jnp.broadcast_to(data[x][star], (h, b)) - predicted
                seen_at.append((pb, star, residual))
                for f in range(4):
                    term = residual * (predicted - column[x][f])
                    total[x][f] = total[x][f] + jnp.where(bin_here > f, term, 0.0)
        for pb, star, residual in seen_at:
            for s in range(s_count):
                seen[pb, pl.ds((s * g.stars + star) * 4 * ra + a, 1), :] = residual[s : s + 1]
        for x, (_, rows, _, _) in enumerate(spots):
            for f in range(4):
                cells[half, rows[f], :] = -density[x][f] * total[x][f]
        return carry

    lax.fori_loop(0, 8 * ra, positions, 0)

    shown = None
    for phase in range(4):
        value = exact_dot(thirds(seen[phase]), place_columns(b, 4, phase))
        shown = value if shown is None else shown + value
    per = 4 * g.stars * ra * s_count
    for part in range(4):
        resid_out[part * per : (part + 1) * per] = shown[:, part * b : (part + 1) * b]


def backward_kernel(g, spread, cells, parent, coarse_sum, edge_sum, tall):
    n, b, s_count, ra, h = g.n, g.b, g.s, g.ra, g.h
    rows_a = 2 * ra + 2
    worker = jnp.minimum(lax.axis_index("rad"), g.w - 1)
    top_in, bottom_in = edges_inside(g, worker)
    cell_rows = functools.partial(cell_rows_of, g)

    def weight_at(level, c, o):
        return spread[(level * 8 + c) * 27 + o]

    tall[...] = jnp.zeros(tall.shape, F32)
    for pr in range(2):
        def gather(c, carry, pr=pr):
            values = {(a, pb): cells[pb, cell_rows(a, c, pr), :] for a in range(2 * ra) for pb in range(2)}
            for dr in range(3):
                sums = {}
                for da in range(3):
                    for db in range(3):
                        weight = weight_at(1 + pr, c, 9 * dr + 3 * da + db)
                        for (a, pb), value in values.items():
                            key = (a + da, pb + db)
                            term = weight * value
                            sums[key] = sums[key] + term if key in sums else term
                for (row, bi), value in sums.items():
                    tall[pr + dr, row, bi] += value
            return carry

        lax.fori_loop(0, 8, gather, 0)
    for row in range(rows_a):
        for pr in range(2):
            for pb in range(2):
                bi, step_b = (3, 1) if pb == 0 else (0, -1)
                ri, step_r = (3, 1) if pr == 0 else (0, -1)
                close = tall[1 + pr, row, 1 + pb] + along_lanes(tall[1 + pr, row, bi], step_b)
                far = tall[ri, row, 1 + pb] + along_lanes(tall[ri, row, bi], step_b)
                value = close + along_rows(far, step_r * s_count)
                if row == 0:
                    value = value * top_in
                if row == rows_a - 1:
                    value = value * bottom_in
                at = ((2 * pr + pb) * rows_a + row) * h
                parent[at : at + h] = value

    coarse_sum[...] = jnp.zeros(coarse_sum.shape, F32)
    for dr in range(3):
        for db in range(3):
            sums = {}
            for c in range(8):
                cr, ca, cb = c // 4, c // 2 % 2, c % 2
                for da in range(3):
                    weight = weight_at(0, c, 9 * dr + 3 * da + db)
                    for row in range(1 - ca, rows_a, 2):
                        at = ((2 * cr + cb) * rows_a + row) * h
                        term = weight * parent[at : at + h]
                        key = (row - 1) // 2 + 1 + da
                        sums[key] = sums[key] + term if key in sums else term
            for a, value in sums.items():
                coarse_sum[a * h : (a + 1) * h] += along_lanes(along_rows(value, (dr - 1) * s_count), db - 1)

    low = worker < g.w // 2
    for x in range(4):
        at, end = x * rows_a * h, (x + 1) * rows_a * h
        edge_sum[x * h : (x + 1) * h] = jnp.where(low, parent[at : at + h], parent[end - h : end])
    edge_sum[4 * h :] = jnp.where(low, coarse_sum[: 2 * h], coarse_sum[(ra + 2) * h :])


def lanes_kernel(g, cells, out, joined):
    n, b, s_count, ra, h = g.n, g.b, g.s, g.ra, g.h
    parts = [thirds(cells[phase]) for phase in range(2)]
    order = [place_columns(b, 2, phase) for phase in range(2)]
    for half in range(2):
        lanes = slice(half * b, (half + 1) * b)
        joined[half] = exact_dot(parts[0], order[0][:, lanes]) + exact_dot(parts[1], order[1][:, lanes])
    for r in range(n):
        for s in range(s_count):
            for half in range(2):
                for a in range(2 * ra):
                    at = ((half * 2 * ra + a) * s_count + s) * 16
                    out[r, at : at + 16] = joined[half, pl.ds(a * 16 * h + r * s_count + s, 16, stride=h), :]


def sums_kernel(g, field, parent_ref, coarse_ref, edge_ref, *rest):
    out_refs, (stage, parent, coarse_sum) = rest[: g.n], rest[g.n :]
    me, ang = lax.axis_index("rad"), lax.axis_index("ang")
    n, s_count, ra, h = g.n, g.s, g.ra, g.h
    rows_a = 2 * ra + 2
    worker = jnp.minimum(me, g.w - 1)
    live = jnp.where(worker < g.w // 2, ang < g.m - 1, ang > 0)
    end_field, end_mid, end = rows_back(g)
    parent[...] = parent_ref[...]
    coarse_sum[...] = coarse_ref[...]
    for q in range(g.w):
        @pl.when(worker == q)
        def _(q=q):
            if q == 0 or q == g.w - 1:
                for x in range(4):
                    at = (x * rows_a + (0 if q == 0 else rows_a - 1)) * h
                    parent[at : at + h] = jnp.where(live, edge_ref[x * h : (x + 1) * h], 0.0)
            for a, place in outside(g, q):
                at = (4 + place) * h
                coarse_sum[a * h : (a + 1) * h] = jnp.where(live, edge_ref[at : at + h], 0.0)
    for r in range(n):
        for s in range(s_count):
            sub = r * s_count + s
            at = s * 4 * rows_a
            stage[r, at : at + 4 * rows_a] = parent[pl.ds(sub, 4 * rows_a, stride=h), :]
            at = end_mid - end_field + (ra + 4) * s
            stage[r, at : at + ra + 4] = coarse_sum[pl.ds(sub, ra + 4, stride=h), :]
    for k in range(n):
        owner = lax.rem(me + k, n)
        out_refs[k][:end_field] = field[owner]
        out_refs[k][end_field:end] = stage[owner]


def join_kernel(g, one, two, after, out):
    rows = one.shape[0]
    out[:rows] = one[...]
    out[rows:] = two[...]


def resid_owner_kernel(g, ids, block, *rest):
    in_refs, (resid_out, mixes, shown) = rest[:-3], rest[-3:]
    me = lax.axis_index("rad")
    b, s_count, ra = g.b, g.s, g.ra
    begins, end = prepared_rows(g)
    per = 4 * g.stars * ra
    mixes[...] = block[begins["mid"] : end]
    for ref, held_ids in zip(in_refs, ids):
        for at, i in enumerate(held_ids):
            shown[me ^ i] = ref[at * 4 * s_count * per : (at + 1) * 4 * s_count * per]
    for q in range(g.w):
        for s in range(s_count):
            for part in range(4):
                for star in range(g.stars):
                    at = (part * s_count + s) * per + star * 4 * ra
                    rows = slice(4 * q * ra, 4 * (q + 1) * ra)
                    resid_out[s, star, rows, part * b : (part + 1) * b] = shown[q, at : at + 4 * ra]


def owner_kernel(g, mixes, *rest):
    in_refs, (coarse_out, mid_out, fine_out, got, fine, grad_mid, grad_coarse) = rest[: g.n], rest[g.n :]
    me = lax.axis_index("rad")
    n, b, s_count, ra, la = g.n, g.b, g.s, g.ra, g.la
    rows_a = 2 * ra + 2
    end_field, end_mid, _ = rows_back(g)
    for k in range(n):
        got[lax.rem(me + n - k, n)] = in_refs[k][...]
    grad_mid[...] = jnp.zeros(grad_mid.shape, F32)
    grad_coarse[...] = jnp.zeros(grad_coarse.shape, F32)
    for q in range(g.w):
        for s in range(s_count):
            for half in range(2):
                for a in range(2 * ra):
                    at = ((half * 2 * ra + a) * s_count + s) * 16
                    rows = pl.ds(s * 32 * la + 2 * q * ra + a, 16, stride=2 * la)
                    fine[half, rows, :] = got[q, at : at + 16]
            for x in range(4):
                at = end_field + s * 4 * rows_a + x * rows_a
                grad_mid[s, x, 2 * q * ra : 2 * q * ra + rows_a] += got[q, at : at + rows_a]
            at = end_mid + (ra + 4) * s
            grad_coarse[s, q * ra : q * ra + ra + 4] += got[q, at : at + ra + 4]
    for s in range(s_count):
        for x in range(4):
            grad_mid[s, x, 1:2] += grad_mid[s, x, 2 * la + 1 :]
            grad_mid[s, x, 2 * la : 2 * la + 1] += grad_mid[s, x, :1]
        grad_coarse[s, 2:4] += grad_coarse[s, la + 2 :]
        grad_coarse[s, la : la + 2] += grad_coarse[s, :2]
    for i in range(2):
        for j in range(8):
            rows = [64 + 64 * i + 8 * c + j for c in range(8)]
            weight = [mixes[row : row + 1] for row in rows]
            for s in range(s_count):
                for half in range(2):
                    total = None
                    for c in range(8):
                        at = ((s * 8 + c) * 2 + i) * 2 * la
                        term = weight[c] * fine[half, at : at + 2 * la]
                        total = term if total is None else total + term
                    fine_out[s, j, i, :, half * b : (half + 1) * b] = total
    for s in range(s_count):
        coarse_out[s, 0] = grad_coarse[s, 2 : 2 + la]
        cells = []
        for c in range(8):
            cr, ca, cb = c // 4, c // 2 % 2, c % 2
            cells.append(grad_mid[s, 2 * cr + cb, pl.ds(1 + ca, la, stride=2), :])
        for j in range(8):
            total = mixes[j : j + 1] * cells[0]
            for c in range(1, 8):
                total = total + mixes[j + 8 * c : j + 8 * c + 1] * cells[c]
            mid_out[s, j, 0] = total


def held(arrays):
    return [(pltpu.SMEM if len(x.shape) == 1 else pltpu.VMEM)(x.shape, x.dtype) for x in arrays]


def call(kernel, name, outs, operands, scratch, unmoved=0, written=0):
    vmem = pl.BlockSpec(memory_space=pltpu.VMEM)
    placed = pl.BlockSpec(memory_space=pl.ANY)
    limit = None if unmoved else VMEM_LIMIT
    return pl.pallas_call(
        kernel,
        name=name,
        out_shape=[jax.ShapeDtypeStruct(shape, kind) for shape, kind in outs],
        in_specs=[placed] * unmoved + [vmem] * (len(operands) - unmoved),
        out_specs=[placed] * written + [vmem] * (len(outs) - written),
        scratch_shapes=[pltpu.VMEM(shape, F32) if isinstance(shape, tuple) else shape for shape in scratch],
        compiler_params=pltpu.CompilerParams(vmem_limit_bytes=limit),
    )(*operands)


def per_device(
    g,
    coarse_field,
    excite_mid,
    excite_fine,
    kernels_mid,
    noise_mid,
    rows_mid,
    kernels_fine,
    noise_fine,
    rows_fine,
    emission,
    star_bins,
    star_data,
):
    n, m, s, la, b, stars, w, ra, h = g
    kernel = functools.partial
    rows_a = 2 * ra + 2
    workers = [(r, a, 1 if min(r, w - 1) < w // 2 else -1) for r in range(n) for a in range(m)]
    sideways = [(r * m + a, r * m + (a - step) % m) for r, a, step in workers]
    inward = [(to, at) for at, to in sideways]

    def exchange(blocks):
        return [blocks[0]] + [lax.ppermute(blocks[k], "rad", [(i, (i + k) % n) for i in range(n)]) for k in range(1, n)]

    noise_mid, noise_fine = noise_mid.transpose(1, 2, 0), noise_fine.transpose(1, 2, 0)
    large = (large_there(g)[-1], b)
    operands = (emission, rows_mid, noise_mid, coarse_field, excite_mid, rows_fine, noise_fine, excite_fine)
    sent = call(
        kernel(scatter_kernel, g),
        "scatter",
        [(large, F32)] * n,
        operands,
        [
            *held(operands),
            pltpu.SemaphoreType.DMA((10 + 2 * s,)),
            pltpu.SemaphoreType.DMA((2 * n,)),
            (32 * s * la, 2 * b),
            (2, 32 * s * la, b),
            (4, 16 * la, b),
            (w, *large),
            (s, 8, la, b),
            (s, la + 4, b),
        ],
        unmoved=8,
        written=n,
    )
    got = exchange(sent)
    operands = (rows_mid, rows_fine, noise_mid, noise_fine, kernels_mid, kernels_fine, star_bins, star_data)
    (block,) = call(
        kernel(prepare_kernel, g),
        "prepare",
        [((prepared_rows(g)[1], b), F32)],
        (*operands, sent[0]),
        [*held(operands), pltpu.SemaphoreType.DMA((8,)), (2, 4 * stars * ra, 4 * b)],
        unmoved=9,
    )
    spread, got[0], block = call(
        kernel(weight_kernel, g),
        "weights",
        [((24 * 27, h, b), F32), (large, F32), (block.shape, F32)],
        (block, sent[0]),
        [],
    )
    (near,) = call(kernel(relay_kernel, g), "relay", [((6 * h, b), F32)], got, [])
    near = lax.ppermute(near, ("rad", "ang"), inward)
    parts = [(64 * ra * h, b), (64 * ra * h, b), (4 * rows_a * h, b), ((ra + 4) * h, b)]
    unpacked = call(kernel(unpack_kernel, g), "unpack", [(part, F32) for part in parts], got, [])
    def everywhere(block, after):
        ids, bit = [0], n // 2
        while True:
            got = lax.ppermute(block, "rad", [(i, i ^ bit) for i in range(n)])
            more = [i ^ bit for i in ids]
            if bit == 1:
                return (block, got), (ids, more)
            shape = (2 * block.shape[0], b)
            (block,) = call(kernel(join_kernel, g), "join", [(shape, F32)], (block, got, after), [])
            ids, bit = ids + more, bit // 2

    end_field, _, end = rows_back(g)
    resid_rows = 16 * stars * ra * s
    cells, shown = call(
        kernel(forward_kernel, g),
        "forward",
        [((2, 32 * ra * h, b), F32), ((resid_rows, b), F32)],
        (block, spread, *unpacked, near),
        [
            (4 * rows_a * h, b),
            ((ra + 4) * h, b),
            (3, ra + 4, 3, h, b),
            (4, rows_a, 4, h, b),
            (4, 4 * stars * ra * s, b),
        ],
    )
    parent, coarse_sum, edge = call(
        kernel(backward_kernel, g),
        "backward",
        [((4 * rows_a * h, b), F32), (((ra + 4) * h, b), F32), ((6 * h, b), F32)],
        (spread, cells),
        [(4, rows_a, 4, h, b)],
    )
    edge = lax.ppermute(edge, ("rad", "ang"), sideways)
    (field,) = call(
        kernel(lanes_kernel, g), "lanes", [((n, end_field, b), F32)], (cells,), [(2, 32 * ra * h, b)]
    )
    got = exchange(
        call(
            kernel(sums_kernel, g),
            "sums",
            [((end, b), F32)] * n,
            (field, parent, coarse_sum, edge),
            [(n, end - end_field, b), parent.shape, coarse_sum.shape],
        )
    )
    shown, ids = everywhere(shown, got[0])
    residual, mixes = call(
        kernel(resid_owner_kernel, g, ids),
        "resid_owner",
        [((s, stars, 4 * la, 4 * b), F32), ((192, b), F32)],
        (block, *shown),
        [(n, resid_rows, b)],
    )
    grad_coarse, grad_mid, grad_fine = call(
        kernel(owner_kernel, g),
        "owner",
        [((s, 1, la, b), F32), ((s, 8, 1, la, b), F32), ((s, 8, 2, 2 * la, 2 * b), F32)],
        (mixes, *got),
        [(n, end, b), (2, 32 * s * la, b), (s, 4, 2 * la + 2, b), (s, la + 4, b)],
    )
    return grad_coarse, grad_mid, grad_fine, residual


def solution(mesh):
    placed = (
        P(None, "rad", "ang", None),
        P(None, None, "rad", "ang", None),
        P(None, None, "rad", "ang", None),
        P(),
        P(),
        P(),
        P(),
        P(),
        P(),
        P("rad", "ang", None),
        P(None, "ang", None),
        P(None, "ang", None),
    )

    def local(*args):
        return per_device(make_plan(mesh, args[0], args[10]), *args)

    return jax.shard_map(
        local,
        mesh=mesh,
        in_specs=placed,
        out_specs=(
            P(None, "rad", "ang", None),
            P(None, None, "rad", "ang", None),
            P(None, None, "rad", "ang", None),
            P(None, None, "ang", None),
        ),
        check_vma=False,
    )
```

```python
import functools
import typing

import jax
import jax.numpy as jnp
from jax import lax
from jax.experimental import pallas as pl
from jax.experimental.pallas import tpu as pltpu
from jax.sharding import PartitionSpec as P

F32 = jnp.float32
BF16 = jnp.bfloat16
VMEM_LIMIT = 24 * 1024 * 1024


class Plan(typing.NamedTuple):
    n: int
    m: int
    s: int
    la: int
    b: int
    stars: int
    w: int
    ra: int
    h: int


def make_plan(mesh, coarse, star_bins):
    n, m = mesh.shape["rad"], mesh.shape["ang"]
    s, rows, la, b = coarse.shape
    w = max(d for d in range(1, min(n, la) + 1) if la % d == 0)
    ra = la // w
    assert rows == 1 and n & (n - 1) == 0 and w % 2 == 0 and (w // 2) * ra >= 2
    return Plan(n, m, s, la, b, star_bins.shape[0], w, ra, n * s)


def eights(rows):
    return -(-rows // 8) * 8


def large_there(g):
    fine = 2 * 2 * g.ra * g.s * 16
    emit = fine + 16 * 4 * g.ra
    mix = emit + g.s * 4 * (2 * g.ra + 2)
    return fine, emit, mix, eights(mix + g.s * (g.ra + 4))


def rows_back(g):
    field = 2 * 2 * g.ra * g.s * 16
    mid = field + g.s * 4 * (2 * g.ra + 2)
    return field, mid, eights(mid + g.s * (g.ra + 4))


def prepared_rows(g):
    sizes = dict(
        stencil=24 * g.h,
        bins=16 * g.stars * g.ra,
        data=16 * g.stars * g.ra,
        mid=64,
        fine=128,
    )
    begins, at = {}, 0
    for part, size in sizes.items():
        begins[part] = at
        at += size
    return begins, at


def table_weights(table_ref, entry):
    lane = lax.broadcasted_iota(jnp.int32, table_ref.shape[1:], 1)
    columns = [
        jnp.sum(jnp.where(lane == entry, table_ref[c], 0.0), axis=1, keepdims=True) for c in range(table_ref.shape[0])
    ]
    return lambda c, j: columns[c][j : j + 1]


def start_all(pairs, sems, first=0):
    copies = [pltpu.make_async_copy(source, here, sems.at[first + i]) for i, (source, here) in enumerate(pairs)]
    for copy in copies:
        copy.start()
    return copies


def wait_all(copies):
    for copy in copies:
        copy.wait()


def pick_columns(length, ways, phase):
    src = lax.broadcasted_iota(jnp.int32, (length * ways, length), 0)
    dst = lax.broadcasted_iota(jnp.int32, (length * ways, length), 1)
    return jnp.where(src == ways * dst + phase, 1.0, 0.0).astype(BF16)


def place_columns(length, ways, phase):
    src = lax.broadcasted_iota(jnp.int32, (length, length * ways), 0)
    dst = lax.broadcasted_iota(jnp.int32, (length, length * ways), 1)
    return jnp.where(dst == ways * src + phase, 1.0, 0.0).astype(BF16)


def thirds(x):
    high = x.astype(BF16)
    rest = x - high.astype(F32)
    middle = rest.astype(BF16)
    return jnp.concatenate([high, middle, (rest - middle.astype(F32)).astype(BF16)], axis=0)


def exact_dot(parts, choice):
    sums = jnp.dot(parts, choice, preferred_element_type=F32)
    rows = sums.shape[0] // 3
    return sums[:rows] + (sums[rows : 2 * rows] + sums[2 * rows :])


def along_lanes(x, step):
    if step == 0:
        return x
    size = x.shape[1]
    lane = lax.broadcasted_iota(jnp.int32, x.shape, 1)
    edge = 0 if step > 0 else size - 1
    return jnp.where(lane == edge, 0.0, pltpu.roll(x, step % size, axis=1))


def along_rows(x, step):
    if step == 0:
        return x
    size = x.shape[0]
    row = lax.broadcasted_iota(jnp.int32, x.shape, 0)
    kept = row >= step if step > 0 else row < size + step
    return jnp.where(kept, pltpu.roll(x, step % size, axis=0), 0.0)


def prepare_kernel(g, *rest):
    sources, block, rest = rest[:8], rest[9], rest[10:]
    held, (sems, gathered) = rest[:8], rest[8:]
    copies = start_all(list(zip(sources, held)), sems)
    rows_mid, rows_fine, noise_mid, noise_fine, mid_table, fine_table, bins_ref, data_ref = held
    begins, _ = prepared_rows(g)
    me = lax.axis_index("rad")
    worker = jnp.minimum(me, g.w - 1)
    per, b = 4 * g.ra, g.b
    choices = [pick_columns(b, 4, phase) for phase in range(4)]
    wait_all(copies)
    for r in range(g.n):
        tables = [mid_table[rows_mid[r]], fine_table[rows_fine[2 * r]], fine_table[rows_fine[2 * r + 1]]]
        for level, table in enumerate(tables):
            for c in range(8):
                at = begins["stencil"] + (level * 8 + c) * g.h + r * g.s
                block[at : at + g.s, :27] = jnp.broadcast_to(table[c : c + 1], (g.s, 27))
    entries = [(begins["mid"], noise_mid, rows_mid[me])]
    entries += [(begins["fine"] + 64 * i, noise_fine, rows_fine[2 * me + i]) for i in range(2)]
    for at, table, entry in entries:
        lane = lax.broadcasted_iota(jnp.int32, table.shape[1:], 1)
        for c in range(8):
            column = jnp.sum(jnp.where(lane == entry, table[c], 0.0), axis=1, keepdims=True)
            block[at + 8 * c : at + 8 * c + 8] = jnp.broadcast_to(column, (8, b))
    for q in range(g.w):
        @pl.when(worker == q)
        def _(q=q):
            for star in range(g.stars):
                gathered[0, star * per : (star + 1) * per] = bins_ref[star, q * per : (q + 1) * per].astype(F32)
                gathered[1, star * per : (star + 1) * per] = data_ref[star, q * per : (q + 1) * per]
    bins = gathered[0].astype(BF16)
    parts = thirds(gathered[1])
    for phase in range(4):
        rows = pl.ds(begins["bins"] + phase, g.stars * per, stride=4)
        block[rows, :] = jnp.dot(bins, choices[phase], preferred_element_type=F32)
        rows = pl.ds(begins["data"] + phase, g.stars * per, stride=4)
        block[rows, :] = exact_dot(parts, choices[phase])


def scatter_kernel(g, *rest):
    sources, out_refs, rest = rest[:8], rest[8 : 8 + g.n], rest[8 + g.n :]
    held, (sems, out_sems, raw, split, lit, stage, mixed, wide) = rest[:8], rest[8:]
    light = start_all([(sources[0].at[f], held[0].at[f]) for f in range(4)], sems)
    copies = start_all(list(zip(sources[1:7], held[1:7])), sems, 4)
    spots = [(s, slice(4 * part, 4 * part + 4)) for s in range(g.s) for part in range(2)]
    copies += start_all([(sources[7].at[spot], held[7].at[spot]) for spot in spots], sems, 10)
    emission_ref, rows_mid, noise_mid, coarse_ref, excite_ref, rows_ref, noise_ref, fine_ref = held
    me = lax.axis_index("rad")
    b, s_count, la = g.b, g.s, g.la
    end_fine, end_emit, end_mix, _ = large_there(g)
    choices = [pick_columns(b, 4, phase) for phase in range(4)]
    halves = [pick_columns(b, 2, phase) for phase in range(2)]
    wait_all(light)
    parts = thirds(emission_ref[...].reshape(16 * la, 4 * b))
    for phase in range(4):
        lit[phase] = exact_dot(parts, choices[phase])
    for q in range(g.w):
        for phase in range(4):
            for f in range(4):
                at = end_fine + (phase * 4 + f) * 4 * g.ra
                rows = slice(f * 4 * la + 4 * q * g.ra, f * 4 * la + 4 * (q + 1) * g.ra)
                stage[q, at : at + 4 * g.ra] = lit[phase, rows]
    wait_all(copies[:4])
    weight = table_weights(noise_mid, rows_mid[me])
    for c in range(8):
        for s in range(s_count):
            total = weight(c, 0) * excite_ref[s, 0, 0]
            for j in range(1, 8):
                total = total + weight(c, j) * excite_ref[s, j, 0]
            mixed[s, c] = total
    for s in range(s_count):
        wide[s, :2] = coarse_ref[s, 0, la - 2 :]
        wide[s, 2 : 2 + la] = coarse_ref[s, 0]
        wide[s, 2 + la :] = coarse_ref[s, 0, :2]
    for q in range(g.w):
        for s in range(s_count):
            for row in range(2 * g.ra + 2):
                a, ca = divmod((2 * q * g.ra - 1 + row) % (2 * la), 2)
                for cr in range(2):
                    for cb in range(2):
                        at = end_emit + ((s * (2 * g.ra + 2) + row) * 2 + cr) * 2 + cb
                        stage[q, at : at + 1] = mixed[s, 4 * cr + 2 * ca + cb, a : a + 1]
            at = end_mix + (g.ra + 4) * s
            stage[q, at : at + g.ra + 4] = wide[s, q * g.ra : q * g.ra + g.ra + 4]
    workers = [jnp.minimum(lax.rem(me + k, g.n), g.w - 1) for k in range(g.n)]
    done = [(stage.at[worker, end_fine:], out.at[end_fine:]) for worker, out in zip(workers, out_refs)]
    done = start_all(done, out_sems)
    wait_all(copies[4:])
    for i in range(2):
        weight = table_weights(noise_ref, rows_ref[2 * me + i])
        for c in range(8):
            weights = [weight(c, j) for j in range(8)]
            for s in range(s_count):
                total = weights[0] * fine_ref[s, 0, i]
                for j in range(1, 8):
                    total = total + weights[j] * fine_ref[s, j, i]
                at = ((s * 8 + c) * 2 + i) * 2 * la
                raw[at : at + 2 * la] = total
    parts = thirds(raw[...])
    for phase in range(2):
        split[phase] = exact_dot(parts, halves[phase])
    for q in range(g.w):
        for phase in range(2):
            for a in range(2 * g.ra):
                for s in range(s_count):
                    at = ((phase * 2 * g.ra + a) * s_count + s) * 16
                    rows = pl.ds(s * 32 * la + 2 * q * g.ra + a, 16, stride=2 * la)
                    stage[q, at : at + 16] = split[phase, rows, :]
    last = [(stage.at[worker, :end_fine], out.at[:end_fine]) for worker, out in zip(workers, out_refs)]
    wait_all(done + start_all(last, out_sems, g.n))


def relay_kernel(g, *rest):
    in_refs, (edge_out,) = rest[: g.n], rest[g.n :]
    me = lax.axis_index("rad")
    low = jnp.minimum(me, g.w - 1) < g.w // 2
    _, end_emit, end_mix, _ = large_there(g)
    rows_a = 2 * g.ra + 2
    for k in range(g.n):
        source = lax.rem(me + g.n - k, g.n)
        for s in range(g.s):
            sub = source * g.s + s
            mid = end_emit + s * 4 * rows_a
            coarse = end_mix + (g.ra + 4) * s
            end_mid, end_coarse = mid + 4 * rows_a, coarse + g.ra + 4
            value = jnp.where(low, in_refs[k][mid : mid + 4], in_refs[k][end_mid - 4 : end_mid])
            edge_out[pl.ds(sub, 4, stride=g.h), :] = value
            value = jnp.where(low, in_refs[k][coarse : coarse + 2], in_refs[k][end_coarse - 2 : end_coarse])
            edge_out[pl.ds(4 * g.h + sub, 2, stride=g.h), :] = value


def outside(g, q):
    low = q < g.w // 2
    rows = [(a, q * g.ra - 2 + a) for a in range(g.ra + 4)]
    return [(a, a if low else a - g.ra - 2) for a, row in rows if row < 0 or row >= g.la]


def unpack_kernel(g, *rest):
    in_refs, (fine_out, emit_out, mix_out, coarse_out) = rest[: g.n], rest[g.n :]
    me = lax.axis_index("rad")
    end_fine, end_emit, end_mix, _ = large_there(g)
    h, ra, rows_a = g.h, g.ra, 2 * g.ra + 2
    for k in range(g.n):
        source = lax.rem(me + g.n - k, g.n)
        got = in_refs[k]
        for s in range(g.s):
            sub = source * g.s + s
            for x in range(4 * ra):
                at = (x * g.s + s) * 16
                fine_out[pl.ds(x * 16 * h + sub, 16, stride=h), :] = got[at : at + 16]
            emit_out[pl.ds(sub, 64 * ra, stride=h), :] = got[end_fine:end_emit]
            at = end_emit + s * 4 * rows_a
            mix_out[pl.ds(sub, 4 * rows_a, stride=h), :] = got[at : at + 4 * rows_a]
            at = end_mix + (ra + 4) * s
            coarse_out[pl.ds(sub, ra + 4, stride=h), :] = got[at : at + ra + 4]


def weight_kernel(g, block, own, spread, own_out, block_out):
    own_out[...] = own[...]
    block_out[...] = block[...]
    begins, _ = prepared_rows(g)
    for x in range(24):
        at = begins["stencil"] + x * g.h
        tile = block[at : at + g.h]
        for o in range(27):
            spread[x * 27 + o] = jnp.broadcast_to(tile[:, o : o + 1], (g.h, g.b))


def edges_inside(g, worker):
    first = lax.axis_index("ang") * g.la + worker * g.ra
    inside = jnp.where(first > 0, 1.0, 0.0), jnp.where(first + g.ra < g.m * g.la, 1.0, 0.0)
    return [x.astype(F32) for x in inside]


def cell_rows_of(g, a, c, pr):
    return pl.ds(pl.multiple_of(((a * 8 + c) * 2 + pr) * g.h, 8), g.h)


def forward_kernel(g, block, spread, *rest):
    n, b, s_count, ra, h = g.n, g.b, g.s, g.ra, g.h
    fine_in, emit_in, mixed, coarse, near = rest[:5]
    cells, resid_out = rest[5:7]
    mix_in, coarse_in, coarse_ext, mid_ext, seen = rest[7:]
    me, ang = lax.axis_index("rad"), lax.axis_index("ang")
    rows_a = 2 * ra + 2
    spacing = 1.0 / (4 * n)
    worker = jnp.minimum(me, g.w - 1)
    begins, _ = prepared_rows(g)

    def weight_at(level, c, o):
        return spread[(level * 8 + c) * 27 + o]

    mix_in[...] = mixed[...]
    coarse_in[...] = coarse[...]
    live = jnp.where(worker < g.w // 2, ang > 0, ang < g.m - 1)
    for q in range(g.w):
        @pl.when(worker == q)
        def _(q=q):
            if q == 0:
                mix_in[: 4 * h] = jnp.where(live, near[: 4 * h], 0.0)
            if q == g.w - 1:
                mix_in[4 * (rows_a - 1) * h :] = jnp.where(live, near[: 4 * h], 0.0)
            for a, place in outside(g, q):
                at = (4 + place) * h
                coarse_in[a * h : (a + 1) * h] = jnp.where(live, near[at : at + h], 0.0)

    top_in, bottom_in = edges_inside(g, worker)
    for a in range(ra + 4):
        x = coarse_in[a * h : (a + 1) * h]
        for db in range(3):
            shifted = along_lanes(x, 1 - db)
            for dr in range(3):
                coarse_ext[dr, a, db] = along_rows(shifted, (1 - dr) * s_count)
    for c in range(8):
        cr, ca, cb = c // 4, c // 2 % 2, c % 2
        weight = [weight_at(0, c, o) for o in range(27)]
        for row in range(1 - ca, rows_a, 2):
            a = (row - 1) // 2
            at = (row * 4 + 2 * cr + cb) * h
            total = mix_in[at : at + h]
            for dr in range(3):
                for da in range(3):
                    for db in range(3):
                        total = total + weight[9 * dr + 3 * da + db] * coarse_ext[dr, a + 1 + da, db]
            if row == 0:
                total = total * top_in
            if row == rows_a - 1:
                total = total * bottom_in
            for bi, step_b in ((1 + cb, 0), (3, -1) if cb == 0 else (0, 1)):
                shifted = along_lanes(total, step_b)
                for ri, step_r in ((1 + cr, 0), (3, -1) if cr == 0 else (0, 1)):
                    mid_ext[ri, row, bi] = along_rows(shifted, step_r * s_count)

    cell_rows = functools.partial(cell_rows_of, g)

    def fine_cells(c, carry):
        for pr in range(2):
            weight = [weight_at(1 + pr, c, o) for o in range(27)]
            for a in range(2 * ra):
                for pb in range(2):
                    at = (((pb * 2 * ra + a) * 8 + c) * 2 + pr) * h
                    total = fine_in[pl.ds(pl.multiple_of(at, 8), h), :]
                    for dr in range(3):
                        for da in range(3):
                            for db in range(3):
                                o = 9 * dr + 3 * da + db
                                total = total + weight[o] * mid_ext[pr + dr, a + da, pb + db]
                    cells[pb, cell_rows(a, c, pr), :] = total
        return carry

    lax.fori_loop(0, 4, lambda i, carry: fine_cells(2 * i + 1, fine_cells(2 * i, carry)), 0)

    radial = (4 * (lax.broadcasted_iota(jnp.int32, (h, b), 0) // s_count)).astype(F32)

    def sum_before(x):
        step = s_count
        while step < h:
            x = x + along_rows(x, step)
            step *= 2
        return along_rows(x, s_count)

    def sum_all(x):
        step = s_count
        while step < h:
            x = x + pltpu.roll(x, step, axis=0)
            step *= 2
        return x

    def positions(at, carry):
        a = at
        spots = []
        for pb in range(4):
            cb = pb % 2
            rows = [cell_rows(a // 2, 4 * (f % 2) + 2 * lax.rem(a, 2) + cb, f // 2) for f in range(4)]
            emit = [pl.multiple_of(((pb * 4 + f) * 4 * ra + a) * h, 8) for f in range(4)]
            stars = [(star * 4 * ra + a) * 4 + pb for star in range(g.stars)]
            spots.append((pb, rows, emit, stars))
        density = [[jnp.exp(cells[pb // 2, rows[f], :]) for f in range(4)] for pb, rows, _, _ in spots]
        glow = [[spacing * emit_in[pl.ds(emit[f], h), :] for f in range(4)] for _, _, emit, _ in spots]
        bins = [[block[pl.ds(begins["bins"] + row, 1), :] for row in stars] for _, _, _, stars in spots]
        data = [[block[pl.ds(begins["data"] + row, 1), :] for row in stars] for _, _, _, stars in spots]
        column = []
        for d, light in zip(density, glow):
            layer = [spacing * x for x in d]
            depth = sum_before(layer[0] + layer[1] + layer[2] + layer[3])
            for f in range(4):
                light[f] = light[f] * jnp.exp(-depth)
                depth = depth + layer[f]
            running = sum_before(light[0] + light[1] + light[2] + light[3])
            column.append([])
            for f in range(4):
                running = running + light[f]
                column[-1].append(running)
        total = [[jnp.zeros((h, b), F32) for f in range(4)] for _ in spots]
        seen_at = []
        for star in range(g.stars):
            for x, (pb, _, _, _) in enumerate(spots):
                bin_here = jnp.broadcast_to(bins[x][star], (h, b)) - radial
                mine = jnp.where(bin_here == 0, column[x][0], 0.0)
                for f in range(1, 4):
                    mine = jnp.where(bin_here == f, column[x][f], mine)
                predicted = sum_all(mine)
                residual = jnp.broadcast_to(data[x][star], (h, b)) - predicted
                seen_at.append((pb, star, residual))
                for f in range(4):
                    term = residual * (predicted - column[x][f])
                    total[x][f] = total[x][f] + jnp.where(bin_here > f, term, 0.0)
        for pb, star, residual in seen_at:
            for s in range(s_count):
                seen[pb, pl.ds((s * g.stars + star) * 4 * ra + a, 1), :] = residual[s : s + 1]
        for x, (pb, rows, _, _) in enumerate(spots):
            for f in range(4):
                cells[pb // 2, rows[f], :] = -density[x][f] * total[x][f]
        return carry

    lax.fori_loop(0, 4 * ra, positions, 0)

    shown = None
    for phase in range(4):
        value = exact_dot(thirds(seen[phase]), place_columns(b, 4, phase))
        shown = value if shown is None else shown + value
    per = 4 * g.stars * ra * s_count
    for part in range(4):
        resid_out[part * per : (part + 1) * per] = shown[:, part * b : (part + 1) * b]


def backward_kernel(g, spread, cells, parent, coarse_sum, edge_sum, tall):
    n, b, s_count, ra, h = g.n, g.b, g.s, g.ra, g.h
    rows_a = 2 * ra + 2
    worker = jnp.minimum(lax.axis_index("rad"), g.w - 1)
    top_in, bottom_in = edges_inside(g, worker)
    cell_rows = functools.partial(cell_rows_of, g)

    def weight_at(level, c, o):
        return spread[(level * 8 + c) * 27 + o]

    tall[...] = jnp.zeros(tall.shape, F32)
    for pr in range(2):
        def gather(c, carry, pr=pr):
            values = {(a, pb): cells[pb, cell_rows(a, c, pr), :] for a in range(2 * ra) for pb in range(2)}
            for dr in range(3):
                sums = {}
                for da in range(3):
                    for db in range(3):
                        weight = weight_at(1 + pr, c, 9 * dr + 3 * da + db)
                        for (a, pb), value in values.items():
                            key = (a + da, pb + db)
                            term = weight * value
                            sums[key] = sums[key] + term if key in sums else term
                for (row, bi), value in sums.items():
                    tall[pr + dr, row, bi] += value
            return carry

        lax.fori_loop(0, 4, lambda i, carry: gather(2 * i + 1, gather(2 * i, carry)), 0)
    for row in range(rows_a):
        for pr in range(2):
            for pb in range(2):
                bi, step_b = (3, 1) if pb == 0 else (0, -1)
                ri, step_r = (3, 1) if pr == 0 else (0, -1)
                close = tall[1 + pr, row, 1 + pb] + along_lanes(tall[1 + pr, row, bi], step_b)
                far = tall[ri, row, 1 + pb] + along_lanes(tall[ri, row, bi], step_b)
                value = close + along_rows(far, step_r * s_count)
                if row == 0:
                    value = value * top_in
                if row == rows_a - 1:
                    value = value * bottom_in
                at = ((2 * pr + pb) * rows_a + row) * h
                parent[at : at + h] = value

    coarse_sum[...] = jnp.zeros(coarse_sum.shape, F32)
    for dr in range(3):
        for db in range(3):
            sums = {}
            for c in range(8):
                cr, ca, cb = c // 4, c // 2 % 2, c % 2
                for da in range(3):
                    weight = weight_at(0, c, 9 * dr + 3 * da + db)
                    for row in range(1 - ca, rows_a, 2):
                        at = ((2 * cr + cb) * rows_a + row) * h
                        term = weight * parent[at : at + h]
                        key = (row - 1) // 2 + 1 + da
                        sums[key] = sums[key] + term if key in sums else term
            for a, value in sums.items():
                coarse_sum[a * h : (a + 1) * h] += along_lanes(along_rows(value, (dr - 1) * s_count), db - 1)

    low = worker < g.w // 2
    for x in range(4):
        at, end = x * rows_a * h, (x + 1) * rows_a * h
        edge_sum[x * h : (x + 1) * h] = jnp.where(low, parent[at : at + h], parent[end - h : end])
    edge_sum[4 * h :] = jnp.where(low, coarse_sum[: 2 * h], coarse_sum[(ra + 2) * h :])


def lanes_kernel(g, cells, out, joined):
    n, b, s_count, ra, h = g.n, g.b, g.s, g.ra, g.h
    parts = [thirds(cells[phase]) for phase in range(2)]
    order = [place_columns(b, 2, phase) for phase in range(2)]
    for half in range(2):
        lanes = slice(half * b, (half + 1) * b)
        joined[half] = exact_dot(parts[0], order[0][:, lanes]) + exact_dot(parts[1], order[1][:, lanes])
    for r in range(n):
        for s in range(s_count):
            for half in range(2):
                for a in range(2 * ra):
                    at = ((half * 2 * ra + a) * s_count + s) * 16
                    out[r, at : at + 16] = joined[half, pl.ds(a * 16 * h + r * s_count + s, 16, stride=h), :]


def sums_kernel(g, field, parent_ref, coarse_ref, edge_ref, *rest):
    out_refs, (stage, parent, coarse_sum) = rest[: g.n], rest[g.n :]
    me, ang = lax.axis_index("rad"), lax.axis_index("ang")
    n, s_count, ra, h = g.n, g.s, g.ra, g.h
    rows_a = 2 * ra + 2
    worker = jnp.minimum(me, g.w - 1)
    live = jnp.where(worker < g.w // 2, ang < g.m - 1, ang > 0)
    end_field, end_mid, end = rows_back(g)
    parent[...] = parent_ref[...]
    coarse_sum[...] = coarse_ref[...]
    for q in range(g.w):
        @pl.when(worker == q)
        def _(q=q):
            if q == 0 or q == g.w - 1:
                for x in range(4):
                    at = (x * rows_a + (0 if q == 0 else rows_a - 1)) * h
                    parent[at : at + h] = jnp.where(live, edge_ref[x * h : (x + 1) * h], 0.0)
            for a, place in outside(g, q):
                at = (4 + place) * h
                coarse_sum[a * h : (a + 1) * h] = jnp.where(live, edge_ref[at : at + h], 0.0)
    for r in range(n):
        for s in range(s_count):
            sub = r * s_count + s
            at = s * 4 * rows_a
            stage[r, at : at + 4 * rows_a] = parent[pl.ds(sub, 4 * rows_a, stride=h), :]
            at = end_mid - end_field + (ra + 4) * s
            stage[r, at : at + ra + 4] = coarse_sum[pl.ds(sub, ra + 4, stride=h), :]
    for k in range(n):
        owner = lax.rem(me + k, n)
        out_refs[k][:end_field] = field[owner]
        out_refs[k][end_field:end] = stage[owner]


def join_kernel(g, one, two, after, out):
    rows = one.shape[0]
    out[:rows] = one[...]
    out[rows:] = two[...]


def resid_owner_kernel(g, ids, block, *rest):
    in_refs, (resid_out, mixes, shown) = rest[:-3], rest[-3:]
    me = lax.axis_index("rad")
    b, s_count, ra = g.b, g.s, g.ra
    begins, end = prepared_rows(g)
    per = 4 * g.stars * ra
    mixes[...] = block[begins["mid"] : end]
    for ref, held_ids in zip(in_refs, ids):
        for at, i in enumerate(held_ids):
            shown[me ^ i] = ref[at * 4 * s_count * per : (at + 1) * 4 * s_count * per]
    for q in range(g.w):
        for s in range(s_count):
            for part in range(4):
                for star in range(g.stars):
                    at = (part * s_count + s) * per + star * 4 * ra
                    rows = slice(4 * q * ra, 4 * (q + 1) * ra)
                    resid_out[s, star, rows, part * b : (part + 1) * b] = shown[q, at : at + 4 * ra]


def owner_kernel(g, mixes, *rest):
    in_refs, (coarse_out, mid_out, fine_out, got, fine, grad_mid, grad_coarse) = rest[: g.n], rest[g.n :]
    me = lax.axis_index("rad")
    n, b, s_count, ra, la = g.n, g.b, g.s, g.ra, g.la
    rows_a = 2 * ra + 2
    end_field, end_mid, _ = rows_back(g)
    for k in range(n):
        got[lax.rem(me + n - k, n)] = in_refs[k][...]
    grad_mid[...] = jnp.zeros(grad_mid.shape, F32)
    grad_coarse[...] = jnp.zeros(grad_coarse.shape, F32)
    for q in range(g.w):
        for s in range(s_count):
            for half in range(2):
                for a in range(2 * ra):
                    at = ((half * 2 * ra + a) * s_count + s) * 16
                    rows = pl.ds(s * 32 * la + 2 * q * ra + a, 16, stride=2 * la)
                    fine[half, rows, :] = got[q, at : at + 16]
            for x in range(4):
                at = end_field + s * 4 * rows_a + x * rows_a
                grad_mid[s, x, 2 * q * ra : 2 * q * ra + rows_a] += got[q, at : at + rows_a]
            at = end_mid + (ra + 4) * s
            grad_coarse[s, q * ra : q * ra + ra + 4] += got[q, at : at + ra + 4]
    for s in range(s_count):
        for x in range(4):
            grad_mid[s, x, 1:2] += grad_mid[s, x, 2 * la + 1 :]
            grad_mid[s, x, 2 * la : 2 * la + 1] += grad_mid[s, x, :1]
        grad_coarse[s, 2:4] += grad_coarse[s, la + 2 :]
        grad_coarse[s, la : la + 2] += grad_coarse[s, :2]
    for i in range(2):
        for j in range(8):
            rows = [64 + 64 * i + 8 * c + j for c in range(8)]
            weight = [mixes[row : row + 1] for row in rows]
            for s in range(s_count):
                for half in range(2):
                    total = None
                    for c in range(8):
                        at = ((s * 8 + c) * 2 + i) * 2 * la
                        term = weight[c] * fine[half, at : at + 2 * la]
                        total = term if total is None else total + term
                    fine_out[s, j, i, :, half * b : (half + 1) * b] = total
    for s in range(s_count):
        coarse_out[s, 0] = grad_coarse[s, 2 : 2 + la]
        cells = []
        for c in range(8):
            cr, ca, cb = c // 4, c // 2 % 2, c % 2
            cells.append(grad_mid[s, 2 * cr + cb, pl.ds(1 + ca, la, stride=2), :])
        for j in range(8):
            total = mixes[j : j + 1] * cells[0]
            for c in range(1, 8):
                total = total + mixes[j + 8 * c : j + 8 * c + 1] * cells[c]
            mid_out[s, j, 0] = total


def held(arrays):
    return [(pltpu.SMEM if len(x.shape) == 1 else pltpu.VMEM)(x.shape, x.dtype) for x in arrays]


def call(kernel, name, outs, operands, scratch, unmoved=0, written=0):
    vmem = pl.BlockSpec(memory_space=pltpu.VMEM)
    placed = pl.BlockSpec(memory_space=pl.ANY)
    limit = None if unmoved else VMEM_LIMIT
    return pl.pallas_call(
        kernel,
        name=name,
        out_shape=[jax.ShapeDtypeStruct(shape, kind) for shape, kind in outs],
        in_specs=[placed] * unmoved + [vmem] * (len(operands) - unmoved),
        out_specs=[placed] * written + [vmem] * (len(outs) - written),
        scratch_shapes=[pltpu.VMEM(shape, F32) if isinstance(shape, tuple) else shape for shape in scratch],
        compiler_params=pltpu.CompilerParams(vmem_limit_bytes=limit),
    )(*operands)


def per_device(
    g,
    coarse_field,
    excite_mid,
    excite_fine,
    kernels_mid,
    noise_mid,
    rows_mid,
    kernels_fine,
    noise_fine,
    rows_fine,
    emission,
    star_bins,
    star_data,
):
    n, m, s, la, b, stars, w, ra, h = g
    kernel = functools.partial
    rows_a = 2 * ra + 2
    workers = [(r, a, 1 if min(r, w - 1) < w // 2 else -1) for r in range(n) for a in range(m)]
    sideways = [(r * m + a, r * m + (a - step) % m) for r, a, step in workers]
    inward = [(to, at) for at, to in sideways]

    def exchange(blocks):
        return [blocks[0]] + [lax.ppermute(blocks[k], "rad", [(i, (i + k) % n) for i in range(n)]) for k in range(1, n)]

    noise_mid, noise_fine = noise_mid.transpose(1, 2, 0), noise_fine.transpose(1, 2, 0)
    large = (large_there(g)[-1], b)
    operands = (emission, rows_mid, noise_mid, coarse_field, excite_mid, rows_fine, noise_fine, excite_fine)
    sent = call(
        kernel(scatter_kernel, g),
        "scatter",
        [(large, F32)] * n,
        operands,
        [
            *held(operands),
            pltpu.SemaphoreType.DMA((10 + 2 * s,)),
            pltpu.SemaphoreType.DMA((2 * n,)),
            (32 * s * la, 2 * b),
            (2, 32 * s * la, b),
            (4, 16 * la, b),
            (w, *large),
            (s, 8, la, b),
            (s, la + 4, b),
        ],
        unmoved=8,
        written=n,
    )
    got = exchange(sent)
    operands = (rows_mid, rows_fine, noise_mid, noise_fine, kernels_mid, kernels_fine, star_bins, star_data)
    (block,) = call(
        kernel(prepare_kernel, g),
        "prepare",
        [((prepared_rows(g)[1], b), F32)],
        (*operands, sent[0]),
        [*held(operands), pltpu.SemaphoreType.DMA((8,)), (2, 4 * stars * ra, 4 * b)],
        unmoved=9,
    )
    spread, got[0], block = call(
        kernel(weight_kernel, g),
        "weights",
        [((24 * 27, h, b), F32), (large, F32), (block.shape, F32)],
        (block, sent[0]),
        [],
    )
    (near,) = call(kernel(relay_kernel, g), "relay", [((6 * h, b), F32)], got, [])
    near = lax.ppermute(near, ("rad", "ang"), inward)
    parts = [(64 * ra * h, b), (64 * ra * h, b), (4 * rows_a * h, b), ((ra + 4) * h, b)]
    unpacked = call(kernel(unpack_kernel, g), "unpack", [(part, F32) for part in parts], got, [])
    def everywhere(block, after):
        ids, bit = [0], n // 2
        while True:
            got = lax.ppermute(block, "rad", [(i, i ^ bit) for i in range(n)])
            more = [i ^ bit for i in ids]
            if bit == 1:
                return (block, got), (ids, more)
            shape = (2 * block.shape[0], b)
            (block,) = call(kernel(join_kernel, g), "join", [(shape, F32)], (block, got, after), [])
            ids, bit = ids + more, bit // 2

    end_field, _, end = rows_back(g)
    resid_rows = 16 * stars * ra * s
    cells, shown = call(
        kernel(forward_kernel, g),
        "forward",
        [((2, 32 * ra * h, b), F32), ((resid_rows, b), F32)],
        (block, spread, *unpacked, near),
        [
            (4 * rows_a * h, b),
            ((ra + 4) * h, b),
            (3, ra + 4, 3, h, b),
            (4, rows_a, 4, h, b),
            (4, 4 * stars * ra * s, b),
        ],
    )
    parent, coarse_sum, edge = call(
        kernel(backward_kernel, g),
        "backward",
        [((4 * rows_a * h, b), F32), (((ra + 4) * h, b), F32), ((6 * h, b), F32)],
        (spread, cells),
        [(4, rows_a, 4, h, b)],
    )
    edge = lax.ppermute(edge, ("rad", "ang"), sideways)
    (field,) = call(
        kernel(lanes_kernel, g), "lanes", [((n, end_field, b), F32)], (cells,), [(2, 32 * ra * h, b)]
    )
    got = exchange(
        call(
            kernel(sums_kernel, g),
            "sums",
            [((end, b), F32)] * n,
            (field, parent, coarse_sum, edge),
            [(n, end - end_field, b), parent.shape, coarse_sum.shape],
        )
    )
    shown, ids = everywhere(shown, got[0])
    residual, mixes = call(
        kernel(resid_owner_kernel, g, ids),
        "resid_owner",
        [((s, stars, 4 * la, 4 * b), F32), ((192, b), F32)],
        (block, *shown),
        [(n, resid_rows, b)],
    )
    grad_coarse, grad_mid, grad_fine = call(
        kernel(owner_kernel, g),
        "owner",
        [((s, 1, la, b), F32), ((s, 8, 1, la, b), F32), ((s, 8, 2, 2 * la, 2 * b), F32)],
        (mixes, *got),
        [(n, end, b), (2, 32 * s * la, b), (s, 4, 2 * la + 2, b), (s, la + 4, b)],
    )
    return grad_coarse, grad_mid, grad_fine, residual


def solution(mesh):
    placed = (
        P(None, "rad", "ang", None),
        P(None, None, "rad", "ang", None),
        P(None, None, "rad", "ang", None),
        P(),
        P(),
        P(),
        P(),
        P(),
        P(),
        P("rad", "ang", None),
        P(None, "ang", None),
        P(None, "ang", None),
    )

    def local(*args):
        return per_device(make_plan(mesh, args[0], args[10]), *args)

    return jax.shard_map(
        local,
        mesh=mesh,
        in_specs=placed,
        out_specs=(
            P(None, "rad", "ang", None),
            P(None, None, "rad", "ang", None),
            P(None, None, "rad", "ang", None),
            P(None, None, "ang", None),
        ),
        check_vma=False,
    )
```

```python
import functools
import typing

import jax
import jax.numpy as jnp
from jax import lax
from jax.experimental import pallas as pl
from jax.experimental.pallas import tpu as pltpu
from jax.sharding import PartitionSpec as P

F32 = jnp.float32
BF16 = jnp.bfloat16
VMEM_LIMIT = 24 * 1024 * 1024


class Plan(typing.NamedTuple):
    n: int
    m: int
    s: int
    la: int
    b: int
    stars: int
    w: int
    ra: int
    h: int


def make_plan(mesh, coarse, star_bins):
    n, m = mesh.shape["rad"], mesh.shape["ang"]
    s, rows, la, b = coarse.shape
    w = max(d for d in range(1, min(n, la) + 1) if la % d == 0)
    ra = la // w
    assert rows == 1 and n & (n - 1) == 0 and w % 2 == 0 and (w // 2) * ra >= 2
    return Plan(n, m, s, la, b, star_bins.shape[0], w, ra, n * s)


def eights(rows):
    return -(-rows // 8) * 8


def large_there(g):
    fine = 2 * 2 * g.ra * g.s * 16
    emit = fine + 16 * 4 * g.ra
    mix = emit + g.s * 4 * (2 * g.ra + 2)
    return fine, emit, mix, eights(mix + g.s * (g.ra + 4))


def rows_back(g):
    field = 2 * 2 * g.ra * g.s * 16
    mid = field + g.s * 4 * (2 * g.ra + 2)
    return field, mid, eights(mid + g.s * (g.ra + 4))


def prepared_rows(g):
    sizes = dict(
        stencil=24 * g.h,
        bins=16 * g.stars * g.ra,
        data=16 * g.stars * g.ra,
        mid=64,
        fine=128,
    )
    begins, at = {}, 0
    for part, size in sizes.items():
        begins[part] = at
        at += size
    return begins, at


def table_weights(table_ref, entry):
    lane = lax.broadcasted_iota(jnp.int32, table_ref.shape[1:], 1)
    columns = [
        jnp.sum(jnp.where(lane == entry, table_ref[c], 0.0), axis=1, keepdims=True) for c in range(table_ref.shape[0])
    ]
    return lambda c, j: columns[c][j : j + 1]


def start_all(pairs, sems, first=0):
    copies = [pltpu.make_async_copy(source, here, sems.at[first + i]) for i, (source, here) in enumerate(pairs)]
    for copy in copies:
        copy.start()
    return copies


def wait_all(copies):
    for copy in copies:
        copy.wait()


def pick_columns(length, ways, phase):
    src = lax.broadcasted_iota(jnp.int32, (length * ways, length), 0)
    dst = lax.broadcasted_iota(jnp.int32, (length * ways, length), 1)
    return jnp.where(src == ways * dst + phase, 1.0, 0.0).astype(BF16)


def place_columns(length, ways, phase):
    src = lax.broadcasted_iota(jnp.int32, (length, length * ways), 0)
    dst = lax.broadcasted_iota(jnp.int32, (length, length * ways), 1)
    return jnp.where(dst == ways * src + phase, 1.0, 0.0).astype(BF16)


def thirds(x):
    high = x.astype(BF16)
    rest = x - high.astype(F32)
    middle = rest.astype(BF16)
    return jnp.concatenate([high, middle, (rest - middle.astype(F32)).astype(BF16)], axis=0)


def exact_dot(parts, choice):
    sums = jnp.dot(parts, choice, preferred_element_type=F32)
    rows = sums.shape[0] // 3
    return sums[:rows] + (sums[rows : 2 * rows] + sums[2 * rows :])


def along_lanes(x, step):
    if step == 0:
        return x
    size = x.shape[1]
    lane = lax.broadcasted_iota(jnp.int32, x.shape, 1)
    edge = 0 if step > 0 else size - 1
    return jnp.where(lane == edge, 0.0, pltpu.roll(x, step % size, axis=1))


def along_rows(x, step):
    if step == 0:
        return x
    size = x.shape[0]
    row = lax.broadcasted_iota(jnp.int32, x.shape, 0)
    kept = row >= step if step > 0 else row < size + step
    return jnp.where(kept, pltpu.roll(x, step % size, axis=0), 0.0)


def prepare_kernel(g, *rest):
    sources, block, rest = rest[:8], rest[9], rest[10:]
    held, (sems, gathered) = rest[:8], rest[8:]
    copies = start_all(list(zip(sources, held)), sems)
    rows_mid, rows_fine, noise_mid, noise_fine, mid_table, fine_table, bins_ref, data_ref = held
    begins, _ = prepared_rows(g)
    me = lax.axis_index("rad")
    worker = jnp.minimum(me, g.w - 1)
    per, b = 4 * g.ra, g.b
    choices = [pick_columns(b, 4, phase) for phase in range(4)]
    wait_all(copies)
    for r in range(g.n):
        tables = [mid_table[rows_mid[r]], fine_table[rows_fine[2 * r]], fine_table[rows_fine[2 * r + 1]]]
        for level, table in enumerate(tables):
            for c in range(8):
                at = begins["stencil"] + (level * 8 + c) * g.h + r * g.s
                block[at : at + g.s, :27] = jnp.broadcast_to(table[c : c + 1], (g.s, 27))
    entries = [(begins["mid"], noise_mid, rows_mid[me])]
    entries += [(begins["fine"] + 64 * i, noise_fine, rows_fine[2 * me + i]) for i in range(2)]
    for at, table, entry in entries:
        lane = lax.broadcasted_iota(jnp.int32, table.shape[1:], 1)
        for c in range(8):
            column = jnp.sum(jnp.where(lane == entry, table[c], 0.0), axis=1, keepdims=True)
            block[at + 8 * c : at + 8 * c + 8] = jnp.broadcast_to(column, (8, b))
    for q in range(g.w):
        @pl.when(worker == q)
        def _(q=q):
            for star in range(g.stars):
                gathered[0, star * per : (star + 1) * per] = bins_ref[star, q * per : (q + 1) * per].astype(F32)
                gathered[1, star * per : (star + 1) * per] = data_ref[star, q * per : (q + 1) * per]
    bins = gathered[0].astype(BF16)
    parts = thirds(gathered[1])
    for phase in range(4):
        rows = pl.ds(begins["bins"] + phase, g.stars * per, stride=4)
        block[rows, :] = jnp.dot(bins, choices[phase], preferred_element_type=F32)
        rows = pl.ds(begins["data"] + phase, g.stars * per, stride=4)
        block[rows, :] = exact_dot(parts, choices[phase])


def scatter_kernel(g, *rest):
    sources, out_refs, rest = rest[:8], rest[8 : 8 + g.n], rest[8 + g.n :]
    held, (sems, out_sems, raw, split, lit, stage, mixed, wide) = rest[:8], rest[8:]
    light = start_all([(sources[0].at[f], held[0].at[f]) for f in range(4)], sems)
    copies = start_all(list(zip(sources[1:7], held[1:7])), sems, 4)
    spots = [(s, slice(4 * part, 4 * part + 4)) for s in range(g.s) for part in range(2)]
    copies += start_all([(sources[7].at[spot], held[7].at[spot]) for spot in spots], sems, 10)
    emission_ref, rows_mid, noise_mid, coarse_ref, excite_ref, rows_ref, noise_ref, fine_ref = held
    me = lax.axis_index("rad")
    b, s_count, la = g.b, g.s, g.la
    end_fine, end_emit, end_mix, _ = large_there(g)
    choices = [pick_columns(b, 4, phase) for phase in range(4)]
    halves = [pick_columns(b, 2, phase) for phase in range(2)]
    wait_all(light)
    parts = thirds(emission_ref[...].reshape(16 * la, 4 * b))
    for phase in range(4):
        lit[phase] = exact_dot(parts, choices[phase])
    for q in range(g.w):
        for phase in range(4):
            for f in range(4):
                at = end_fine + (phase * 4 + f) * 4 * g.ra
                rows = slice(f * 4 * la + 4 * q * g.ra, f * 4 * la + 4 * (q + 1) * g.ra)
                stage[q, at : at + 4 * g.ra] = lit[phase, rows]
    wait_all(copies[:4])
    weight = table_weights(noise_mid, rows_mid[me])
    for c in range(8):
        for s in range(s_count):
            total = weight(c, 0) * excite_ref[s, 0, 0]
            for j in range(1, 8):
                total = total + weight(c, j) * excite_ref[s, j, 0]
            mixed[s, c] = total
    for s in range(s_count):
        wide[s, :2] = coarse_ref[s, 0, la - 2 :]
        wide[s, 2 : 2 + la] = coarse_ref[s, 0]
        wide[s, 2 + la :] = coarse_ref[s, 0, :2]
    for q in range(g.w):
        for s in range(s_count):
            for row in range(2 * g.ra + 2):
                a, ca = divmod((2 * q * g.ra - 1 + row) % (2 * la), 2)
                for cr in range(2):
                    for cb in range(2):
                        at = end_emit + ((s * (2 * g.ra + 2) + row) * 2 + cr) * 2 + cb
                        stage[q, at : at + 1] = mixed[s, 4 * cr + 2 * ca + cb, a : a + 1]
            at = end_mix + (g.ra + 4) * s
            stage[q, at : at + g.ra + 4] = wide[s, q * g.ra : q * g.ra + g.ra + 4]
    workers = [jnp.minimum(lax.rem(me + k, g.n), g.w - 1) for k in range(g.n)]
    done = [(stage.at[worker, end_fine:], out.at[end_fine:]) for worker, out in zip(workers, out_refs)]
    done = start_all(done, out_sems)
    wait_all(copies[4:])
    for i in range(2):
        weight = table_weights(noise_ref, rows_ref[2 * me + i])
        for c in range(8):
            weights = [weight(c, j) for j in range(8)]
            for s in range(s_count):
                total = weights[0] * fine_ref[s, 0, i]
                for j in range(1, 8):
                    total = total + weights[j] * fine_ref[s, j, i]
                at = ((s * 8 + c) * 2 + i) * 2 * la
                raw[at : at + 2 * la] = total
    parts = thirds(raw[...])
    for phase in range(2):
        split[phase] = exact_dot(parts, halves[phase])
    for q in range(g.w):
        for phase in range(2):
            for a in range(2 * g.ra):
                for s in range(s_count):
                    at = ((phase * 2 * g.ra + a) * s_count + s) * 16
                    rows = pl.ds(s * 32 * la + 2 * q * g.ra + a, 16, stride=2 * la)
                    stage[q, at : at + 16] = split[phase, rows, :]
    last = [(stage.at[worker, :end_fine], out.at[:end_fine]) for worker, out in zip(workers, out_refs)]
    wait_all(done + start_all(last, out_sems, g.n))


def relay_kernel(g, *rest):
    in_refs, (edge_out,) = rest[: g.n], rest[g.n :]
    me = lax.axis_index("rad")
    low = jnp.minimum(me, g.w - 1) < g.w // 2
    _, end_emit, end_mix, _ = large_there(g)
    rows_a = 2 * g.ra + 2
    for k in range(g.n):
        source = lax.rem(me + g.n - k, g.n)
        for s in range(g.s):
            sub = source * g.s + s
            mid = end_emit + s * 4 * rows_a
            coarse = end_mix + (g.ra + 4) * s
            end_mid, end_coarse = mid + 4 * rows_a, coarse + g.ra + 4
            value = jnp.where(low, in_refs[k][mid : mid + 4], in_refs[k][end_mid - 4 : end_mid])
            edge_out[pl.ds(sub, 4, stride=g.h), :] = value
            value = jnp.where(low, in_refs[k][coarse : coarse + 2], in_refs[k][end_coarse - 2 : end_coarse])
            edge_out[pl.ds(4 * g.h + sub, 2, stride=g.h), :] = value


def outside(g, q):
    low = q < g.w // 2
    rows = [(a, q * g.ra - 2 + a) for a in range(g.ra + 4)]
    return [(a, a if low else a - g.ra - 2) for a, row in rows if row < 0 or row >= g.la]


def unpack_kernel(g, *rest):
    in_refs, (fine_out, emit_out, mix_out, coarse_out) = rest[: g.n], rest[g.n :]
    me = lax.axis_index("rad")
    end_fine, end_emit, end_mix, _ = large_there(g)
    h, ra, rows_a = g.h, g.ra, 2 * g.ra + 2
    for k in range(g.n):
        source = lax.rem(me + g.n - k, g.n)
        got = in_refs[k]
        for s in range(g.s):
            sub = source * g.s + s
            for x in range(4 * ra):
                at = (x * g.s + s) * 16
                fine_out[pl.ds(x * 16 * h + sub, 16, stride=h), :] = got[at : at + 16]
            emit_out[pl.ds(sub, 64 * ra, stride=h), :] = got[end_fine:end_emit]
            at = end_emit + s * 4 * rows_a
            mix_out[pl.ds(sub, 4 * rows_a, stride=h), :] = got[at : at + 4 * rows_a]
            at = end_mix + (ra + 4) * s
            coarse_out[pl.ds(sub, ra + 4, stride=h), :] = got[at : at + ra + 4]


def weight_kernel(g, block, own, spread, own_out, block_out):
    own_out[...] = own[...]
    block_out[...] = block[...]
    begins, _ = prepared_rows(g)
    for x in range(24):
        at = begins["stencil"] + x * g.h
        tile = block[at : at + g.h]
        for o in range(27):
            spread[x * 27 + o] = jnp.broadcast_to(tile[:, o : o + 1], (g.h, g.b))


def edges_inside(g, worker):
    first = lax.axis_index("ang") * g.la + worker * g.ra
    inside = jnp.where(first > 0, 1.0, 0.0), jnp.where(first + g.ra < g.m * g.la, 1.0, 0.0)
    return [x.astype(F32) for x in inside]


def cell_rows_of(g, a, c, pr):
    return pl.ds(pl.multiple_of(((a * 8 + c) * 2 + pr) * g.h, 8), g.h)


def forward_kernel(g, block, spread, *rest):
    n, b, s_count, ra, h = g.n, g.b, g.s, g.ra, g.h
    fine_in, emit_in, mixed, coarse, near = rest[:5]
    cells, resid_out = rest[5:7]
    mix_in, coarse_in, coarse_ext, mid_ext, seen = rest[7:]
    me, ang = lax.axis_index("rad"), lax.axis_index("ang")
    rows_a = 2 * ra + 2
    spacing = 1.0 / (4 * n)
    worker = jnp.minimum(me, g.w - 1)
    begins, _ = prepared_rows(g)

    def weight_at(level, c, o):
        return spread[(level * 8 + c) * 27 + o]

    mix_in[...] = mixed[: 4 * rows_a * h]
    coarse_in[...] = coarse[: (ra + 4) * h]
    live = jnp.where(worker < g.w // 2, ang > 0, ang < g.m - 1)
    for q in range(g.w):
        @pl.when(worker == q)
        def _(q=q):
            if q == 0:
                mix_in[: 4 * h] = jnp.where(live, near[: 4 * h], 0.0)
            if q == g.w - 1:
                mix_in[4 * (rows_a - 1) * h :] = jnp.where(live, near[: 4 * h], 0.0)
            for a, place in outside(g, q):
                at = (4 + place) * h
                coarse_in[a * h : (a + 1) * h] = jnp.where(live, near[at : at + h], 0.0)

    top_in, bottom_in = edges_inside(g, worker)
    for a in range(ra + 4):
        x = coarse_in[a * h : (a + 1) * h]
        for db in range(3):
            shifted = along_lanes(x, 1 - db)
            for dr in range(3):
                coarse_ext[dr, a, db] = along_rows(shifted, (1 - dr) * s_count)
    for c in range(8):
        cr, ca, cb = c // 4, c // 2 % 2, c % 2
        weight = [weight_at(0, c, o) for o in range(27)]
        for row in range(1 - ca, rows_a, 2):
            a = (row - 1) // 2
            at = (row * 4 + 2 * cr + cb) * h
            total = mix_in[at : at + h]
            for dr in range(3):
                for da in range(3):
                    for db in range(3):
                        total = total + weight[9 * dr + 3 * da + db] * coarse_ext[dr, a + 1 + da, db]
            if row == 0:
                total = total * top_in
            if row == rows_a - 1:
                total = total * bottom_in
            for bi, step_b in ((1 + cb, 0), (3, -1) if cb == 0 else (0, 1)):
                shifted = along_lanes(total, step_b)
                for ri, step_r in ((1 + cr, 0), (3, -1) if cr == 0 else (0, 1)):
                    mid_ext[ri, row, bi] = along_rows(shifted, step_r * s_count)

    cell_rows = functools.partial(cell_rows_of, g)

    def fine_cells(c, carry):
        for pr in range(2):
            weight = [weight_at(1 + pr, c, o) for o in range(27)]
            for a in range(2 * ra):
                for pb in range(2):
                    at = (((pb * 2 * ra + a) * 8 + c) * 2 + pr) * h
                    total = fine_in[pl.ds(pl.multiple_of(at, 8), h), :]
                    for dr in range(3):
                        for da in range(3):
                            for db in range(3):
                                o = 9 * dr + 3 * da + db
                                total = total + weight[o] * mid_ext[pr + dr, a + da, pb + db]
                    cells[pb, cell_rows(a, c, pr), :] = total
        return carry

    lax.fori_loop(0, 4, lambda i, carry: fine_cells(2 * i + 1, fine_cells(2 * i, carry)), 0)

    radial = (4 * (lax.broadcasted_iota(jnp.int32, (h, b), 0) // s_count)).astype(F32)

    def sum_before(x):
        step = s_count
        while step < h:
            x = x + along_rows(x, step)
            step *= 2
        return along_rows(x, s_count)

    def sum_all(x):
        step = s_count
        while step < h:
            x = x + pltpu.roll(x, step, axis=0)
            step *= 2
        return x

    def positions(at, carry):
        a = at
        spots = []
        for pb in range(4):
            cb = pb % 2
            rows = [cell_rows(a // 2, 4 * (f % 2) + 2 * lax.rem(a, 2) + cb, f // 2) for f in range(4)]
            emit = [pl.multiple_of(((pb * 4 + f) * 4 * ra + a) * h, 8) for f in range(4)]
            stars = [(star * 4 * ra + a) * 4 + pb for star in range(g.stars)]
            spots.append((pb, rows, emit, stars))
        density = [[jnp.exp(cells[pb // 2, rows[f], :]) for f in range(4)] for pb, rows, _, _ in spots]
        glow = [[spacing * emit_in[pl.ds(emit[f], h), :] for f in range(4)] for _, _, emit, _ in spots]
        bins = [[block[pl.ds(begins["bins"] + row, 1), :] for row in stars] for _, _, _, stars in spots]
        data = [[block[pl.ds(begins["data"] + row, 1), :] for row in stars] for _, _, _, stars in spots]
        column = []
        for d, light in zip(density, glow):
            layer = [spacing * x for x in d]
            depth = sum_before(layer[0] + layer[1] + layer[2] + layer[3])
            for f in range(4):
                light[f] = light[f] * jnp.exp(-depth)
                depth = depth + layer[f]
            running = sum_before(light[0] + light[1] + light[2] + light[3])
            column.append([])
            for f in range(4):
                running = running + light[f]
                column[-1].append(running)
        total = [[jnp.zeros((h, b), F32) for f in range(4)] for _ in spots]
        seen_at = []
        for star in range(g.stars):
            for x, (pb, _, _, _) in enumerate(spots):
                bin_here = jnp.broadcast_to(bins[x][star], (h, b)) - radial
                mine = jnp.where(bin_here == 0, column[x][0], 0.0)
                for f in range(1, 4):
                    mine = jnp.where(bin_here == f, column[x][f], mine)
                predicted = sum_all(mine)
                residual = jnp.broadcast_to(data[x][star], (h, b)) - predicted
                seen_at.append((pb, star, residual))
                for f in range(4):
                    term = residual * (predicted - column[x][f])
                    total[x][f] = total[x][f] + jnp.where(bin_here > f, term, 0.0)
        for pb, star, residual in seen_at:
            for s in range(s_count):
                seen[pb, pl.ds((s * g.stars + star) * 4 * ra + a, 1), :] = residual[s : s + 1]
        for x, (pb, rows, _, _) in enumerate(spots):
            for f in range(4):
                cells[pb // 2, rows[f], :] = -density[x][f] * total[x][f]
        return carry

    lax.fori_loop(0, 4 * ra, positions, 0)

    shown = None
    for phase in range(4):
        value = exact_dot(thirds(seen[phase]), place_columns(b, 4, phase))
        shown = value if shown is None else shown + value
    per = 4 * g.stars * ra * s_count
    for part in range(4):
        resid_out[part * per : (part + 1) * per] = shown[:, part * b : (part + 1) * b]


def backward_kernel(g, spread, cells, parent, coarse_sum, edge_sum, tall):
    n, b, s_count, ra, h = g.n, g.b, g.s, g.ra, g.h
    rows_a = 2 * ra + 2
    worker = jnp.minimum(lax.axis_index("rad"), g.w - 1)
    top_in, bottom_in = edges_inside(g, worker)
    cell_rows = functools.partial(cell_rows_of, g)

    def weight_at(level, c, o):
        return spread[(level * 8 + c) * 27 + o]

    tall[...] = jnp.zeros(tall.shape, F32)
    for pr in range(2):
        def gather(c, carry, pr=pr):
            values = {(a, pb): cells[pb, cell_rows(a, c, pr), :] for a in range(2 * ra) for pb in range(2)}
            for dr in range(3):
                sums = {}
                for da in range(3):
                    for db in range(3):
                        weight = weight_at(1 + pr, c, 9 * dr + 3 * da + db)
                        for (a, pb), value in values.items():
                            key = (a + da, pb + db)
                            term = weight * value
                            sums[key] = sums[key] + term if key in sums else term
                for (row, bi), value in sums.items():
                    tall[pr + dr, row, bi] += value
            return carry

        lax.fori_loop(0, 4, lambda i, carry: gather(2 * i + 1, gather(2 * i, carry)), 0)
    for row in range(rows_a):
        for pr in range(2):
            for pb in range(2):
                bi, step_b = (3, 1) if pb == 0 else (0, -1)
                ri, step_r = (3, 1) if pr == 0 else (0, -1)
                close = tall[1 + pr, row, 1 + pb] + along_lanes(tall[1 + pr, row, bi], step_b)
                far = tall[ri, row, 1 + pb] + along_lanes(tall[ri, row, bi], step_b)
                value = close + along_rows(far, step_r * s_count)
                if row == 0:
                    value = value * top_in
                if row == rows_a - 1:
                    value = value * bottom_in
                at = ((2 * pr + pb) * rows_a + row) * h
                parent[at : at + h] = value

    coarse_sum[...] = jnp.zeros(coarse_sum.shape, F32)
    for dr in range(3):
        for db in range(3):
            sums = {}
            for c in range(8):
                cr, ca, cb = c // 4, c // 2 % 2, c % 2
                for da in range(3):
                    weight = weight_at(0, c, 9 * dr + 3 * da + db)
                    for row in range(1 - ca, rows_a, 2):
                        at = ((2 * cr + cb) * rows_a + row) * h
                        term = weight * parent[at : at + h]
                        key = (row - 1) // 2 + 1 + da
                        sums[key] = sums[key] + term if key in sums else term
            for a, value in sums.items():
                coarse_sum[a * h : (a + 1) * h] += along_lanes(along_rows(value, (dr - 1) * s_count), db - 1)

    low = worker < g.w // 2
    for x in range(4):
        at, end = x * rows_a * h, (x + 1) * rows_a * h
        edge_sum[x * h : (x + 1) * h] = jnp.where(low, parent[at : at + h], parent[end - h : end])
    edge_sum[4 * h :] = jnp.where(low, coarse_sum[: 2 * h], coarse_sum[(ra + 2) * h :])


def lanes_kernel(g, cells, out, joined):
    n, b, s_count, ra, h = g.n, g.b, g.s, g.ra, g.h
    parts = [thirds(cells[phase]) for phase in range(2)]
    order = [place_columns(b, 2, phase) for phase in range(2)]
    for half in range(2):
        lanes = slice(half * b, (half + 1) * b)
        joined[half] = exact_dot(parts[0], order[0][:, lanes]) + exact_dot(parts[1], order[1][:, lanes])
    for r in range(n):
        for s in range(s_count):
            for half in range(2):
                for a in range(2 * ra):
                    at = ((half * 2 * ra + a) * s_count + s) * 16
                    out[r, at : at + 16] = joined[half, pl.ds(a * 16 * h + r * s_count + s, 16, stride=h), :]


def sums_kernel(g, field, parent_ref, coarse_ref, edge_ref, *rest):
    out_refs, (stage, parent, coarse_sum) = rest[: g.n], rest[g.n :]
    me, ang = lax.axis_index("rad"), lax.axis_index("ang")
    n, s_count, ra, h = g.n, g.s, g.ra, g.h
    rows_a = 2 * ra + 2
    worker = jnp.minimum(me, g.w - 1)
    live = jnp.where(worker < g.w // 2, ang < g.m - 1, ang > 0)
    end_field, end_mid, end = rows_back(g)
    parent[...] = parent_ref[...]
    coarse_sum[...] = coarse_ref[...]
    for q in range(g.w):
        @pl.when(worker == q)
        def _(q=q):
            if q == 0 or q == g.w - 1:
                for x in range(4):
                    at = (x * rows_a + (0 if q == 0 else rows_a - 1)) * h
                    parent[at : at + h] = jnp.where(live, edge_ref[x * h : (x + 1) * h], 0.0)
            for a, place in outside(g, q):
                at = (4 + place) * h
                coarse_sum[a * h : (a + 1) * h] = jnp.where(live, edge_ref[at : at + h], 0.0)
    for r in range(n):
        for s in range(s_count):
            sub = r * s_count + s
            at = s * 4 * rows_a
            stage[r, at : at + 4 * rows_a] = parent[pl.ds(sub, 4 * rows_a, stride=h), :]
            at = end_mid - end_field + (ra + 4) * s
            stage[r, at : at + ra + 4] = coarse_sum[pl.ds(sub, ra + 4, stride=h), :]
    for k in range(n):
        owner = lax.rem(me + k, n)
        out_refs[k][:end_field] = field[owner]
        out_refs[k][end_field:end] = stage[owner]


def join_kernel(g, one, two, after, out):
    rows = one.shape[0]
    out[:rows] = one[...]
    out[rows:] = two[...]


def resid_owner_kernel(g, ids, block, *rest):
    in_refs, (resid_out, mixes, shown) = rest[:-3], rest[-3:]
    me = lax.axis_index("rad")
    b, s_count, ra = g.b, g.s, g.ra
    begins, end = prepared_rows(g)
    per = 4 * g.stars * ra
    mixes[...] = block[begins["mid"] : end]
    for ref, held_ids in zip(in_refs, ids):
        for at, i in enumerate(held_ids):
            shown[me ^ i] = ref[at * 4 * s_count * per : (at + 1) * 4 * s_count * per]
    for q in range(g.w):
        for s in range(s_count):
            for part in range(4):
                for star in range(g.stars):
                    at = (part * s_count + s) * per + star * 4 * ra
                    rows = slice(4 * q * ra, 4 * (q + 1) * ra)
                    resid_out[s, star, rows, part * b : (part + 1) * b] = shown[q, at : at + 4 * ra]


def owner_kernel(g, mixes, *rest):
    in_refs, (coarse_out, mid_out, fine_out, got, fine, grad_mid, grad_coarse) = rest[: g.n], rest[g.n :]
    me = lax.axis_index("rad")
    n, b, s_count, ra, la = g.n, g.b, g.s, g.ra, g.la
    rows_a = 2 * ra + 2
    end_field, end_mid, _ = rows_back(g)
    for k in range(n):
        got[lax.rem(me + n - k, n)] = in_refs[k][...]
    grad_mid[...] = jnp.zeros(grad_mid.shape, F32)
    grad_coarse[...] = jnp.zeros(grad_coarse.shape, F32)
    for q in range(g.w):
        for s in range(s_count):
            for half in range(2):
                for a in range(2 * ra):
                    at = ((half * 2 * ra + a) * s_count + s) * 16
                    rows = pl.ds(s * 32 * la + 2 * q * ra + a, 16, stride=2 * la)
                    fine[half, rows, :] = got[q, at : at + 16]
            for x in range(4):
                at = end_field + s * 4 * rows_a + x * rows_a
                grad_mid[s, x, 2 * q * ra : 2 * q * ra + rows_a] += got[q, at : at + rows_a]
            at = end_mid + (ra + 4) * s
            grad_coarse[s, q * ra : q * ra + ra + 4] += got[q, at : at + ra + 4]
    for s in range(s_count):
        for x in range(4):
            grad_mid[s, x, 1:2] += grad_mid[s, x, 2 * la + 1 :]
            grad_mid[s, x, 2 * la : 2 * la + 1] += grad_mid[s, x, :1]
        grad_coarse[s, 2:4] += grad_coarse[s, la + 2 :]
        grad_coarse[s, la : la + 2] += grad_coarse[s, :2]
    for i in range(2):
        for j in range(8):
            rows = [64 + 64 * i + 8 * c + j for c in range(8)]
            weight = [mixes[row : row + 1] for row in rows]
            for s in range(s_count):
                for half in range(2):
                    total = None
                    for c in range(8):
                        at = ((s * 8 + c) * 2 + i) * 2 * la
                        term = weight[c] * fine[half, at : at + 2 * la]
                        total = term if total is None else total + term
                    fine_out[s, j, i, :, half * b : (half + 1) * b] = total
    for s in range(s_count):
        coarse_out[s, 0] = grad_coarse[s, 2 : 2 + la]
        cells = []
        for c in range(8):
            cr, ca, cb = c // 4, c // 2 % 2, c % 2
            cells.append(grad_mid[s, 2 * cr + cb, pl.ds(1 + ca, la, stride=2), :])
        for j in range(8):
            total = mixes[j : j + 1] * cells[0]
            for c in range(1, 8):
                total = total + mixes[j + 8 * c : j + 8 * c + 1] * cells[c]
            mid_out[s, j, 0] = total


def held(arrays):
    return [(pltpu.SMEM if len(x.shape) == 1 else pltpu.VMEM)(x.shape, x.dtype) for x in arrays]


def call(kernel, name, outs, operands, scratch, unmoved=0, written=0):
    vmem = pl.BlockSpec(memory_space=pltpu.VMEM)
    placed = pl.BlockSpec(memory_space=pl.ANY)
    limit = None if unmoved else VMEM_LIMIT
    return pl.pallas_call(
        kernel,
        name=name,
        out_shape=[jax.ShapeDtypeStruct(shape, kind) for shape, kind in outs],
        in_specs=[placed] * unmoved + [vmem] * (len(operands) - unmoved),
        out_specs=[placed] * written + [vmem] * (len(outs) - written),
        scratch_shapes=[pltpu.VMEM(shape, F32) if isinstance(shape, tuple) else shape for shape in scratch],
        compiler_params=pltpu.CompilerParams(vmem_limit_bytes=limit),
    )(*operands)


def per_device(
    g,
    coarse_field,
    excite_mid,
    excite_fine,
    kernels_mid,
    noise_mid,
    rows_mid,
    kernels_fine,
    noise_fine,
    rows_fine,
    emission,
    star_bins,
    star_data,
):
    n, m, s, la, b, stars, w, ra, h = g
    kernel = functools.partial
    rows_a = 2 * ra + 2
    workers = [(r, a, 1 if min(r, w - 1) < w // 2 else -1) for r in range(n) for a in range(m)]
    sideways = [(r * m + a, r * m + (a - step) % m) for r, a, step in workers]
    inward = [(to, at) for at, to in sideways]

    def exchange(blocks):
        return [blocks[0]] + [lax.ppermute(blocks[k], "rad", [(i, (i + k) % n) for i in range(n)]) for k in range(1, n)]

    noise_mid, noise_fine = noise_mid.transpose(1, 2, 0), noise_fine.transpose(1, 2, 0)
    large = (large_there(g)[-1], b)
    operands = (emission, rows_mid, noise_mid, coarse_field, excite_mid, rows_fine, noise_fine, excite_fine)
    sent = call(
        kernel(scatter_kernel, g),
        "scatter",
        [(large, F32)] * n,
        operands,
        [
            *held(operands),
            pltpu.SemaphoreType.DMA((10 + 2 * s,)),
            pltpu.SemaphoreType.DMA((2 * n,)),
            (32 * s * la, 2 * b),
            (2, 32 * s * la, b),
            (4, 16 * la, b),
            (w, *large),
            (s, 8, la, b),
            (s, la + 4, b),
        ],
        unmoved=8,
        written=n,
    )
    got = exchange(sent)
    operands = (rows_mid, rows_fine, noise_mid, noise_fine, kernels_mid, kernels_fine, star_bins, star_data)
    (block,) = call(
        kernel(prepare_kernel, g),
        "prepare",
        [((prepared_rows(g)[1], b), F32)],
        (*operands, sent[0]),
        [*held(operands), pltpu.SemaphoreType.DMA((8,)), (2, 4 * stars * ra, 4 * b)],
        unmoved=9,
    )
    spread, got[0], block = call(
        kernel(weight_kernel, g),
        "weights",
        [((24 * 27, h, b), F32), (large, F32), (block.shape, F32)],
        (block, sent[0]),
        [],
    )
    (near,) = call(kernel(relay_kernel, g), "relay", [((7 * h, b), F32)], got, [])
    near = lax.ppermute(near, ("rad", "ang"), inward)
    parts = [((x + 1) * h, b) for x in (64 * ra, 64 * ra, 4 * rows_a, ra + 4)]
    unpacked = call(kernel(unpack_kernel, g), "unpack", [(part, F32) for part in parts], got, [])
    def everywhere(block, after):
        ids, bit = [0], n // 2
        while True:
            got = lax.ppermute(block, "rad", [(i, i ^ bit) for i in range(n)])
            more = [i ^ bit for i in ids]
            if bit == 1:
                return (block, got), (ids, more)
            shape = (2 * block.shape[0], b)
            (block,) = call(kernel(join_kernel, g), "join", [(shape, F32)], (block, got, after), [])
            ids, bit = ids + more, bit // 2

    end_field, _, end = rows_back(g)
    resid_rows = 16 * stars * ra * s
    cells, shown = call(
        kernel(forward_kernel, g),
        "forward",
        [((2, 32 * ra * h, b), F32), ((resid_rows, b), F32)],
        (block, spread, *unpacked, near),
        [
            (4 * rows_a * h, b),
            ((ra + 4) * h, b),
            (3, ra + 4, 3, h, b),
            (4, rows_a, 4, h, b),
            (4, 4 * stars * ra * s, b),
        ],
    )
    parent, coarse_sum, edge = call(
        kernel(backward_kernel, g),
        "backward",
        [((4 * rows_a * h, b), F32), (((ra + 4) * h, b), F32), ((6 * h, b), F32)],
        (spread, cells),
        [(4, rows_a, 4, h, b)],
    )
    edge = lax.ppermute(edge, ("rad", "ang"), sideways)
    (field,) = call(
        kernel(lanes_kernel, g), "lanes", [((n, end_field, b), F32)], (cells,), [(2, 32 * ra * h, b)]
    )
    got = exchange(
        call(
            kernel(sums_kernel, g),
            "sums",
            [((end, b), F32)] * n,
            (field, parent, coarse_sum, edge),
            [(n, end - end_field, b), parent.shape, coarse_sum.shape],
        )
    )
    shown, ids = everywhere(shown, got[0])
    residual, mixes = call(
        kernel(resid_owner_kernel, g, ids),
        "resid_owner",
        [((s, stars, 4 * la, 4 * b), F32), ((192, b), F32)],
        (block, *shown),
        [(n, resid_rows, b)],
    )
    grad_coarse, grad_mid, grad_fine = call(
        kernel(owner_kernel, g),
        "owner",
        [((s, 1, la, b), F32), ((s, 8, 1, la, b), F32), ((s, 8, 2, 2 * la, 2 * b), F32)],
        (mixes, *got),
        [(n, end, b), (2, 32 * s * la, b), (s, 4, 2 * la + 2, b), (s, la + 4, b)],
    )
    return grad_coarse, grad_mid, grad_fine, residual


def solution(mesh):
    placed = (
        P(None, "rad", "ang", None),
        P(None, None, "rad", "ang", None),
        P(None, None, "rad", "ang", None),
        P(),
        P(),
        P(),
        P(),
        P(),
        P(),
        P("rad", "ang", None),
        P(None, "ang", None),
        P(None, "ang", None),
    )

    def local(*args):
        return per_device(make_plan(mesh, args[0], args[10]), *args)

    return jax.shard_map(
        local,
        mesh=mesh,
        in_specs=placed,
        out_specs=(
            P(None, "rad", "ang", None),
            P(None, None, "rad", "ang", None),
            P(None, None, "rad", "ang", None),
            P(None, None, "ang", None),
        ),
        check_vma=False,
    )
```
